512 devices in a mesh: shot: 32 (over y, z_lo), dom: 16 (over z_hi, x, core).
Axes of the slice: x: 4, y: 4, z: 16 (z_hi: 2, z_lo: 8; z = z_hi * 8 + z_lo), core: 2. Of those that a mesh axis runs over, the one named last changes fastest.
Arguments:
- pressure_now: float32 [32, 128, 32, 128], P('shot', 'dom'), may hold values from -6 to 6
- pressure_prev: float32 [32, 128, 32, 128], P('shot', 'dom'), may hold values from -6 to 6
- adjoint_last: float32 [32, 128, 32, 128], P('shot', 'dom'), may hold values from -6 to 6
- adjoint_after: float32 [32, 128, 32, 128], P('shot', 'dom'), may hold values from -6 to 6
- kappa_model: float32 [4, 128, 4096], P(None, 'dom', 'shot'), may hold values from 1 to 4
- buoy_model: float32 [4, 128, 4096], P(None, 'dom', 'shot'), may hold values from 0.5 to 2
- aperture: int32 [32, 16], replicated, may hold values from 0 to 3
- source_cell: int32 [32], P('shot'), may hold values from 0 to 524287
- source_wave: float32 [32, 3], P('shot'), may hold values from -8 to 8
- receiver_cell: int32 [32, 512], P('shot'), may hold values from 0 to 524287
- observed: float32 [32, 3, 512], P('shot'), may hold values from -6 to 6
Outputs:
- grad_kappa: float32 [4, 128, 4096], P(None, 'dom', 'shot')
- grad_buoy: float32 [4, 128, 4096], P(None, 'dom', 'shot')
- adjoint_first: float32 [32, 128, 32, 128], P('shot', 'dom')
- adjoint_second: float32 [32, 128, 32, 128], P('shot', 'dom')
The draws below stay inside these ranges and needn't reach their ends.
Inputs may be any that keep to these rules, and one draw needn't show every extreme that they name: `aperture`: the tile of the survey model that lies under slab x // 8 of each shot. `source_cell`: a flat cell index x * 32 * 128 + y * 128 + z of the shot's grid. `receiver_cell`: flat cell indices x * 32 * 128 + y * 128 + z of the shot's grid; cells may repeat.
All inputs are finite; a program needn't handle non-finite values.
Results may differ from the reference program's by a relative error of at most 0.0003.
Values sent between devices are 32-bit elements; how exact they have to be, the bound alone decides.
No kernel may reach another device: no remote copies, remote signals or barrier semaphores. Data moves between devices by JAX's collectives and lax.ppermute only.
A program may use at most 64 MiB of HBM per device.

```python
import math
import jax
import jax.numpy as jnp
from jax import lax

CX = 8
CY = 32
CZ = 128
TILES = 4
STEPS = 3
REC = 512
SHOTS = 32
NX = 128
N_DOM = 16


def place_ends(drawn, key, low, largest):
    longest = drawn.shape.index(max(drawn.shape))
    spots = []
    for shift in (0, 1):
        where = [jax.random.randint(jax.random.fold_in(key, axis), (), 0, length) for axis, length in enumerate(drawn.shape)]
        where[longest] = (where[longest] + shift) % drawn.shape[longest]
        spots.append(tuple(where))
    return drawn.at[spots[0]].set(low).at[spots[1]].set(largest)


def levels(key, shape, split, smallest, largest):
    loudness = 1.0
    for axis_at, shards_of in split:
        draws = jax.random.uniform(jax.random.fold_in(jax.random.fold_in(key, 6), axis_at), (shards_of,), jnp.float32, smallest / len(split), largest / len(split))
        loudness = loudness * jnp.repeat(jnp.exp(draws), shape[axis_at] // shards_of).reshape((-1,) + (1,) * (len(shape) - 1 - axis_at))
    return loudness


def normal_values(stream_key, dims, spread, reach, cuts=(), kind=jnp.bfloat16):
    gain = levels(stream_key, dims, cuts, -0.22, 0.18) if cuts else 1.0
    values = jax.random.normal(stream_key, dims, jnp.float32) * spread * gain
    return jnp.minimum(jnp.maximum(values, -reach), reach).astype(kind)


def setup_inputs(seed: int = 0) -> dict:
    streams_of = jax.random.split(jax.random.key(seed), 12)
    return {
        "pressure_now": normal_values(streams_of[0], (SHOTS, NX, CY, CZ), 1.0, 6.0, ((0, 32), (1, 16)), jnp.float32),
        "pressure_prev": normal_values(streams_of[1], (SHOTS, NX, CY, CZ), 1.0, 6.0, ((0, 32), (1, 16)), jnp.float32),
        "adjoint_last": normal_values(streams_of[2], (SHOTS, NX, CY, CZ), 1.0, 6.0, ((0, 32), (1, 16)), jnp.float32),
        "adjoint_after": normal_values(streams_of[3], (SHOTS, NX, CY, CZ), 1.0, 6.0, ((0, 32), (1, 16)), jnp.float32),
        "kappa_model": jnp.clip(jnp.exp(math.log(4.0) - 1.3862944 * jax.random.uniform(streams_of[4], (TILES, NX, CY * CZ), jnp.float32) ** levels(streams_of[4], (TILES, NX, CY * CZ), ((1, 16), (2, 32)), -0.2, 0.2)), 1.0, 4.0),
        "buoy_model": jnp.clip(jnp.exp(math.log(2.0) - 1.3862944 * jax.random.uniform(streams_of[5], (TILES, NX, CY * CZ), jnp.float32) ** levels(streams_of[5], (TILES, NX, CY * CZ), ((1, 16), (2, 32)), -0.2, 0.2)), 0.5, 2.0),
        "aperture": place_ends(jax.random.randint(streams_of[6], (SHOTS, N_DOM), 0, TILES), jax.random.fold_in(streams_of[6], 1), 0, TILES - 1).astype(jnp.int32),
        "source_cell": place_ends(jax.random.randint(streams_of[7], (SHOTS,), 0, NX * CY * CZ), jax.random.fold_in(streams_of[7], 1), 0, (NX * CY * CZ) - 1).astype(jnp.int32),
        "source_wave": normal_values(streams_of[8], (SHOTS, STEPS), 2.0, 8.0, ((0, 32),), jnp.float32),
        "receiver_cell": place_ends(jax.random.randint(streams_of[9], (SHOTS, REC), 0, NX * CY * CZ), jax.random.fold_in(streams_of[9], 1), 0, (NX * CY * CZ) - 1).astype(jnp.int32),
        "observed": normal_values(streams_of[10], (SHOTS, STEPS, REC), 1.0, 6.0, ((0, 32),), jnp.float32),
    }


COEFFS = (1225.0 / 1024.0, -245.0 / 3072.0, 49.0 / 5120.0, -5.0 / 7168.0)
step_squared = 0.02


def minus_diff(wavefield, dim_axis):
    length = wavefield.shape[dim_axis]
    widths = [(0, 0), (0, 0), (0, 0)]
    widths[dim_axis] = (4, 4)
    padded = jnp.pad(wavefield, widths)
    summed = jnp.zeros_like(wavefield)
    for k, weight in enumerate(COEFFS):
        leading = lax.slice_in_dim(padded, 4 + k, 4 + k + length, axis=dim_axis)
        trailing = lax.slice_in_dim(padded, 3 - k, 3 - k + length, axis=dim_axis)
        summed = summed + weight * (leading - trailing)
    return summed


def plus_diff(wavefield, dim_axis):
    length = wavefield.shape[dim_axis]
    widths = [(0, 0), (0, 0), (0, 0)]
    widths[dim_axis] = (4, 4)
    padded = jnp.pad(wavefield, widths)
    summed = jnp.zeros_like(wavefield)
    for k, weight in enumerate(COEFFS):
        leading = lax.slice_in_dim(padded, 5 + k, 5 + k + length, axis=dim_axis)
        trailing = lax.slice_in_dim(padded, 4 - k, 4 - k + length, axis=dim_axis)
        summed = summed + weight * (leading - trailing)
    return summed


def apply_operator(wavefield, buoyancy):
    slopes = [minus_diff(wavefield, dim_axis) for dim_axis in range(3)]
    divergence = plus_diff(buoyancy * slopes[0], 0)
    divergence = divergence + plus_diff(buoyancy * slopes[1], 1)
    divergence = divergence + plus_diff(buoyancy * slopes[2], 2)
    return divergence, slopes


def reference(pressure_now, pressure_prev, adjoint_last, adjoint_after, kappa_model, buoy_model, aperture, source_cell, source_wave, receiver_cell, observed):
    tile_ids = jnp.arange(TILES, dtype=jnp.int32)
    x_cells = jnp.arange(NX, dtype=jnp.int32)
    grid_shape = (NX, CY, CZ)

    def one_shot(totals, inputs):
        grad_kappa, grad_buoy = totals
        present, former, adjoint_now, adjoint_later, columns, source, wavelet, receivers, measured = inputs
        tile_of_x = jnp.repeat(columns, CX).astype(jnp.int32)
        stiffness = kappa_model[tile_of_x, x_cells].reshape(grid_shape)
        buoyancy = buoy_model[tile_of_x, x_cells].reshape(grid_shape)
        history = []
        residuals = []
        previous = former
        for n in range(STEPS):
            divergence, slopes = apply_operator(present, buoyancy)
            history.append((divergence, slopes))
            following = 2.0 * present - previous + step_squared * stiffness * divergence
            following = following.reshape(-1).at[source].add(wavelet[n]).reshape(grid_shape)
            residuals.append(following.reshape(-1)[receivers] - measured[n])
            previous, present = present, following
        current, later = adjoint_now, adjoint_later
        image_kappa = jnp.zeros(grid_shape, jnp.float32)
        image_buoy = jnp.zeros(grid_shape, jnp.float32)
        for m in range(STEPS + 1, 0, -1):
            divergence, slopes = apply_operator(stiffness * current, buoyancy)
            if m <= STEPS:
                stored_div, stored_slopes = history[m - 1]
                image_kappa = image_kappa + current * stored_div
                image_buoy = image_buoy + (stored_slopes[0] * slopes[0] + stored_slopes[1] * slopes[1] + stored_slopes[2] * slopes[2])
            if m >= 2:
                earlier = 2.0 * current - later + step_squared * divergence
                earlier = earlier.reshape(-1).at[receivers].add(residuals[m - 2]).reshape(grid_shape)
                later, current = current, earlier
        scaled_kappa = (step_squared * image_kappa).reshape(NX, CY * CZ)
        scaled_buoy = (-step_squared * image_buoy).reshape(NX, CY * CZ)
        chosen = (tile_of_x[None, :] == tile_ids[:, None]).astype(jnp.float32)
        grad_kappa = grad_kappa + chosen[:, :, None] * scaled_kappa[None]
        grad_buoy = grad_buoy + chosen[:, :, None] * scaled_buoy[None]
        return (grad_kappa, grad_buoy), (current, later)

    start = (jnp.zeros((TILES, NX, CY * CZ), jnp.float32), jnp.zeros((TILES, NX, CY * CZ), jnp.float32))
    inputs = (pressure_now, pressure_prev, adjoint_last, adjoint_after, aperture, source_cell, source_wave, receiver_cell, observed)
    totals, fields = lax.scan(one_shot, start, inputs)
    return totals[0], totals[1], fields[0], fields[1]
```

```python
import jax
import jax.numpy as jnp
from jax import lax
from jax.sharding import PartitionSpec as P

CY = 32
CZ = 128
TILES = 4
STEPS = 3


COEFFS = (1225.0 / 1024.0, -245.0 / 3072.0, 49.0 / 5120.0, -5.0 / 7168.0)
step_squared = 0.02


def extended(cells, sides, width):
    for axis, dim in sides:
        count = lax.axis_size(axis)
        ends = count - 1
        head = lax.slice_in_dim(cells, 0, width, axis=dim)
        tail = lax.slice_in_dim(cells, cells.shape[dim] - width, cells.shape[dim], axis=dim)
        cells = jnp.concatenate(
            [
                lax.ppermute(tail, axis, [(i, (i + 1) % count) for i in range(ends)]),
                cells,
                lax.ppermute(head, axis, [((i + 1) % count, i) for i in range(ends)]),
            ],
            axis=dim,
        )
    return cells


def minus_diff(wavefield, dim_axis):
    length = wavefield.shape[dim_axis]
    widths = [(0, 0), (0, 0), (0, 0)]
    widths[dim_axis] = (4, 4)
    padded = jnp.pad(wavefield, widths)
    summed = jnp.zeros_like(wavefield)
    for k, weight in enumerate(COEFFS):
        leading = lax.slice_in_dim(padded, 4 + k, 4 + k + length, axis=dim_axis)
        trailing = lax.slice_in_dim(padded, 3 - k, 3 - k + length, axis=dim_axis)
        summed = summed + weight * (leading - trailing)
    return summed


def plus_diff(wavefield, dim_axis):
    length = wavefield.shape[dim_axis]
    widths = [(0, 0), (0, 0), (0, 0)]
    widths[dim_axis] = (4, 4)
    padded = jnp.pad(wavefield, widths)
    summed = jnp.zeros_like(wavefield)
    for k, weight in enumerate(COEFFS):
        leading = lax.slice_in_dim(padded, 5 + k, 5 + k + length, axis=dim_axis)
        trailing = lax.slice_in_dim(padded, 4 - k, 4 - k + length, axis=dim_axis)
        summed = summed + weight * (leading - trailing)
    return summed


def slab_minus(widened, length):
    span = length + 7
    summed = jnp.zeros((span,) + widened.shape[1:], jnp.float32)
    for k, weight in enumerate(COEFFS):
        summed = summed + weight * (widened[4 + k : 4 + k + span] - widened[3 - k : 3 - k + span])
    return summed


def slab_plus(fluxes, length):
    summed = jnp.zeros((length,) + fluxes.shape[1:], jnp.float32)
    for k, weight in enumerate(COEFFS):
        summed = summed + weight * (fluxes[4 + k : 4 + k + length] - fluxes[3 - k : 3 - k + length])
    return summed


def widen(wavefield):
    return extended(wavefield, (("dom", 0),), 7)


def slab_operator(widened, buoy_wide, length):
    centre = widened[7 : 7 + length]
    slopes_x = slab_minus(widened, length)
    divergence = slab_plus(buoy_wide[1 : length + 8] * slopes_x, length)
    buoyancy = buoy_wide[4 : 4 + length]
    slope_y = minus_diff(centre, 1)
    slope_z = minus_diff(centre, 2)
    divergence = divergence + plus_diff(buoyancy * slope_y, 1)
    divergence = divergence + plus_diff(buoyancy * slope_z, 2)
    return (divergence, (slopes_x[3 : 3 + length], slope_y, slope_z))


def shards(
    pressure_now,
    pressure_prev,
    adjoint_last,
    adjoint_after,
    kappa_model,
    buoy_model,
    aperture,
    source_cell,
    source_wave,
    receiver_cell,
    observed,
):
    dom_index = lax.axis_index("dom")
    length = pressure_now.shape[1]
    grid_shape = (length, CY, CZ)
    cell_count = length * CY * CZ
    column = lax.dynamic_index_in_dim(aperture, dom_index, 1, keepdims=False)
    stacked = jnp.stack((kappa_model, buoy_model), axis=1)
    picks = column[:, None, None, None]
    chosen = stacked[0][None]
    for t in range(1, TILES):
        chosen = jnp.where(picks == t, stacked[t][None], chosen)
    my_block = lax.all_to_all(chosen, "shot", 0, 0, tiled=True)
    stiffness = my_block[:, 0].transpose(1, 0, 2)
    buoyancy = my_block[:, 1].transpose(1, 0, 2)
    buoy_wide = extended(buoyancy, (("dom", 0),), 4)
    offset = dom_index * cell_count
    source_local = source_cell[0] - offset
    source_owned = (source_local >= 0) & (source_local < cell_count)
    source_slot = jnp.clip(source_local, 0, cell_count - 1)
    receiver_local = receiver_cell[0] - offset
    receiver_owned = (receiver_local >= 0) & (receiver_local < cell_count)
    receiver_slot = jnp.clip(receiver_local, 0, cell_count - 1)
    present = pressure_now[0]
    previous = pressure_prev[0]
    history = []
    residuals = []
    for n in range(STEPS):
        divergence, slopes = slab_operator(widen(present), buoy_wide, length)
        history.append((divergence, slopes))
        following = 2.0 * present - previous + step_squared * stiffness * divergence
        amount = jnp.where(source_owned, source_wave[0, n], 0.0)
        following = following.reshape(-1).at[source_slot].add(amount).reshape(grid_shape)
        recorded = following.reshape(-1)[receiver_slot]
        residuals.append(jnp.where(receiver_owned, recorded - observed[0, n], 0.0))
        previous, present = (present, following)
    current = adjoint_last[0]
    later = adjoint_after[0]
    image_kappa = jnp.zeros(grid_shape, jnp.float32)
    image_buoy = jnp.zeros(grid_shape, jnp.float32)
    for m in range(STEPS + 1, 0, -1):
        divergence, slopes = slab_operator(widen(stiffness * current), buoy_wide, length)
        if m <= STEPS:
            stored_div, stored_slopes = history[m - 1]
            image_kappa = image_kappa + current * stored_div
            image_buoy = image_buoy + (
                stored_slopes[0] * slopes[0]
                + stored_slopes[1] * slopes[1]
                + stored_slopes[2] * slopes[2]
            )
        if m >= 2:
            earlier = 2.0 * current - later + step_squared * divergence
            earlier = (
                earlier.reshape(-1).at[receiver_slot].add(residuals[m - 2]).reshape(grid_shape)
            )
            later, current = (current, earlier)
    image_stack = jnp.stack((step_squared * image_kappa, -step_squared * image_buoy))
    arrived = lax.all_to_all(image_stack.transpose(2, 0, 1, 3), "shot", 0, 0, tiled=True)
    owned = [
        jnp.sum(jnp.where(picks == t, arrived, 0.0), axis=0) for t in range(TILES)
    ]
    return (
        jnp.stack([o[0] for o in owned]),
        jnp.stack([o[1] for o in owned]),
        current[None],
        later[None],
    )


def solution(mesh):
    in_specs = (
        P("shot", "dom", None, None),
        P("shot", "dom", None, None),
        P("shot", "dom", None, None),
        P("shot", "dom", None, None),
        P(None, "dom", "shot"),
        P(None, "dom", "shot"),
        P(),
        P("shot"),
        P("shot", None),
        P("shot", None),
        P("shot", None, None),
    )
    out_specs = (
        P(None, "dom", "shot"),
        P(None, "dom", "shot"),
        P("shot", "dom", None, None),
        P("shot", "dom", None, None),
    )
    return jax.shard_map(shards, mesh=mesh, in_specs=in_specs, out_specs=out_specs, check_vma=False)
```

```python
import jax
import jax.numpy as jnp
from jax import lax
from jax.experimental import pallas as pl
from jax.experimental.pallas import tpu as pltpu
from jax.sharding import PartitionSpec as P

CX = 8
CY = 32
CZ = 128
TILES = 4
STEPS = 3
REC = 512
PAD = 8
ROWS = CY + 2 * PAD
WIDE = CX + 14

COEFFS = (1225.0 / 1024.0, -245.0 / 3072.0, 49.0 / 5120.0, -5.0 / 7168.0)
step_squared = 0.02

VMEM = pl.BlockSpec(memory_space=pltpu.VMEM)
SMEM = pl.BlockSpec(memory_space=pltpu.SMEM)
F32 = jnp.float32


def plane_field(count):
    return jax.ShapeDtypeStruct((count, CY, CZ), F32)


def lane_shift(plane, by, lane):
    if by == 0:
        return plane
    moved = pltpu.roll(plane, (-by) % CZ, 1)
    keep = lane < CZ - by if by > 0 else lane >= -by
    return jnp.where(keep, moved, 0.0)


def stencil(at):
    total = COEFFS[0] * (at(0) - at(-1))
    for k in range(2, 5):
        total = total + COEFFS[k - 1] * (at(k - 1) - at(-k))
    return total


def place(info, target, own, first, second, width):
    target[:, 0:PAD, :] = jnp.zeros((target.shape[0], PAD, CZ), F32)
    target[:, PAD + CY : ROWS, :] = jnp.zeros((target.shape[0], PAD, CZ), F32)
    inner = slice(PAD, PAD + CY)
    target[width : width + CX, inner, :] = own
    odd = info[0] == 1

    @pl.when(odd)
    def _():
        target[0:width, inner, :] = first
        target[width + CX : 2 * width + CX, inner, :] = second

    @pl.when(jnp.logical_not(odd))
    def _():
        target[0:width, inner, :] = second
        target[width + CX : 2 * width + CX, inner, :] = first


def hand_over(info, first, second, head, tail):
    odd = info[0] == 1

    @pl.when(odd)
    def _():
        first[...] = head()
        second[...] = tail()

    @pl.when(jnp.logical_not(odd))
    def _():
        first[...] = tail()
        second[...] = head()


def slope_x(field, at):
    return stencil(lambda s: field[at + s, PAD : PAD + CY, :])


def slope_y(field, at):
    return stencil(lambda s: field[at, PAD + s : PAD + CY + s, :])


def slope_z(plane, lane):
    return stencil(lambda s: lane_shift(plane, s, lane))


def operate(field, width, buoy, gx, gy, acc, slopes):
    lane = lax.broadcasted_iota(jnp.int32, (CY, CZ), 1)
    gy[:, 0:PAD, :] = jnp.zeros((CX, PAD, CZ), F32)
    gy[:, PAD + CY : ROWS, :] = jnp.zeros((CX, PAD, CZ), F32)
    for cell in range(-3, CX + 4):
        sx = slope_x(field, cell + width)
        gx[cell + 3] = buoy[cell + 4] * sx
        if 0 <= cell < CX:
            weight = buoy[cell + 4]
            plane = field[cell + width, PAD : PAD + CY, :]
            sy = slope_y(field, cell + width)
            sz = slope_z(plane, lane)
            gy[cell, PAD : PAD + CY, :] = weight * sy
            gz = weight * sz
            acc[cell] = stencil(lambda s: lane_shift(gz, s + 1, lane))
            slopes(cell, sx, sy, sz)
    for cell in range(CX):
        div = stencil(lambda s: gx[cell + 4 + s])
        div = div + stencil(lambda s: gy[cell, PAD + 1 + s : PAD + 1 + s + CY, :])
        yield cell, div + acc[cell]


def receivers_kernel(info, cells, seen, out):
    index = cells[...] - info[4]
    row = lax.shift_right_arithmetic(index, 7)
    z = lax.bitwise_and(index, 127)
    rows = lax.broadcasted_iota(jnp.int32, (CX * CY, REC), 0)
    pick = jnp.where(rows == row, 1.0, 0.0).astype(jnp.bfloat16)
    lanes = lax.broadcasted_iota(jnp.int32, (CZ, REC), 0)
    here = lanes == z

    def spread(values):
        right = jnp.where(here, values, 0.0).astype(jnp.bfloat16)
        return lax.dot_general(
            pick, right, (((1,), (1,)), ((), ())), preferred_element_type=F32
        )

    out[0] = spread(jnp.ones((1, REC), F32)).reshape(CX, CY, CZ)
    for n in range(STEPS):
        rest = seen[n : n + 1, :]
        total = None
        for _ in range(3):
            part = rest.astype(jnp.bfloat16).astype(F32)
            rest = rest - part
            total = spread(part) if total is None else total + spread(part)
        out[n + 1] = total.reshape(CX, CY, CZ)


def model_kernel(info, stiff, buoy, last, send_a, send_b, scaled):
    scaled[...] = stiff[...] * last[...]
    hand_over(
        info,
        send_a,
        send_b,
        lambda: jnp.concatenate([buoy[0:4], scaled[0:7]], axis=0),
        lambda: jnp.concatenate([buoy[4:8], scaled[1:8]], axis=0),
    )


def source_plane(info, amount):
    y = lax.broadcasted_iota(jnp.int32, (CY, CZ), 0)
    z = lax.broadcasted_iota(jnp.int32, (CY, CZ), 1)
    hit = (y == info[2]) & (z == info[3])
    spot = jnp.where(hit, amount, 0.0)
    return lambda cell: jnp.where(info[1] == cell, spot, 0.0)


def forward(info, wave, n, now, before, stiff, field, buoy, gx, gy, acc, div_out, slope_out, after):
    source = source_plane(info, wave[n])

    def keep(cell, sx, sy, sz):
        slope_out[0, cell] = sx
        slope_out[1, cell] = sy
        slope_out[2, cell] = sz

    for cell, div in operate(field, 7, buoy, gx, gy, acc, keep):
        div_out[cell] = div
        value = 2.0 * now[cell] - before[cell] + step_squared * stiff[cell] * div
        after(cell, value + source(cell))


def widen_buoy(info, buoy, first, second, target):
    target[4 : 4 + CX] = buoy[...]
    odd = info[0] == 1

    @pl.when(odd)
    def _():
        target[0:4] = first[0:4]
        target[4 + CX : 8 + CX] = second[0:4]

    @pl.when(jnp.logical_not(odd))
    def _():
        target[0:4] = second[0:4]
        target[4 + CX : 8 + CX] = first[0:4]


def first_kernel(
    info, wave, now, now_a, now_b, before, last, after, stiff, buoy, edge_a, edge_b, scaled,
    p_out, send_a, send_b, div_out, slope_out, buoy_out, q_out,
    field, gx, gy, acc,
):
    widen_buoy(info, buoy, edge_a, edge_b, buoy_out)
    place(info, field, now[...], now_a[...], now_b[...], 7)

    def store(cell, value):
        p_out[cell] = value

    forward(info, wave, 0, now, before, stiff, field, buoy_out, gx, gy, acc, div_out, slope_out, store)
    hand_over(info, send_a, send_b, lambda: p_out[0:7], lambda: p_out[1:8])
    place(info, field, scaled[...], edge_a[4:11], edge_b[4:11], 7)
    for cell, div in operate(field, 7, buoy_out, gx, gy, acc, lambda *_: None):
        q_out[cell] = 2.0 * last[cell] - after[cell] + step_squared * div


def second_kernel(
    info, wave, now, now_a, now_b, before, stiff, buoy,
    p_out, send_a, send_b, div_out, slope_out,
    field, gx, gy, acc,
):
    place(info, field, now[...], now_a[...], now_b[...], 7)

    def store(cell, value):
        p_out[cell] = value

    forward(info, wave, 1, now, before, stiff, field, buoy, gx, gy, acc, div_out, slope_out, store)
    hand_over(info, send_a, send_b, lambda: p_out[0:7], lambda: p_out[1:8])


def third_kernel(
    info, wave, now, now_a, now_b, before, stiff, buoy, q_part, spots,
    q_out, scaled, send_a, send_b, div_out, slope_out,
    field, gx, gy, acc,
):
    place(info, field, now[...], now_a[...], now_b[...], 7)

    def store(cell, value):
        q = q_part[cell] + (spots[0, cell] * value - spots[3, cell])
        q_out[cell] = q
        scaled[cell] = stiff[cell] * q

    forward(info, wave, 2, now, before, stiff, field, buoy, gx, gy, acc, div_out, slope_out, store)
    hand_over(info, send_a, send_b, lambda: scaled[0:7], lambda: scaled[1:8])


def adjoint_kernel(
    n, width, info, q_now, q_after, scaled, scaled_a, scaled_b, stiff, buoy, spots, p_then, div, slope, images,
    q_out, scaled_out, send_a, send_b, images_out,
    field, gx, gy, acc,
):
    place(info, field, scaled[...], scaled_a[...], scaled_b[...], 7)

    def image(cell, sx, sy, sz):
        kappa = q_now[cell] * div[cell]
        rho = slope[0, cell] * sx + slope[1, cell] * sy + slope[2, cell] * sz
        if images is not None:
            kappa = images[0, cell] + kappa
            rho = images[1, cell] + rho
        images_out[0, cell] = kappa
        images_out[1, cell] = rho

    for cell, total in operate(field, 7, buoy, gx, gy, acc, image):
        q = 2.0 * q_now[cell] - q_after[cell] + step_squared * total
        q = q + (spots[0, cell] * p_then[cell] - spots[n + 1, cell])
        q_out[cell] = q
        scaled_out[cell] = stiff[cell] * q
    hand_over(info, send_a, send_b, lambda: scaled_out[0:width], lambda: scaled_out[CX - width : CX])


def adjoint_first_kernel(info, q_now, q_after, scaled, scaled_a, scaled_b, stiff, buoy, spots, p_then, div, slope, *rest):
    adjoint_kernel(1, 7, info, q_now, q_after, scaled, scaled_a, scaled_b, stiff, buoy, spots, p_then, div, slope, None, *rest)


def adjoint_second_kernel(info, q_now, q_after, scaled, scaled_a, scaled_b, stiff, buoy, spots, p_then, div, slope, images, *rest):
    adjoint_kernel(0, 4, info, q_now, q_after, scaled, scaled_a, scaled_b, stiff, buoy, spots, p_then, div, slope, images, *rest)


def image_kernel(info, q_now, scaled, scaled_a, scaled_b, div, slope, images, out, field):
    lane = lax.broadcasted_iota(jnp.int32, (CY, CZ), 1)
    place(info, field, scaled[...], scaled_a[...], scaled_b[...], 4)
    for cell in range(CX):
        plane = field[cell + 4, PAD : PAD + CY, :]
        rho = images[1, cell] + slope[0, cell] * slope_x(field, cell + 4)
        rho = rho + slope[1, cell] * slope_y(field, cell + 4)
        rho = rho + slope[2, cell] * slope_z(plane, lane)
        out[0, cell] = step_squared * (images[0, cell] + q_now[cell] * div[cell])
        out[1, cell] = -step_squared * rho


def gather_kernel(column, arrived, out_kappa, out_buoy):
    out_kappa[...] = jnp.zeros_like(out_kappa)
    out_buoy[...] = jnp.zeros_like(out_buoy)
    for s in range(arrived.shape[0]):
        t = column[s]
        out_kappa[t] = out_kappa[t] + arrived[s, 0]
        out_buoy[t] = out_buoy[t] + arrived[s, 1]


def work():
    return [
        pltpu.VMEM((WIDE, ROWS, CZ), F32),
        pltpu.VMEM((CX + 7, CY, CZ), F32),
        pltpu.VMEM((CX, ROWS, CZ), F32),
        pltpu.VMEM((CX, CY, CZ), F32),
    ]


def call(kernel, scalars, arrays, outs, scratch=(), flops=2_000_000):
    moved = sum(4 * a.size for a in arrays) + sum(4 * o.size for o in outs)
    return pl.pallas_call(
        kernel,
        out_shape=outs,
        in_specs=[SMEM] * len(scalars) + [VMEM] * len(arrays),
        out_specs=[VMEM] * len(outs),
        scratch_shapes=list(scratch),
        compiler_params=pltpu.CompilerParams(vmem_limit_bytes=32 * 1024 * 1024),
        cost_estimate=pl.CostEstimate(flops=flops, bytes_accessed=moved, transcendentals=0),
    )(*scalars, *arrays)


def swap(first, second):
    count = lax.axis_size("dom")
    pairs_a = [(i ^ 1, i) for i in range(count)]
    pairs_b = []
    for i in range(1, count - 1, 2):
        pairs_b += [(i, i + 1), (i + 1, i)]
    second = lax.ppermute(second, "dom", pairs_b)
    return lax.ppermute(first, "dom", pairs_a), second


def shards(
    pressure_now,
    pressure_prev,
    adjoint_last,
    adjoint_after,
    kappa_model,
    buoy_model,
    aperture,
    source_cell,
    source_wave,
    receiver_cell,
    observed,
):
    dom = lax.axis_index("dom")
    odd = lax.rem(dom, 2)
    offset = dom * (CX * CY * CZ)
    source = source_cell[0]
    info = jnp.stack(
        [odd, source // (CY * CZ) - dom * CX, (source // CZ) % CY, source % CZ, offset]
    ).astype(jnp.int32)
    wave = source_wave[0]
    column = lax.dynamic_index_in_dim(aperture, dom, 1, keepdims=False)

    stacked = jnp.stack((kappa_model, buoy_model), axis=1)
    picks = column[:, None, None, None]
    chosen = stacked[0][None]
    for t in range(1, TILES):
        chosen = jnp.where(picks == t, stacked[t][None], chosen)
    block = lax.all_to_all(chosen, "shot", 0, 0, tiled=True)

    p0, p_prev = pressure_now[0], pressure_prev[0]
    q4, q5 = adjoint_last[0], adjoint_after[0]
    head, tail = p0[0:7], p0[1:8]
    p0_a, p0_b = swap(jnp.where(odd == 1, head, tail), jnp.where(odd == 1, tail, head))
    (spots,) = call(
        receivers_kernel,
        [info],
        [receiver_cell, observed[0]],
        [jax.ShapeDtypeStruct((STEPS + 1, CX, CY, CZ), F32)],
        flops=400_000_000,
    )

    stiff = block[:, 0].transpose(1, 0, 2)
    buoy = block[:, 1].transpose(1, 0, 2)
    own, seven, four = plane_field(CX), plane_field(7), plane_field(4)
    slopes = jax.ShapeDtypeStruct((3, CX, CY, CZ), F32)
    images = jax.ShapeDtypeStruct((2, CX, CY, CZ), F32)

    send_a, send_b, f4 = call(
        model_kernel, [info], [stiff, buoy, q4], [plane_field(11), plane_field(11), own]
    )
    edge_a, edge_b = swap(send_a, send_b)
    p1, send_a, send_b, div0, slope0, wide, q_part = call(
        first_kernel,
        [info, wave],
        [p0, p0_a, p0_b, p_prev, q4, q5, stiff, buoy, edge_a, edge_b, f4],
        [own, seven, seven, own, slopes, plane_field(CX + 8), own],
        work(),
    )
    from_a, from_b = swap(send_a, send_b)
    p2, send_a, send_b, div1, slope1 = call(
        second_kernel,
        [info, wave],
        [p1, from_a, from_b, p0, stiff, wide],
        [own, seven, seven, own, slopes],
        work(),
    )
    from_a, from_b = swap(send_a, send_b)
    q3, f3, send_a, send_b, div2, slope2 = call(
        third_kernel,
        [info, wave],
        [p2, from_a, from_b, p1, stiff, wide, q_part, spots],
        [own, own, seven, seven, own, slopes],
        work(),
    )
    from_a, from_b = swap(send_a, send_b)
    q2, f2, send_a, send_b, image = call(
        adjoint_first_kernel,
        [info],
        [q3, q4, f3, from_a, from_b, stiff, wide, spots, p2, div2, slope2],
        [own, own, seven, seven, images],
        work(),
    )
    from_a, from_b = swap(send_a, send_b)
    q1, f1, send_a, send_b, image = call(
        adjoint_second_kernel,
        [info],
        [q2, q3, f2, from_a, from_b, stiff, wide, spots, p1, div1, slope1, image],
        [own, own, four, four, images],
        work(),
    )
    from_a, from_b = swap(send_a, send_b)
    (image,) = call(
        image_kernel,
        [info],
        [q1, f1, from_a, from_b, div0, slope0, image],
        [images],
        [pltpu.VMEM((CX + 8, ROWS, CZ), F32)],
    )
    arrived = lax.all_to_all(image.transpose(2, 0, 1, 3), "shot", 0, 0, tiled=True)
    tiles = jax.ShapeDtypeStruct((TILES, CX, CZ), F32)
    grad_kappa, grad_buoy = call(gather_kernel, [column], [arrived], [tiles, tiles])
    return (grad_kappa, grad_buoy, q1[None], q2[None])


def solution(mesh):
    in_specs = (
        P("shot", "dom", None, None),
        P("shot", "dom", None, None),
        P("shot", "dom", None, None),
        P("shot", "dom", None, None),
        P(None, "dom", "shot"),
        P(None, "dom", "shot"),
        P(),
        P("shot"),
        P("shot", None),
        P("shot", None),
        P("shot", None, None),
    )
    out_specs = (
        P(None, "dom", "shot"),
        P(None, "dom", "shot"),
        P("shot", "dom", None, None),
        P("shot", "dom", None, None),
    )
    return jax.shard_map(shards, mesh=mesh, in_specs=in_specs, out_specs=out_specs, check_vma=False)
```

```python
import jax
import jax.numpy as jnp
from jax import lax
from jax.experimental import pallas as pl
from jax.experimental.pallas import tpu as pltpu
from jax.sharding import PartitionSpec as P

CX = 8
CY = 32
CZ = 128
TILES = 4
STEPS = 3
REC = 512
PAD = 8
ROWS = CY + 2 * PAD
WIDE = CX + 14
BESIDE = 400_000_000

COEFFS = (1225.0 / 1024.0, -245.0 / 3072.0, 49.0 / 5120.0, -5.0 / 7168.0)
step_squared = 0.02

VMEM = pl.BlockSpec(memory_space=pltpu.VMEM)
SMEM = pl.BlockSpec(memory_space=pltpu.SMEM)
F32 = jnp.float32


def plane_field(count):
    return jax.ShapeDtypeStruct((count, CY, CZ), F32)


def lane_shift(plane, by, lane):
    if by == 0:
        return plane
    moved = pltpu.roll(plane, (-by) % CZ, 1)
    keep = lane < CZ - by if by > 0 else lane >= -by
    return jnp.where(keep, moved, 0.0)


def stencil(at):
    total = COEFFS[0] * (at(0) - at(-1))
    for k in range(2, 5):
        total = total + COEFFS[k - 1] * (at(k - 1) - at(-k))
    return total


def place(info, target, own, first, second, width):
    target[:, 0:PAD, :] = jnp.zeros((target.shape[0], PAD, CZ), F32)
    target[:, PAD + CY : ROWS, :] = jnp.zeros((target.shape[0], PAD, CZ), F32)
    inner = slice(PAD, PAD + CY)
    target[width : width + CX, inner, :] = own
    odd = info[0] == 1

    @pl.when(odd)
    def _():
        target[0:width, inner, :] = first
        target[width + CX : 2 * width + CX, inner, :] = second

    @pl.when(jnp.logical_not(odd))
    def _():
        target[0:width, inner, :] = second
        target[width + CX : 2 * width + CX, inner, :] = first


def for_partner(info, target, head, tail):
    odd = info[0] == 1

    @pl.when(odd)
    def _():
        target[...] = head()

    @pl.when(jnp.logical_not(odd))
    def _():
        target[...] = tail()


def choose_kernel(where, aperture, kappa, buoy, out):
    for s in range(out.shape[0]):
        t = aperture[s, where[0]]
        out[s, 0] = kappa[t]
        out[s, 1] = buoy[t]


def first_swap_kernel(info, field, out):
    width = out.shape[0]
    for_partner(info, out, lambda: field[0:width], lambda: field[CX - width : CX])


def slope_x(field, at):
    return stencil(lambda s: field[at + s, PAD : PAD + CY, :])


def slope_y(field, at):
    return stencil(lambda s: field[at, PAD + s : PAD + CY + s, :])


def slope_z(plane, lane):
    return stencil(lambda s: lane_shift(plane, s, lane))


def operate(field, width, buoy, gx, gy, acc, slopes):
    lane = lax.broadcasted_iota(jnp.int32, (CY, CZ), 1)
    gy[:, 0:PAD, :] = jnp.zeros((CX, PAD, CZ), F32)
    gy[:, PAD + CY : ROWS, :] = jnp.zeros((CX, PAD, CZ), F32)
    for cell in range(-3, CX + 4):
        sx = slope_x(field, cell + width)
        gx[cell + 3] = buoy[cell + 4] * sx
        if 0 <= cell < CX:
            weight = buoy[cell + 4]
            plane = field[cell + width, PAD : PAD + CY, :]
            sy = slope_y(field, cell + width)
            sz = slope_z(plane, lane)
            gy[cell, PAD : PAD + CY, :] = weight * sy
            gz = weight * sz
            acc[cell] = stencil(lambda s: lane_shift(gz, s + 1, lane))
            slopes(cell, sx, sy, sz)
    for cell in range(CX):
        div = stencil(lambda s: gx[cell + 4 + s])
        div = div + stencil(lambda s: gy[cell, PAD + 1 + s : PAD + 1 + s + CY, :])
        yield cell, div + acc[cell]


def receivers_kernel(info, cells, seen, out):
    index = cells[...] - info[4]
    row = lax.shift_right_arithmetic(index, 7)
    z = lax.bitwise_and(index, 127)
    rows = lax.broadcasted_iota(jnp.int32, (CX * CY, REC), 0)
    pick = jnp.where(rows == row, 1.0, 0.0).astype(jnp.bfloat16)
    lanes = lax.broadcasted_iota(jnp.int32, (CZ, REC), 0)
    here = lanes == z

    def spread(values):
        right = jnp.where(here, values, 0.0).astype(jnp.bfloat16)
        return lax.dot_general(
            pick, right, (((1,), (1,)), ((), ())), preferred_element_type=F32
        )

    out[0] = spread(jnp.ones((1, REC), F32)).reshape(CX, CY, CZ)
    for n in range(STEPS):
        rest = seen[n : n + 1, :]
        total = None
        for _ in range(3):
            part = rest.astype(jnp.bfloat16).astype(F32)
            rest = rest - part
            total = spread(part) if total is None else total + spread(part)
        out[n + 1] = total.reshape(CX, CY, CZ)


def model_kernel(info, stiff, buoy, last, send_b, scaled):
    scaled[...] = stiff[...] * last[...]
    for_partner(
        info,
        send_b,
        lambda: jnp.concatenate([buoy[4:8], scaled[1:8]], axis=0),
        lambda: jnp.concatenate([buoy[0:4], scaled[0:7]], axis=0),
    )


def model_swap_kernel(info, buoy, scaled, out):
    for_partner(
        info,
        out,
        lambda: jnp.concatenate([buoy[0:4], scaled[0:7]], axis=0),
        lambda: jnp.concatenate([buoy[4:8], scaled[1:8]], axis=0),
    )


def source_plane(info, amount):
    y = lax.broadcasted_iota(jnp.int32, (CY, CZ), 0)
    z = lax.broadcasted_iota(jnp.int32, (CY, CZ), 1)
    hit = (y == info[2]) & (z == info[3])
    spot = jnp.where(hit, amount, 0.0)
    return lambda cell: jnp.where(info[1] == cell, spot, 0.0)


def forward(info, wave, n, now, before, stiff, field, buoy, gx, gy, acc, div_out, slope_out, after):
    source = source_plane(info, wave[n])

    def keep(cell, sx, sy, sz):
        slope_out[0, cell] = sx
        slope_out[1, cell] = sy
        slope_out[2, cell] = sz

    for cell, div in operate(field, 7, buoy, gx, gy, acc, keep):
        div_out[cell] = div
        value = 2.0 * now[cell] - before[cell] + step_squared * stiff[cell] * div
        after(cell, value + source(cell))


def widen_buoy(info, buoy, first, second, target):
    target[4 : 4 + CX] = buoy[...]
    odd = info[0] == 1

    @pl.when(odd)
    def _():
        target[0:4] = first[0:4]
        target[4 + CX : 8 + CX] = second[0:4]

    @pl.when(jnp.logical_not(odd))
    def _():
        target[0:4] = second[0:4]
        target[4 + CX : 8 + CX] = first[0:4]


def first_kernel(
    info, wave, now, now_a, now_b, before, stiff, buoy, edge_a, edge_b,
    p_out, send_b, div_out, slope_out, buoy_out,
    field, gx, gy, acc,
):
    widen_buoy(info, buoy, edge_a, edge_b, buoy_out)
    place(info, field, now[...], now_a[...], now_b[...], 7)

    def store(cell, value):
        p_out[cell] = value

    forward(info, wave, 0, now, before, stiff, field, buoy_out, gx, gy, acc, div_out, slope_out, store)
    for_partner(info, send_b, lambda: p_out[1:8], lambda: p_out[0:7])


def adjoint_part_kernel(
    info, p, last, after, scaled, edge_a, edge_b, buoy,
    send_a, q_out,
    field, gx, gy, acc,
):
    for_partner(info, send_a, lambda: p[0:7], lambda: p[1:8])
    place(info, field, scaled[...], edge_a[4:11], edge_b[4:11], 7)
    for cell, div in operate(field, 7, buoy, gx, gy, acc, lambda *_: None):
        q_out[cell] = 2.0 * last[cell] - after[cell] + step_squared * div


def second_kernel(
    info, wave, now, now_a, now_b, before, stiff, buoy,
    p_out, send_b, div_out, slope_out,
    field, gx, gy, acc,
):
    place(info, field, now[...], now_a[...], now_b[...], 7)

    def store(cell, value):
        p_out[cell] = value

    forward(info, wave, 1, now, before, stiff, field, buoy, gx, gy, acc, div_out, slope_out, store)
    for_partner(info, send_b, lambda: p_out[1:8], lambda: p_out[0:7])


def third_kernel(
    info, wave, now, now_a, now_b, before, stiff, buoy, q_part, spots,
    q_out, scaled, send_b, div_out, slope_out,
    field, gx, gy, acc,
):
    place(info, field, now[...], now_a[...], now_b[...], 7)

    def store(cell, value):
        q = q_part[cell] + (spots[0, cell] * value - spots[3, cell])
        q_out[cell] = q
        scaled[cell] = stiff[cell] * q

    forward(info, wave, 2, now, before, stiff, field, buoy, gx, gy, acc, div_out, slope_out, store)
    for_partner(info, send_b, lambda: scaled[1:8], lambda: scaled[0:7])


def adjoint_kernel(
    n, width, info, q_now, q_after, scaled, scaled_a, scaled_b, stiff, buoy, spots, p_then,
    q_out, scaled_out, send_b, slope_out,
    field, gx, gy, acc,
):
    place(info, field, scaled[...], scaled_a[...], scaled_b[...], 7)

    def keep(cell, sx, sy, sz):
        slope_out[0, cell] = sx
        slope_out[1, cell] = sy
        slope_out[2, cell] = sz

    for cell, total in operate(field, 7, buoy, gx, gy, acc, keep):
        q = 2.0 * q_now[cell] - q_after[cell] + step_squared * total
        q = q + (spots[0, cell] * p_then[cell] - spots[n + 1, cell])
        q_out[cell] = q
        scaled_out[cell] = stiff[cell] * q
    for_partner(info, send_b, lambda: scaled_out[CX - width : CX], lambda: scaled_out[0:width])


def adjoint_first_kernel(*refs):
    adjoint_kernel(1, 7, *refs)


def adjoint_second_kernel(*refs):
    adjoint_kernel(0, 4, *refs)


def image_first_kernel(info, scaled, q_now, slope_q, div, slope_p, q_new, send_a, out, q_out):
    q_out[...] = q_new[...]
    width = send_a.shape[0]
    for_partner(info, send_a, lambda: scaled[0:width], lambda: scaled[CX - width : CX])
    for cell in range(CX):
        out[0, cell] = q_now[cell] * div[cell]
        rho = slope_p[0, cell] * slope_q[0, cell] + slope_p[1, cell] * slope_q[1, cell]
        out[1, cell] = rho + slope_p[2, cell] * slope_q[2, cell]


def image_second_kernel(
    info, scaled, q_now, slope_q, div, slope_p, images, q_new, send_a, out, q_out
):
    q_out[...] = q_new[...]
    width = send_a.shape[0]
    for_partner(info, send_a, lambda: scaled[0:width], lambda: scaled[CX - width : CX])
    for cell in range(CX):
        out[0, cell] = images[0, cell] + q_now[cell] * div[cell]
        rho = slope_p[0, cell] * slope_q[0, cell] + slope_p[1, cell] * slope_q[1, cell]
        out[1, cell] = images[1, cell] + (rho + slope_p[2, cell] * slope_q[2, cell])


def image_kernel(info, q_now, scaled, scaled_a, scaled_b, div, slope, images, out, field):
    lane = lax.broadcasted_iota(jnp.int32, (CY, CZ), 1)
    place(info, field, scaled[...], scaled_a[...], scaled_b[...], 4)
    for cell in range(CX):
        plane = field[cell + 4, PAD : PAD + CY, :]
        rho = images[1, cell] + slope[0, cell] * slope_x(field, cell + 4)
        rho = rho + slope[1, cell] * slope_y(field, cell + 4)
        rho = rho + slope[2, cell] * slope_z(plane, lane)
        out[0, cell] = step_squared * (images[0, cell] + q_now[cell] * div[cell])
        out[1, cell] = -step_squared * rho


def gather_kernel(column, arrived, out_kappa, out_buoy):
    out_kappa[...] = jnp.zeros_like(out_kappa)
    out_buoy[...] = jnp.zeros_like(out_buoy)
    for s in range(arrived.shape[0]):
        t = column[s]
        out_kappa[t] = out_kappa[t] + arrived[s, 0]
        out_buoy[t] = out_buoy[t] + arrived[s, 1]


def work():
    return [
        pltpu.VMEM((WIDE, ROWS, CZ), F32),
        pltpu.VMEM((CX + 7, CY, CZ), F32),
        pltpu.VMEM((CX, ROWS, CZ), F32),
        pltpu.VMEM((CX, CY, CZ), F32),
    ]


def call(kernel, scalars, arrays, outs, scratch=(), flops=2_000_000):
    moved = sum(4 * a.size for a in arrays) + sum(4 * o.size for o in outs)
    return pl.pallas_call(
        kernel,
        out_shape=outs,
        in_specs=[SMEM] * len(scalars) + [VMEM] * len(arrays),
        out_specs=[VMEM] * len(outs),
        scratch_shapes=list(scratch),
        compiler_params=pltpu.CompilerParams(vmem_limit_bytes=32 * 1024 * 1024),
        cost_estimate=pl.CostEstimate(flops=flops, bytes_accessed=moved, transcendentals=0),
    )(*scalars, *arrays)


def swap_first(planes):
    count = lax.axis_size("dom")
    return lax.ppermute(planes, "dom", [(i ^ 1, i) for i in range(count)])


def swap_second(planes):
    pairs = []
    for i in range(1, lax.axis_size("dom") - 1, 2):
        pairs += [(i, i + 1), (i + 1, i)]
    return lax.ppermute(planes, "dom", pairs)


def shards(
    pressure_now,
    pressure_prev,
    adjoint_last,
    adjoint_after,
    kappa_model,
    buoy_model,
    aperture,
    source_cell,
    source_wave,
    receiver_cell,
    observed,
):
    dom = lax.axis_index("dom")
    odd = lax.rem(dom, 2)
    offset = dom * (CX * CY * CZ)
    source = source_cell[0]
    info = jnp.stack(
        [odd, source // (CY * CZ) - dom * CX, (source // CZ) % CY, source % CZ, offset]
    ).astype(jnp.int32)
    wave = source_wave[0]
    column = lax.dynamic_index_in_dim(aperture, dom, 1, keepdims=False)

    shots = aperture.shape[0]
    (chosen,) = call(
        choose_kernel,
        [dom.reshape(1).astype(jnp.int32), aperture],
        [kappa_model, buoy_model],
        [jax.ShapeDtypeStruct((shots, 2, CX, CZ), F32)],
    )
    block = lax.all_to_all(chosen, "shot", 0, 0, tiled=True)

    p0, p_prev = pressure_now[0], pressure_prev[0]
    q4, q5 = adjoint_last[0], adjoint_after[0]
    head, tail = p0[0:7], p0[1:8]
    p0_b = swap_second(jnp.where(odd == 1, tail, head))
    p0_a = swap_first(jnp.where(odd == 1, head, tail))
    (spots,) = call(
        receivers_kernel,
        [info],
        [receiver_cell, observed[0]],
        [jax.ShapeDtypeStruct((STEPS + 1, CX, CY, CZ), F32)],
        flops=400_000_000,
    )
    block, p0_a, p0_b, spots = lax.optimization_barrier((block, p0_a, p0_b, spots))

    stiff = block[:, 0].transpose(1, 0, 2)
    buoy = block[:, 1].transpose(1, 0, 2)
    own, seven, four = plane_field(CX), plane_field(7), plane_field(4)
    slopes = jax.ShapeDtypeStruct((3, CX, CY, CZ), F32)
    images = jax.ShapeDtypeStruct((2, CX, CY, CZ), F32)

    send_b, f4 = call(model_kernel, [info], [stiff, buoy, q4], [plane_field(11), own])
    edge_b = swap_second(send_b)
    (send_a,) = call(model_swap_kernel, [info], [buoy, f4], [plane_field(11)], flops=BESIDE)
    edge_a = swap_first(send_a)

    p1, send_b, div0, slope0, wide = call(
        first_kernel,
        [info, wave],
        [p0, p0_a, p0_b, p_prev, stiff, buoy, edge_a, edge_b],
        [own, seven, own, slopes, plane_field(CX + 8)],
        work(),
    )
    from_b = swap_second(send_b)
    send_a, q_part = call(
        adjoint_part_kernel, [info], [p1, q4, q5, f4, edge_a, edge_b, wide], [seven, own], work(), BESIDE
    )
    from_a = swap_first(send_a)

    p2, send_b, div1, slope1 = call(
        second_kernel,
        [info, wave],
        [p1, from_a, from_b, p0, stiff, wide],
        [own, seven, own, slopes],
        work(),
    )
    from_b = swap_second(send_b)
    (send_a,) = call(first_swap_kernel, [info], [p2], [seven], flops=BESIDE)
    from_a = swap_first(send_a)

    q3, f3, send_b, div2, slope2 = call(
        third_kernel,
        [info, wave],
        [p2, from_a, from_b, p1, stiff, wide, q_part, spots],
        [own, own, seven, own, slopes],
        work(),
    )
    from_b = swap_second(send_b)
    (send_a,) = call(first_swap_kernel, [info], [f3], [seven], flops=BESIDE)
    from_a = swap_first(send_a)

    q2, f2, send_b, slope_q = call(
        adjoint_first_kernel,
        [info],
        [q3, q4, f3, from_a, from_b, stiff, wide, spots, p2],
        [own, own, seven, slopes],
        work(),
    )
    from_b = swap_second(send_b)
    send_a, image, q2_out = call(
        image_first_kernel,
        [info],
        [f2, q3, slope_q, div2, slope2, q2],
        [seven, images, own],
        flops=BESIDE,
    )
    from_a = swap_first(send_a)

    q1, f1, send_b, slope_q = call(
        adjoint_second_kernel,
        [info],
        [q2, q3, f2, from_a, from_b, stiff, wide, spots, p1],
        [own, own, four, slopes],
        work(),
    )
    from_b = swap_second(send_b)
    send_a, image, q1_out = call(
        image_second_kernel,
        [info],
        [f1, q2, slope_q, div1, slope1, image, q1],
        [four, images, own],
        flops=BESIDE,
    )
    from_a = swap_first(send_a)

    (image,) = call(
        image_kernel,
        [info],
        [q1, f1, from_a, from_b, div0, slope0, image],
        [images],
        [pltpu.VMEM((CX + 8, ROWS, CZ), F32)],
    )
    arrived = lax.all_to_all(image.transpose(2, 0, 1, 3), "shot", 0, 0, tiled=True)
    tiles = jax.ShapeDtypeStruct((TILES, CX, CZ), F32)
    grad_kappa, grad_buoy = call(gather_kernel, [column], [arrived], [tiles, tiles])
    return (grad_kappa, grad_buoy, q1_out[None], q2_out[None])


def solution(mesh):
    in_specs = (
        P("shot", "dom", None, None),
        P("shot", "dom", None, None),
        P("shot", "dom", None, None),
        P("shot", "dom", None, None),
        P(None, "dom", "shot"),
        P(None, "dom", "shot"),
        P(),
        P("shot"),
        P("shot", None),
        P("shot", None),
        P("shot", None, None),
    )
    out_specs = (
        P(None, "dom", "shot"),
        P(None, "dom", "shot"),
        P("shot", "dom", None, None),
        P("shot", "dom", None, None),
    )
    return jax.shard_map(shards, mesh=mesh, in_specs=in_specs, out_specs=out_specs, check_vma=False)
```

```python
import jax
import jax.numpy as jnp
from jax import lax
from jax.experimental import pallas as pl
from jax.experimental.pallas import tpu as pltpu
from jax.sharding import PartitionSpec as P

CX = 8
CY = 32
CZ = 128
TILES = 4
STEPS = 3
REC = 512
PAD = 8
ROWS = CY + 2 * PAD
WIDE = CX + 14

COEFFS = (1225.0 / 1024.0, -245.0 / 3072.0, 49.0 / 5120.0, -5.0 / 7168.0)
step_squared = 0.02

VMEM = pl.BlockSpec(memory_space=pltpu.VMEM)
SMEM = pl.BlockSpec(memory_space=pltpu.SMEM)
F32 = jnp.float32


def plane_field(count):
    return jax.ShapeDtypeStruct((count, CY, CZ), F32)


def lane_shift(plane, by, lane):
    if by == 0:
        return plane
    moved = pltpu.roll(plane, (-by) % CZ, 1)
    keep = lane < CZ - by if by > 0 else lane >= -by
    return jnp.where(keep, moved, 0.0)


def stencil(at):
    total = COEFFS[0] * (at(0) - at(-1))
    for k in range(2, 5):
        total = total + COEFFS[k - 1] * (at(k - 1) - at(-k))
    return total


def place(info, target, own, first, second, width):
    target[:, 0:PAD, :] = jnp.zeros((target.shape[0], PAD, CZ), F32)
    target[:, PAD + CY : ROWS, :] = jnp.zeros((target.shape[0], PAD, CZ), F32)
    inner = slice(PAD, PAD + CY)
    target[width : width + CX, inner, :] = own
    odd = info[0] == 1

    @pl.when(odd)
    def _():
        target[0:width, inner, :] = first
        target[width + CX : 2 * width + CX, inner, :] = second[0:width]

    @pl.when(jnp.logical_not(odd))
    def _():
        target[0:width, inner, :] = second[CX - width : CX]
        target[width + CX : 2 * width + CX, inner, :] = first


def for_partner(info, target, head, tail):
    odd = info[0] == 1

    @pl.when(odd)
    def _():
        target[...] = head()

    @pl.when(jnp.logical_not(odd))
    def _():
        target[...] = tail()


def hand_over(info, send_a, field):
    width = send_a.shape[0]
    for_partner(info, send_a, lambda: field[0:width], lambda: field[CX - width : CX])


def slope_x(field, at):
    return stencil(lambda s: field[at + s, PAD : PAD + CY, :])


def slope_y(field, at):
    return stencil(lambda s: field[at, PAD + s : PAD + CY + s, :])


def slope_z(plane, lane):
    return stencil(lambda s: lane_shift(plane, s, lane))


def operate(field, width, buoy, gx, gy, acc, slopes):
    lane = lax.broadcasted_iota(jnp.int32, (CY, CZ), 1)
    gy[:, 0:PAD, :] = jnp.zeros((CX, PAD, CZ), F32)
    gy[:, PAD + CY : ROWS, :] = jnp.zeros((CX, PAD, CZ), F32)
    for cell in range(-3, CX + 4):
        sx = slope_x(field, cell + width)
        gx[cell + 3] = buoy[cell + 4] * sx
        if 0 <= cell < CX:
            weight = buoy[cell + 4]
            plane = field[cell + width, PAD : PAD + CY, :]
            sy = slope_y(field, cell + width)
            sz = slope_z(plane, lane)
            gy[cell, PAD : PAD + CY, :] = weight * sy
            gz = weight * sz
            acc[cell] = stencil(lambda s: lane_shift(gz, s + 1, lane))
            slopes(cell, sx, sy, sz)
    for cell in range(CX):
        div = stencil(lambda s: gx[cell + 4 + s])
        div = div + stencil(lambda s: gy[cell, PAD + 1 + s : PAD + 1 + s + CY, :])
        yield cell, div + acc[cell]


def prepare_kernel(
    info, wave, cells, seen, now, before, last, after, out, base_p, base_q, last_out, source_out
):
    base_p[...] = 2.0 * now[...] - before[...]
    base_q[...] = 2.0 * last[...] - after[...]
    last_out[...] = last[...]
    y = lax.broadcasted_iota(jnp.int32, (CY, CZ), 0)
    z = lax.broadcasted_iota(jnp.int32, (CY, CZ), 1)
    hit = (y == info[2]) & (z == info[3])
    for n in range(STEPS):
        source_out[n] = jnp.where(hit, wave[n], 0.0)

    index = cells[...] - info[4]
    row = lax.shift_right_arithmetic(index, 7)
    z = lax.bitwise_and(index, 127)
    rows = lax.broadcasted_iota(jnp.int32, (CX * CY, REC), 0)
    pick = jnp.where(rows == row, 1.0, 0.0).astype(jnp.bfloat16)
    lanes = lax.broadcasted_iota(jnp.int32, (CZ, REC), 0)
    here = lanes == z

    def spread(values):
        right = jnp.where(here, values, 0.0).astype(jnp.bfloat16)
        return lax.dot_general(
            pick, right, (((1,), (1,)), ((), ())), preferred_element_type=F32
        )

    out[0] = spread(jnp.ones((1, REC), F32)).reshape(CX, CY, CZ)
    for n in range(STEPS):
        rest = seen[n : n + 1, :]
        total = None
        for _ in range(3):
            part = rest.astype(jnp.bfloat16).astype(F32)
            rest = rest - part
            total = spread(part) if total is None else total + spread(part)
        out[n + 1] = total.reshape(CX, CY, CZ)


def model_kernel(info, stiff, buoy, last, send_a, send_b, scaled):
    scaled[...] = stiff[...] * last[...]
    send_b[0:8] = buoy[...]
    send_b[8:16] = scaled[...]
    for_partner(
        info,
        send_a,
        lambda: jnp.concatenate([buoy[0:4], scaled[0:7]], axis=0),
        lambda: jnp.concatenate([buoy[4:8], scaled[1:8]], axis=0),
    )


def forward(info, source, base, stiff, field, buoy, gx, gy, acc, div_out, slope_out, store):
    def keep(cell, sx, sy, sz):
        slope_out[0, cell] = sx
        slope_out[1, cell] = sy
        slope_out[2, cell] = sz

    for cell, div in operate(field, 7, buoy, gx, gy, acc, keep):
        div_out[cell] = div
        value = base(cell) + step_squared * stiff[cell] * div
        store(cell, value + jnp.where(info[1] == cell, source, 0.0))


def widen_buoy(info, buoy, first, second, target):
    target[4 : 4 + CX] = buoy[...]
    odd = info[0] == 1

    @pl.when(odd)
    def _():
        target[0:4] = first[0:4]
        target[4 + CX : 8 + CX] = second[0:4]

    @pl.when(jnp.logical_not(odd))
    def _():
        target[0:4] = second[4:8]
        target[4 + CX : 8 + CX] = first[0:4]


def first_kernel(
    info, now, now_a, now_b, base, source, stiff, buoy, edge_a, edge_b,
    p_out, send_a, div_out, slope_out, buoy_out,
    field, gx, gy, acc,
):
    widen_buoy(info, buoy, edge_a, edge_b, buoy_out)
    place(info, field, now[...], now_a[...], now_b[...], 7)

    def store(cell, value):
        p_out[cell] = value

    forward(
        info, source[0], lambda cell: base[cell],
        stiff, field, buoy_out, gx, gy, acc, div_out, slope_out, store,
    )
    hand_over(info, send_a, p_out)


def adjoint_part_kernel(
    info, base, scaled, edge_a, edge_b, buoy,
    q_out,
    field, gx, gy, acc,
):
    place(info, field, scaled[...], edge_a[4:11], edge_b[8:16], 7)
    for cell, div in operate(field, 7, buoy, gx, gy, acc, lambda *_: None):
        q_out[cell] = base[cell] + step_squared * div


def second_kernel(
    info, now, now_a, now_b, before, source, stiff, buoy,
    p_out, send_a, div_out, slope_out,
    field, gx, gy, acc,
):
    place(info, field, now[...], now_a[...], now_b[...], 7)

    def store(cell, value):
        p_out[cell] = value

    forward(
        info, source[1], lambda cell: 2.0 * now[cell] - before[cell],
        stiff, field, buoy, gx, gy, acc, div_out, slope_out, store,
    )
    hand_over(info, send_a, p_out)


def third_kernel(
    info, now, now_a, now_b, before, source, stiff, buoy, q_part, spots,
    q_out, scaled, send_a, div_out, slope_out,
    field, gx, gy, acc,
):
    place(info, field, now[...], now_a[...], now_b[...], 7)

    def store(cell, value):
        q = q_part[cell] + (spots[0, cell] * value - spots[3, cell])
        q_out[cell] = q
        scaled[cell] = stiff[cell] * q

    forward(
        info, source[2], lambda cell: 2.0 * now[cell] - before[cell],
        stiff, field, buoy, gx, gy, acc, div_out, slope_out, store,
    )
    hand_over(info, send_a, scaled)


def adjoint_kernel(
    n, info, q_now, q_after, scaled, scaled_a, scaled_b, stiff, buoy, spots, p_then,
    q_out, scaled_out, send_a, slope_out,
    field, gx, gy, acc,
):
    place(info, field, scaled[...], scaled_a[...], scaled_b[...], 7)

    def keep(cell, sx, sy, sz):
        slope_out[0, cell] = sx
        slope_out[1, cell] = sy
        slope_out[2, cell] = sz

    for cell, total in operate(field, 7, buoy, gx, gy, acc, keep):
        q = 2.0 * q_now[cell] - q_after[cell] + step_squared * total
        q = q + (spots[0, cell] * p_then[cell] - spots[n + 1, cell])
        q_out[cell] = q
        scaled_out[cell] = stiff[cell] * q
    hand_over(info, send_a, scaled_out)


def adjoint_first_kernel(*refs):
    adjoint_kernel(1, *refs)


def adjoint_second_kernel(*refs):
    adjoint_kernel(0, *refs)


def image_first_kernel(q_now, slope_q, div, slope_p, q_new, out, q_out):
    q_out[...] = q_new[...]
    for cell in range(CX):
        out[0, cell] = q_now[cell] * div[cell]
        rho = slope_p[0, cell] * slope_q[0, cell] + slope_p[1, cell] * slope_q[1, cell]
        out[1, cell] = rho + slope_p[2, cell] * slope_q[2, cell]


def image_second_kernel(
    q_now, slope_q, div, slope_p, images, q_new, out, q_out
):
    q_out[...] = q_new[...]
    for cell in range(CX):
        out[0, cell] = images[0, cell] + q_now[cell] * div[cell]
        rho = slope_p[0, cell] * slope_q[0, cell] + slope_p[1, cell] * slope_q[1, cell]
        out[1, cell] = images[1, cell] + (rho + slope_p[2, cell] * slope_q[2, cell])


def image_kernel(info, q_now, scaled, scaled_a, scaled_b, div, slope, images, out, field):
    lane = lax.broadcasted_iota(jnp.int32, (CY, CZ), 1)
    place(info, field, scaled[...], scaled_a[...], scaled_b[...], 4)
    for cell in range(CX):
        plane = field[cell + 4, PAD : PAD + CY, :]
        rho = images[1, cell] + slope[0, cell] * slope_x(field, cell + 4)
        rho = rho + slope[1, cell] * slope_y(field, cell + 4)
        rho = rho + slope[2, cell] * slope_z(plane, lane)
        out[0, cell] = step_squared * (images[0, cell] + q_now[cell] * div[cell])
        out[1, cell] = -step_squared * rho


def gather_kernel(picked, arrived, out_kappa, out_buoy):
    for t in range(TILES):
        kappa = jnp.zeros((CX, CZ), F32)
        rho = jnp.zeros((CX, CZ), F32)
        for s in range(arrived.shape[0]):
            here = picked[t, s : s + 1, :] > 0.0
            kappa = kappa + jnp.where(here, arrived[s, 0], 0.0)
            rho = rho + jnp.where(here, arrived[s, 1], 0.0)
        out_kappa[t] = kappa
        out_buoy[t] = rho


def work():
    return [
        pltpu.VMEM((WIDE, ROWS, CZ), F32),
        pltpu.VMEM((CX + 7, CY, CZ), F32),
        pltpu.VMEM((CX, ROWS, CZ), F32),
        pltpu.VMEM((CX, CY, CZ), F32),
    ]


def call(kernel, scalars, arrays, outs, scratch=(), flops=2_000_000):
    moved = sum(4 * a.size for a in arrays) + sum(4 * o.size for o in outs)
    return pl.pallas_call(
        kernel,
        out_shape=outs,
        in_specs=[SMEM] * len(scalars) + [VMEM] * len(arrays),
        out_specs=[VMEM] * len(outs),
        scratch_shapes=list(scratch),
        compiler_params=pltpu.CompilerParams(vmem_limit_bytes=32 * 1024 * 1024),
        cost_estimate=pl.CostEstimate(flops=flops, bytes_accessed=moved, transcendentals=0),
    )(*scalars, *arrays)


def swap_first(planes):
    count = lax.axis_size("dom")
    return lax.ppermute(planes, "dom", [(i ^ 1, i) for i in range(count)])


def swap_second(planes):
    pairs = []
    for i in range(1, lax.axis_size("dom") - 1, 2):
        pairs += [(i, i + 1), (i + 1, i)]
    return lax.ppermute(planes, "dom", pairs)


def shards(
    pressure_now,
    pressure_prev,
    adjoint_last,
    adjoint_after,
    kappa_model,
    buoy_model,
    aperture,
    source_cell,
    source_wave,
    receiver_cell,
    observed,
):
    dom = lax.axis_index("dom")
    odd = lax.rem(dom, 2)
    offset = dom * (CX * CY * CZ)
    source = source_cell[0]
    info = jnp.stack(
        [odd, source // (CY * CZ) - dom * CX, (source // CZ) % CY, source % CZ, offset]
    ).astype(jnp.int32)

    column = lax.dynamic_index_in_dim(aperture, dom, 1, keepdims=False)
    stacked = jnp.stack((kappa_model, buoy_model), axis=1)
    picks = column[:, None, None, None]
    chosen = stacked[0][None]
    for t in range(1, TILES):
        chosen = jnp.where(picks == t, stacked[t][None], chosen)
    block = lax.all_to_all(chosen, "shot", 0, 0, tiled=True)

    p0, p_prev = pressure_now[0], pressure_prev[0]
    q4, q5 = adjoint_last[0], adjoint_after[0]
    p0_b = swap_second(p0)
    p0_a = swap_first(jnp.where(odd == 1, p0[0:7], p0[1:8]))
    own, seven, four = plane_field(CX), plane_field(7), plane_field(4)
    spots, base_p, base_q, q4, source_planes = call(
        prepare_kernel,
        [info, source_wave[0]],
        [receiver_cell, observed[0], p0, p_prev, q4, q5],
        [jax.ShapeDtypeStruct((STEPS + 1, CX, CY, CZ), F32), own, own, own, plane_field(STEPS)],
        flops=400_000_000,
    )
    ids = jnp.arange(TILES, dtype=jnp.int32)[:, None, None]
    picked = jnp.broadcast_to(
        (column[None, :, None] == ids).astype(F32), (TILES, column.shape[0], CZ)
    )
    block, p0_a, p0_b, spots, base_p, base_q, q4, source_planes, picked = lax.optimization_barrier(
        (block, p0_a, p0_b, spots, base_p, base_q, q4, source_planes, picked)
    )

    stiff = block[:, 0].transpose(1, 0, 2)
    buoy = block[:, 1].transpose(1, 0, 2)
    slopes = jax.ShapeDtypeStruct((3, CX, CY, CZ), F32)
    images = jax.ShapeDtypeStruct((2, CX, CY, CZ), F32)

    send_a, send_b, f4 = call(
        model_kernel, [info], [stiff, buoy, q4], [plane_field(11), plane_field(16), own]
    )
    edge_b = swap_second(send_b)
    edge_a = swap_first(send_a)

    p1, send_a, div0, slope0, wide = call(
        first_kernel,
        [info],
        [p0, p0_a, p0_b, base_p, source_planes, stiff, buoy, edge_a, edge_b],
        [own, seven, own, slopes, plane_field(CX + 8)],
        work(),
    )
    from_b = swap_second(p1)
    (q_part,) = call(adjoint_part_kernel, [info], [base_q, f4, edge_a, edge_b, wide], [own], work())
    from_a = swap_first(send_a)

    p2, send_a, div1, slope1 = call(
        second_kernel,
        [info],
        [p1, from_a, from_b, p0, source_planes, stiff, wide],
        [own, seven, own, slopes],
        work(),
    )
    from_b = swap_second(p2)
    from_a = swap_first(send_a)

    q3, f3, send_a, div2, slope2 = call(
        third_kernel,
        [info],
        [p2, from_a, from_b, p1, source_planes, stiff, wide, q_part, spots],
        [own, own, seven, own, slopes],
        work(),
    )
    from_b = swap_second(f3)
    from_a = swap_first(send_a)

    q2, f2, send_a, slope_q = call(
        adjoint_first_kernel,
        [info],
        [q3, q4, f3, from_a, from_b, stiff, wide, spots, p2],
        [own, own, seven, slopes],
        work(),
    )
    from_b = swap_second(f2)
    from_a = swap_first(send_a)
    image, q2_out = call(image_first_kernel, [], [q3, slope_q, div2, slope2, q2], [images, own])

    q1, f1, send_a, slope_q = call(
        adjoint_second_kernel,
        [info],
        [q2, q3, f2, from_a, from_b, stiff, wide, spots, p1],
        [own, own, four, slopes],
        work(),
    )
    from_b = swap_second(f1)
    from_a = swap_first(send_a)
    image, q1_out = call(
        image_second_kernel, [], [q2, slope_q, div1, slope1, image, q1], [images, own]
    )

    (image,) = call(
        image_kernel,
        [info],
        [q1, f1, from_a, from_b, div0, slope0, image],
        [images],
        [pltpu.VMEM((CX + 8, ROWS, CZ), F32)],
    )
    arrived = lax.all_to_all(image.transpose(2, 0, 1, 3), "shot", 0, 0, tiled=True)
    tiles = jax.ShapeDtypeStruct((TILES, CX, CZ), F32)
    grad_kappa, grad_buoy = call(gather_kernel, [], [picked, arrived], [tiles, tiles])
    return (grad_kappa, grad_buoy, q1_out[None], q2_out[None])


def solution(mesh):
    in_specs = (
        P("shot", "dom", None, None),
        P("shot", "dom", None, None),
        P("shot", "dom", None, None),
        P("shot", "dom", None, None),
        P(None, "dom", "shot"),
        P(None, "dom", "shot"),
        P(),
        P("shot"),
        P("shot", None),
        P("shot", None),
        P("shot", None, None),
    )
    out_specs = (
        P(None, "dom", "shot"),
        P(None, "dom", "shot"),
        P("shot", "dom", None, None),
        P("shot", "dom", None, None),
    )
    return jax.shard_map(shards, mesh=mesh, in_specs=in_specs, out_specs=out_specs, check_vma=False)
```

```python
import jax
import jax.numpy as jnp
from jax import lax
from jax.experimental import pallas as pl
from jax.experimental.pallas import tpu as pltpu
from jax.sharding import PartitionSpec as P

CX = 8
CY = 32
CZ = 128
TILES = 4
STEPS = 3
REC = 512
PAD = 8
ROWS = CY + 2 * PAD
WIDE = CX + 14

COEFFS = (1225.0 / 1024.0, -245.0 / 3072.0, 49.0 / 5120.0, -5.0 / 7168.0)
step_squared = 0.02

VMEM = pl.BlockSpec(memory_space=pltpu.VMEM)
SMEM = pl.BlockSpec(memory_space=pltpu.SMEM)
F32 = jnp.float32


def plane_field(count):
    return jax.ShapeDtypeStruct((count, CY, CZ), F32)


def lane_shift(plane, by, lane):
    if by == 0:
        return plane
    moved = pltpu.roll(plane, (-by) % CZ, 1)
    keep = lane < CZ - by if by > 0 else lane >= -by
    return jnp.where(keep, moved, 0.0)


def stencil(at):
    total = COEFFS[0] * (at(0) - at(-1))
    for k in range(2, 5):
        total = total + COEFFS[k - 1] * (at(k - 1) - at(-k))
    return total


def place(info, target, own, first, second, width):
    target[:, 0:PAD, :] = jnp.zeros((target.shape[0], PAD, CZ), F32)
    target[:, PAD + CY : ROWS, :] = jnp.zeros((target.shape[0], PAD, CZ), F32)
    inner = slice(PAD, PAD + CY)
    target[width : width + CX, inner, :] = own
    odd = info[0] == 1

    @pl.when(odd)
    def _():
        target[0:width, inner, :] = first
        target[width + CX : 2 * width + CX, inner, :] = second[0:width]

    @pl.when(jnp.logical_not(odd))
    def _():
        target[0:width, inner, :] = second[second.shape[0] - width :]
        target[width + CX : 2 * width + CX, inner, :] = first


def for_partner(info, target, head, tail):
    odd = info[0] == 1

    @pl.when(odd)
    def _():
        target[...] = head()

    @pl.when(jnp.logical_not(odd))
    def _():
        target[...] = tail()


def hand_over(info, send_a, field):
    width = send_a.shape[0]
    for_partner(info, send_a, lambda: field[0:width], lambda: field[CX - width : CX])


def slope_x(field, at):
    return stencil(lambda s: field[at + s, PAD : PAD + CY, :])


def slope_y(field, at):
    return stencil(lambda s: field[at, PAD + s : PAD + CY + s, :])


def slope_z(plane, lane):
    return stencil(lambda s: lane_shift(plane, s, lane))


def operate(field, width, buoy, gx, gy, acc, slopes):
    lane = lax.broadcasted_iota(jnp.int32, (CY, CZ), 1)
    gy[:, 0:PAD, :] = jnp.zeros((CX, PAD, CZ), F32)
    gy[:, PAD + CY : ROWS, :] = jnp.zeros((CX, PAD, CZ), F32)
    for cell in range(-3, CX + 4):
        sx = slope_x(field, cell + width)
        gx[cell + 3] = buoy[cell + 4] * sx
        if 0 <= cell < CX:
            weight = buoy[cell + 4]
            plane = field[cell + width, PAD : PAD + CY, :]
            sy = slope_y(field, cell + width)
            sz = slope_z(plane, lane)
            gy[cell, PAD : PAD + CY, :] = weight * sy
            gz = weight * sz
            acc[cell] = stencil(lambda s: lane_shift(gz, s + 1, lane))
            slopes(cell, sx, sy, sz)
    for cell in range(CX):
        div = stencil(lambda s: gx[cell + 4 + s])
        div = div + stencil(lambda s: gy[cell, PAD + 1 + s : PAD + 1 + s + CY, :])
        yield cell, div + acc[cell]


def prepare_kernel(
    info, wave, cells, seen, now, before, last, after, out, base_p, base_q, now_out, last_out, source_out
):
    base_p[...] = 2.0 * now[...] - before[...]
    base_q[...] = 2.0 * last[...] - after[...]
    now_out[...] = now[...]
    last_out[...] = last[...]
    y = lax.broadcasted_iota(jnp.int32, (CY, CZ), 0)
    z = lax.broadcasted_iota(jnp.int32, (CY, CZ), 1)
    hit = (y == info[2]) & (z == info[3])
    for n in range(STEPS):
        source_out[n] = jnp.where(hit, wave[n], 0.0)

    index = cells[...] - info[4]
    row = lax.shift_right_arithmetic(index, 7)
    z = lax.bitwise_and(index, 127)
    rows = lax.broadcasted_iota(jnp.int32, (CX * CY, REC), 0)
    pick = jnp.where(rows == row, 1.0, 0.0).astype(jnp.bfloat16)
    lanes = lax.broadcasted_iota(jnp.int32, (CZ, REC), 0)
    here = lanes == z

    def spread(values):
        right = jnp.where(here, values, 0.0).astype(jnp.bfloat16)
        return lax.dot_general(
            pick, right, (((1,), (1,)), ((), ())), preferred_element_type=F32
        )

    out[0] = spread(jnp.ones((1, REC), F32)).reshape(CX, CY, CZ)
    for n in range(STEPS):
        rest = seen[n : n + 1, :]
        total = None
        for _ in range(3):
            part = rest.astype(jnp.bfloat16).astype(F32)
            rest = rest - part
            total = spread(part) if total is None else total + spread(part)
        out[n + 1] = total.reshape(CX, CY, CZ)


def model_kernel(info, stiff, buoy, last, now, send_a, send_b, scaled):
    scaled[...] = stiff[...] * last[...]
    send_b[4:12] = now[...]
    for_partner(
        info,
        send_a,
        lambda: jnp.concatenate([buoy[0:4], now[0:7]], axis=0),
        lambda: jnp.concatenate([buoy[4:8], now[1:8]], axis=0),
    )
    for_partner(info, send_b.at[0:4], lambda: buoy[4:8], lambda: buoy[0:4])


def forward(info, source, base, stiff, field, buoy, gx, gy, acc, div_out, slope_out, store):
    def keep(cell, sx, sy, sz):
        slope_out[0, cell] = sx
        slope_out[1, cell] = sy
        slope_out[2, cell] = sz

    for cell, div in operate(field, 7, buoy, gx, gy, acc, keep):
        div_out[cell] = div
        value = base(cell) + step_squared * stiff[cell] * div
        store(cell, value + jnp.where(info[1] == cell, source, 0.0))


def widen_buoy(info, buoy, first, second, target):
    target[4 : 4 + CX] = buoy[...]
    odd = info[0] == 1

    @pl.when(odd)
    def _():
        target[0:4] = first[0:4]
        target[4 + CX : 8 + CX] = second[0:4]

    @pl.when(jnp.logical_not(odd))
    def _():
        target[0:4] = second[0:4]
        target[4 + CX : 8 + CX] = first[0:4]


def first_kernel(
    info, now, base, source, stiff, buoy, edge_a, edge_b, scaled,
    p_out, send_a, send_b, div_out, slope_out, buoy_out,
    field, gx, gy, acc,
):
    widen_buoy(info, buoy, edge_a, edge_b, buoy_out)
    place(info, field, now[...], edge_a[4:11], edge_b[4:12], 7)

    def store(cell, value):
        p_out[cell] = value

    forward(
        info, source[0], lambda cell: base[cell],
        stiff, field, buoy_out, gx, gy, acc, div_out, slope_out, store,
    )
    send_b[0:8] = p_out[...]
    for_partner(
        info,
        send_a,
        lambda: jnp.concatenate([p_out[0:7], scaled[0:7]], axis=0),
        lambda: jnp.concatenate([p_out[1:8], scaled[1:8]], axis=0),
    )
    for_partner(info, send_b.at[8:15], lambda: scaled[1:8], lambda: scaled[0:7])


def adjoint_part_kernel(
    info, base, scaled, both_a, both_b, buoy,
    q_out,
    field, gx, gy, acc,
):
    place(info, field, scaled[...], both_a[7:14], both_b[8:15], 7)
    for cell, div in operate(field, 7, buoy, gx, gy, acc, lambda *_: None):
        q_out[cell] = base[cell] + step_squared * div


def second_kernel(
    info, now, now_a, now_b, before, source, stiff, buoy,
    p_out, send_a, div_out, slope_out,
    field, gx, gy, acc,
):
    place(info, field, now[...], now_a[0:7], now_b[0:8], 7)

    def store(cell, value):
        p_out[cell] = value

    forward(
        info, source[1], lambda cell: 2.0 * now[cell] - before[cell],
        stiff, field, buoy, gx, gy, acc, div_out, slope_out, store,
    )
    hand_over(info, send_a, p_out)


def third_kernel(
    info, now, now_a, now_b, before, source, stiff, buoy, q_part, spots,
    q_out, scaled, send_a, div_out, slope_out,
    field, gx, gy, acc,
):
    place(info, field, now[...], now_a[...], now_b[...], 7)

    def store(cell, value):
        q = q_part[cell] + (spots[0, cell] * value - spots[3, cell])
        q_out[cell] = q
        scaled[cell] = stiff[cell] * q

    forward(
        info, source[2], lambda cell: 2.0 * now[cell] - before[cell],
        stiff, field, buoy, gx, gy, acc, div_out, slope_out, store,
    )
    hand_over(info, send_a, scaled)


def adjoint_kernel(
    n, info, q_now, q_after, scaled, scaled_a, scaled_b, stiff, buoy, spots, p_then,
    q_out, scaled_out, send_a, slope_out,
    field, gx, gy, acc,
):
    place(info, field, scaled[...], scaled_a[...], scaled_b[...], 7)

    def keep(cell, sx, sy, sz):
        slope_out[0, cell] = sx
        slope_out[1, cell] = sy
        slope_out[2, cell] = sz

    for cell, total in operate(field, 7, buoy, gx, gy, acc, keep):
        q = 2.0 * q_now[cell] - q_after[cell] + step_squared * total
        q = q + (spots[0, cell] * p_then[cell] - spots[n + 1, cell])
        q_out[cell] = q
        scaled_out[cell] = stiff[cell] * q
    hand_over(info, send_a, scaled_out)


def adjoint_first_kernel(*refs):
    adjoint_kernel(1, *refs)


def adjoint_second_kernel(*refs):
    adjoint_kernel(0, *refs)


def image_first_kernel(q_now, slope_q, div, slope_p, q_new, out, q_out):
    q_out[...] = q_new[...]
    for cell in range(CX):
        out[0, cell] = q_now[cell] * div[cell]
        rho = slope_p[0, cell] * slope_q[0, cell] + slope_p[1, cell] * slope_q[1, cell]
        out[1, cell] = rho + slope_p[2, cell] * slope_q[2, cell]


def image_second_kernel(
    q_now, slope_q, div, slope_p, images, q_new, out, q_out
):
    q_out[...] = q_new[...]
    for cell in range(CX):
        out[0, cell] = images[0, cell] + q_now[cell] * div[cell]
        rho = slope_p[0, cell] * slope_q[0, cell] + slope_p[1, cell] * slope_q[1, cell]
        out[1, cell] = images[1, cell] + (rho + slope_p[2, cell] * slope_q[2, cell])


def image_kernel(info, q_now, scaled, scaled_a, scaled_b, div, slope, images, out, field):
    lane = lax.broadcasted_iota(jnp.int32, (CY, CZ), 1)
    place(info, field, scaled[...], scaled_a[...], scaled_b[...], 4)
    for cell in range(CX):
        plane = field[cell + 4, PAD : PAD + CY, :]
        rho = images[1, cell] + slope[0, cell] * slope_x(field, cell + 4)
        rho = rho + slope[1, cell] * slope_y(field, cell + 4)
        rho = rho + slope[2, cell] * slope_z(plane, lane)
        out[0, cell] = step_squared * (images[0, cell] + q_now[cell] * div[cell])
        out[1, cell] = -step_squared * rho


def gather_kernel(picked, arrived, out_kappa, out_buoy):
    for t in range(TILES):
        kappa = jnp.zeros((CX, CZ), F32)
        rho = jnp.zeros((CX, CZ), F32)
        for s in range(arrived.shape[0]):
            here = picked[t, s : s + 1, :] > 0.0
            kappa = kappa + jnp.where(here, arrived[s, 0], 0.0)
            rho = rho + jnp.where(here, arrived[s, 1], 0.0)
        out_kappa[t] = kappa
        out_buoy[t] = rho


def work():
    return [
        pltpu.VMEM((WIDE, ROWS, CZ), F32),
        pltpu.VMEM((CX + 7, CY, CZ), F32),
        pltpu.VMEM((CX, ROWS, CZ), F32),
        pltpu.VMEM((CX, CY, CZ), F32),
    ]


def call(kernel, scalars, arrays, outs, scratch=(), flops=2_000_000):
    moved = sum(4 * a.size for a in arrays) + sum(4 * o.size for o in outs)
    return pl.pallas_call(
        kernel,
        out_shape=outs,
        in_specs=[SMEM] * len(scalars) + [VMEM] * len(arrays),
        out_specs=[VMEM] * len(outs),
        scratch_shapes=list(scratch),
        compiler_params=pltpu.CompilerParams(vmem_limit_bytes=32 * 1024 * 1024),
        cost_estimate=pl.CostEstimate(flops=flops, bytes_accessed=moved, transcendentals=0),
    )(*scalars, *arrays)


def swap_first(planes):
    count = lax.axis_size("dom")
    return lax.ppermute(planes, "dom", [(i ^ 1, i) for i in range(count)])


def swap_second(planes):
    pairs = []
    for i in range(1, lax.axis_size("dom") - 1, 2):
        pairs += [(i, i + 1), (i + 1, i)]
    return lax.ppermute(planes, "dom", pairs)


def shards(
    pressure_now,
    pressure_prev,
    adjoint_last,
    adjoint_after,
    kappa_model,
    buoy_model,
    aperture,
    source_cell,
    source_wave,
    receiver_cell,
    observed,
):
    dom = lax.axis_index("dom")
    odd = lax.rem(dom, 2)
    offset = dom * (CX * CY * CZ)
    source = source_cell[0]
    info = jnp.stack(
        [odd, source // (CY * CZ) - dom * CX, (source // CZ) % CY, source % CZ, offset]
    ).astype(jnp.int32)

    column = lax.dynamic_index_in_dim(aperture, dom, 1, keepdims=False)
    stacked = jnp.stack((kappa_model, buoy_model), axis=1)
    picks = column[:, None, None, None]
    chosen = stacked[0][None]
    for t in range(1, TILES):
        chosen = jnp.where(picks == t, stacked[t][None], chosen)
    block = lax.all_to_all(chosen, "shot", 0, 0, tiled=True)

    p0, p_prev = pressure_now[0], pressure_prev[0]
    q4, q5 = adjoint_last[0], adjoint_after[0]
    own, seven, four = plane_field(CX), plane_field(7), plane_field(4)
    spots, base_p, base_q, p0, q4, source_planes = call(
        prepare_kernel,
        [info, source_wave[0]],
        [receiver_cell, observed[0], p0, p_prev, q4, q5],
        [jax.ShapeDtypeStruct((STEPS + 1, CX, CY, CZ), F32), own, own, own, own, plane_field(STEPS)],
        flops=400_000_000,
    )
    ids = jnp.arange(TILES, dtype=jnp.int32)[:, None, None]
    picked = jnp.broadcast_to(
        (column[None, :, None] == ids).astype(F32), (TILES, column.shape[0], CZ)
    )
    block, spots, base_p, base_q, p0, q4, source_planes, picked = lax.optimization_barrier(
        (block, spots, base_p, base_q, p0, q4, source_planes, picked)
    )

    stiff = block[:, 0].transpose(1, 0, 2)
    buoy = block[:, 1].transpose(1, 0, 2)
    slopes = jax.ShapeDtypeStruct((3, CX, CY, CZ), F32)
    images = jax.ShapeDtypeStruct((2, CX, CY, CZ), F32)

    send_a, send_b, f4 = call(
        model_kernel, [info], [stiff, buoy, q4, p0], [plane_field(11), plane_field(12), own]
    )
    edge_b = swap_second(send_b)
    edge_a = swap_first(send_a)

    p1, send_a, send_b, div0, slope0, wide = call(
        first_kernel,
        [info],
        [p0, base_p, source_planes, stiff, buoy, edge_a, edge_b, f4],
        [own, plane_field(14), plane_field(15), own, slopes, plane_field(CX + 8)],
        work(),
    )
    both_b = swap_second(send_b)
    both_a = swap_first(send_a)
    (q_part,) = call(adjoint_part_kernel, [info], [base_q, f4, both_a, both_b, wide], [own], work())

    p2, send_a, div1, slope1 = call(
        second_kernel,
        [info],
        [p1, both_a, both_b, p0, source_planes, stiff, wide],
        [own, seven, own, slopes],
        work(),
    )
    from_b = swap_second(p2)
    from_a = swap_first(send_a)

    q3, f3, send_a, div2, slope2 = call(
        third_kernel,
        [info],
        [p2, from_a, from_b, p1, source_planes, stiff, wide, q_part, spots],
        [own, own, seven, own, slopes],
        work(),
    )
    from_b = swap_second(f3)
    from_a = swap_first(send_a)

    q2, f2, send_a, slope_q = call(
        adjoint_first_kernel,
        [info],
        [q3, q4, f3, from_a, from_b, stiff, wide, spots, p2],
        [own, own, seven, slopes],
        work(),
    )
    from_b = swap_second(f2)
    from_a = swap_first(send_a)
    image, q2_out = call(image_first_kernel, [], [q3, slope_q, div2, slope2, q2], [images, own])

    q1, f1, send_a, slope_q = call(
        adjoint_second_kernel,
        [info],
        [q2, q3, f2, from_a, from_b, stiff, wide, spots, p1],
        [own, own, four, slopes],
        work(),
    )
    from_b = swap_second(f1)
    from_a = swap_first(send_a)
    image, q1_out = call(
        image_second_kernel, [], [q2, slope_q, div1, slope1, image, q1], [images, own]
    )

    (image,) = call(
        image_kernel,
        [info],
        [q1, f1, from_a, from_b, div0, slope0, image],
        [images],
        [pltpu.VMEM((CX + 8, ROWS, CZ), F32)],
    )
    arrived = lax.all_to_all(image.transpose(2, 0, 1, 3), "shot", 0, 0, tiled=True)
    tiles = jax.ShapeDtypeStruct((TILES, CX, CZ), F32)
    grad_kappa, grad_buoy = call(gather_kernel, [], [picked, arrived], [tiles, tiles])
    return (grad_kappa, grad_buoy, q1_out[None], q2_out[None])


def solution(mesh):
    in_specs = (
        P("shot", "dom", None, None),
        P("shot", "dom", None, None),
        P("shot", "dom", None, None),
        P("shot", "dom", None, None),
        P(None, "dom", "shot"),
        P(None, "dom", "shot"),
        P(),
        P("shot"),
        P("shot", None),
        P("shot", None),
        P("shot", None, None),
    )
    out_specs = (
        P(None, "dom", "shot"),
        P(None, "dom", "shot"),
        P("shot", "dom", None, None),
        P("shot", "dom", None, None),
    )
    return jax.shard_map(shards, mesh=mesh, in_specs=in_specs, out_specs=out_specs, check_vma=False)
```

```python
import jax
import jax.numpy as jnp
from jax import lax
from jax.experimental import pallas as pl
from jax.experimental.pallas import tpu as pltpu
from jax.sharding import PartitionSpec as P

CX = 8
CY = 32
CZ = 128
TILES = 4
STEPS = 3
REC = 512
PAD = 8
ROWS = CY + 2 * PAD
WIDE = CX + 14

COEFFS = (1225.0 / 1024.0, -245.0 / 3072.0, 49.0 / 5120.0, -5.0 / 7168.0)
step_squared = 0.02

VMEM = pl.BlockSpec(memory_space=pltpu.VMEM)
SMEM = pl.BlockSpec(memory_space=pltpu.SMEM)
F32 = jnp.float32


def plane_field(count):
    return jax.ShapeDtypeStruct((count, CY, CZ), F32)


def lane_shift(plane, by, lane):
    if by == 0:
        return plane
    moved = pltpu.roll(plane, (-by) % CZ, 1)
    keep = lane < CZ - by if by > 0 else lane >= -by
    return jnp.where(keep, moved, 0.0)


def stencil(at):
    total = COEFFS[0] * (at(0) - at(-1))
    for k in range(2, 5):
        total = total + COEFFS[k - 1] * (at(k - 1) - at(-k))
    return total


def place(info, target, own, first, second, width):
    target[:, 0:PAD, :] = jnp.zeros((target.shape[0], PAD, CZ), F32)
    target[:, PAD + CY : ROWS, :] = jnp.zeros((target.shape[0], PAD, CZ), F32)
    inner = slice(PAD, PAD + CY)
    target[width : width + CX, inner, :] = own
    odd = info[0] == 1

    @pl.when(odd)
    def _():
        target[0:width, inner, :] = first
        target[width + CX : 2 * width + CX, inner, :] = second[0:width]

    @pl.when(jnp.logical_not(odd))
    def _():
        target[0:width, inner, :] = second[second.shape[0] - width :]
        target[width + CX : 2 * width + CX, inner, :] = first


def for_partner(info, target, head, tail):
    odd = info[0] == 1

    @pl.when(odd)
    def _():
        target[...] = head()

    @pl.when(jnp.logical_not(odd))
    def _():
        target[...] = tail()


def hand_over(info, send_a, field):
    width = send_a.shape[0]
    for_partner(info, send_a, lambda: field[0:width], lambda: field[CX - width : CX])


def slope_x(field, at):
    return stencil(lambda s: field[at + s, PAD : PAD + CY, :])


def slope_y(field, at):
    return stencil(lambda s: field[at, PAD + s : PAD + CY + s, :])


def slope_z(plane, lane):
    return stencil(lambda s: lane_shift(plane, s, lane))


def operate(field, width, buoy, gx, gy, acc, slopes):
    lane = lax.broadcasted_iota(jnp.int32, (CY, CZ), 1)
    gy[:, 0:PAD, :] = jnp.zeros((CX, PAD, CZ), F32)
    gy[:, PAD + CY : ROWS, :] = jnp.zeros((CX, PAD, CZ), F32)
    for cell in range(-3, CX + 4):
        sx = slope_x(field, cell + width)
        gx[cell + 3] = buoy[cell + 4] * sx
        if 0 <= cell < CX:
            weight = buoy[cell + 4]
            plane = field[cell + width, PAD : PAD + CY, :]
            sy = slope_y(field, cell + width)
            sz = slope_z(plane, lane)
            gy[cell, PAD : PAD + CY, :] = weight * sy
            gz = weight * sz
            acc[cell] = stencil(lambda s: lane_shift(gz, s + 1, lane))
            slopes(cell, sx, sy, sz)
    for cell in range(CX):
        div = stencil(lambda s: gx[cell + 4 + s])
        div = div + stencil(lambda s: gy[cell, PAD + 1 + s : PAD + 1 + s + CY, :])
        yield cell, div + acc[cell]


def prepare_kernel(
    info, wave, cells, seen, now, before, last, after, out, base_p, base_q, now_out, last_out, source_out
):
    base_p[...] = 2.0 * now[...] - before[...]
    base_q[...] = 2.0 * last[...] - after[...]
    now_out[...] = now[...]
    last_out[...] = last[...]
    y = lax.broadcasted_iota(jnp.int32, (CY, CZ), 0)
    z = lax.broadcasted_iota(jnp.int32, (CY, CZ), 1)
    hit = (y == info[2]) & (z == info[3])
    for n in range(STEPS):
        source_out[n] = jnp.where(hit, wave[n], 0.0)

    index = cells[...] - info[4]
    row = lax.shift_right_arithmetic(index, 7)
    z = lax.bitwise_and(index, 127)
    rows = lax.broadcasted_iota(jnp.int32, (CX * CY, REC), 0)
    pick = jnp.where(rows == row, 1.0, 0.0).astype(jnp.bfloat16)
    lanes = lax.broadcasted_iota(jnp.int32, (CZ, REC), 0)
    here = lanes == z

    def spread(values):
        right = jnp.where(here, values, 0.0).astype(jnp.bfloat16)
        return lax.dot_general(
            pick, right, (((1,), (1,)), ((), ())), preferred_element_type=F32
        )

    out[0] = spread(jnp.ones((1, REC), F32)).reshape(CX, CY, CZ)
    for n in range(STEPS):
        rest = seen[n : n + 1, :]
        total = None
        for _ in range(3):
            part = rest.astype(jnp.bfloat16).astype(F32)
            rest = rest - part
            total = spread(part) if total is None else total + spread(part)
        out[n + 1] = total.reshape(CX, CY, CZ)


def model_kernel(info, stiff, buoy, last, send_a, send_b, scaled):
    scaled[...] = stiff[...] * last[...]
    send_b[4:5] = buoy[0:1]
    for_partner(info, send_a, lambda: buoy[0:4], lambda: buoy[4:8])
    for_partner(info, send_b.at[0:4], lambda: buoy[4:8], lambda: buoy[0:4])


def forward(info, source, base, stiff, field, buoy, gx, gy, acc, div_out, slope_out, store):
    def keep(cell, sx, sy, sz):
        slope_out[0, cell] = sx
        slope_out[1, cell] = sy
        slope_out[2, cell] = sz

    for cell, div in operate(field, 7, buoy, gx, gy, acc, keep):
        div_out[cell] = div
        value = base(cell) + step_squared * stiff[cell] * div
        store(cell, value + jnp.where(info[1] == cell, source, 0.0))


def widen_buoy(info, buoy, first, second, target):
    target[4 : 4 + CX] = buoy[...]
    odd = info[0] == 1

    @pl.when(odd)
    def _():
        target[0:4] = first[0:4]
        target[4 + CX : 8 + CX] = second[0:4]

    @pl.when(jnp.logical_not(odd))
    def _():
        target[0:4] = second[0:4]
        target[4 + CX : 8 + CX] = first[0:4]


def first_kernel(
    info, now, now_a, now_b, base, source, stiff, buoy, edge_a, edge_b, scaled,
    p_out, send_a, near, far, div_out, slope_out, buoy_out,
    field, gx, gy, acc,
):
    widen_buoy(info, buoy, edge_a, edge_b, buoy_out)
    place(info, field, now[...], now_a[...], now_b[...], 7)

    def store(cell, value):
        p_out[cell] = value

    forward(
        info, source[0], lambda cell: base[cell],
        stiff, field, buoy_out, gx, gy, acc, div_out, slope_out, store,
    )
    hand_over(info, send_a, p_out)
    hand_over(info, near, scaled)
    far[...] = scaled[...]


def adjoint_part_kernel(
    info, base, scaled, near, far, buoy,
    q_out,
    field, gx, gy, acc,
):
    place(info, field, scaled[...], near[...], far[...], 7)
    for cell, div in operate(field, 7, buoy, gx, gy, acc, lambda *_: None):
        q_out[cell] = base[cell] + step_squared * div


def second_kernel(
    info, now, now_a, now_b, before, source, stiff, buoy,
    p_out, send_a, div_out, slope_out,
    field, gx, gy, acc,
):
    place(info, field, now[...], now_a[...], now_b[...], 7)

    def store(cell, value):
        p_out[cell] = value

    forward(
        info, source[1], lambda cell: 2.0 * now[cell] - before[cell],
        stiff, field, buoy, gx, gy, acc, div_out, slope_out, store,
    )
    hand_over(info, send_a, p_out)


def third_kernel(
    info, now, now_a, now_b, before, source, stiff, buoy, q_part, spots,
    q_out, scaled, send_a, div_out, slope_out,
    field, gx, gy, acc,
):
    place(info, field, now[...], now_a[...], now_b[...], 7)

    def store(cell, value):
        q = q_part[cell] + (spots[0, cell] * value - spots[3, cell])
        q_out[cell] = q
        scaled[cell] = stiff[cell] * q

    forward(
        info, source[2], lambda cell: 2.0 * now[cell] - before[cell],
        stiff, field, buoy, gx, gy, acc, div_out, slope_out, store,
    )
    hand_over(info, send_a, scaled)


def adjoint_kernel(
    n, info, q_now, q_after, scaled, scaled_a, scaled_b, stiff, buoy, spots, p_then,
    q_out, scaled_out, send_a, slope_out,
    field, gx, gy, acc,
):
    place(info, field, scaled[...], scaled_a[...], scaled_b[...], 7)

    def keep(cell, sx, sy, sz):
        slope_out[0, cell] = sx
        slope_out[1, cell] = sy
        slope_out[2, cell] = sz

    for cell, total in operate(field, 7, buoy, gx, gy, acc, keep):
        q = 2.0 * q_now[cell] - q_after[cell] + step_squared * total
        q = q + (spots[0, cell] * p_then[cell] - spots[n + 1, cell])
        q_out[cell] = q
        scaled_out[cell] = stiff[cell] * q
    hand_over(info, send_a, scaled_out)


def adjoint_first_kernel(*refs):
    adjoint_kernel(1, *refs)


def adjoint_second_kernel(*refs):
    adjoint_kernel(0, *refs)


def image_first_kernel(q_now, slope_q, div, slope_p, q_new, out, q_out):
    q_out[...] = q_new[...]
    for cell in range(CX):
        out[0, cell] = q_now[cell] * div[cell]
        rho = slope_p[0, cell] * slope_q[0, cell] + slope_p[1, cell] * slope_q[1, cell]
        out[1, cell] = rho + slope_p[2, cell] * slope_q[2, cell]


def image_second_kernel(
    q_now, slope_q, div, slope_p, images, q_new, out, q_out
):
    q_out[...] = q_new[...]
    for cell in range(CX):
        out[0, cell] = images[0, cell] + q_now[cell] * div[cell]
        rho = slope_p[0, cell] * slope_q[0, cell] + slope_p[1, cell] * slope_q[1, cell]
        out[1, cell] = images[1, cell] + (rho + slope_p[2, cell] * slope_q[2, cell])


def image_kernel(info, q_now, scaled, scaled_a, scaled_b, div, slope, images, out, field):
    lane = lax.broadcasted_iota(jnp.int32, (CY, CZ), 1)
    place(info, field, scaled[...], scaled_a[...], scaled_b[...], 4)
    for cell in range(CX):
        plane = field[cell + 4, PAD : PAD + CY, :]
        rho = images[1, cell] + slope[0, cell] * slope_x(field, cell + 4)
        rho = rho + slope[1, cell] * slope_y(field, cell + 4)
        rho = rho + slope[2, cell] * slope_z(plane, lane)
        out[0, cell] = step_squared * (images[0, cell] + q_now[cell] * div[cell])
        out[1, cell] = -step_squared * rho


def gather_kernel(picked, arrived, out_kappa, out_buoy):
    for t in range(TILES):
        kappa = jnp.zeros((CX, CZ), F32)
        rho = jnp.zeros((CX, CZ), F32)
        for s in range(arrived.shape[0]):
            here = picked[t, s : s + 1, :] > 0.0
            kappa = kappa + jnp.where(here, arrived[s, 0], 0.0)
            rho = rho + jnp.where(here, arrived[s, 1], 0.0)
        out_kappa[t] = kappa
        out_buoy[t] = rho


def work():
    return [
        pltpu.VMEM((WIDE, ROWS, CZ), F32),
        pltpu.VMEM((CX + 7, CY, CZ), F32),
        pltpu.VMEM((CX, ROWS, CZ), F32),
        pltpu.VMEM((CX, CY, CZ), F32),
    ]


def call(kernel, scalars, arrays, outs, scratch=(), flops=2_000_000):
    moved = sum(4 * a.size for a in arrays) + sum(4 * o.size for o in outs)
    return pl.pallas_call(
        kernel,
        out_shape=outs,
        in_specs=[SMEM] * len(scalars) + [VMEM] * len(arrays),
        out_specs=[VMEM] * len(outs),
        scratch_shapes=list(scratch),
        compiler_params=pltpu.CompilerParams(vmem_limit_bytes=32 * 1024 * 1024),
        cost_estimate=pl.CostEstimate(flops=flops, bytes_accessed=moved, transcendentals=0),
    )(*scalars, *arrays)


def swap_first(planes):
    count = lax.axis_size("dom")
    return lax.ppermute(planes, "dom", [(i ^ 1, i) for i in range(count)])


def swap_second(planes):
    pairs = []
    for i in range(1, lax.axis_size("dom") - 1, 2):
        pairs += [(i, i + 1), (i + 1, i)]
    return lax.ppermute(planes, "dom", pairs)


def shards(
    pressure_now,
    pressure_prev,
    adjoint_last,
    adjoint_after,
    kappa_model,
    buoy_model,
    aperture,
    source_cell,
    source_wave,
    receiver_cell,
    observed,
):
    dom = lax.axis_index("dom")
    odd = lax.rem(dom, 2)
    offset = dom * (CX * CY * CZ)
    source = source_cell[0]
    info = jnp.stack(
        [odd, source // (CY * CZ) - dom * CX, (source // CZ) % CY, source % CZ, offset]
    ).astype(jnp.int32)

    column = lax.dynamic_index_in_dim(aperture, dom, 1, keepdims=False)
    stacked = jnp.stack((kappa_model, buoy_model), axis=1)
    picks = column[:, None, None, None]
    chosen = stacked[0][None]
    for t in range(1, TILES):
        chosen = jnp.where(picks == t, stacked[t][None], chosen)
    block = lax.all_to_all(chosen, "shot", 0, 0, tiled=True)

    p0, p_prev = pressure_now[0], pressure_prev[0]
    q4, q5 = adjoint_last[0], adjoint_after[0]
    p0_b = swap_second(p0)
    p0_a = swap_first(jnp.where(odd == 1, p0[0:7], p0[1:8]))
    own, seven, four = plane_field(CX), plane_field(7), plane_field(4)
    spots, base_p, base_q, p0, q4, source_planes = call(
        prepare_kernel,
        [info, source_wave[0]],
        [receiver_cell, observed[0], p0, p_prev, q4, q5],
        [jax.ShapeDtypeStruct((STEPS + 1, CX, CY, CZ), F32), own, own, own, own, plane_field(STEPS)],
        flops=400_000_000,
    )
    ids = jnp.arange(TILES, dtype=jnp.int32)[:, None, None]
    picked = jnp.broadcast_to(
        (column[None, :, None] == ids).astype(F32), (TILES, column.shape[0], CZ)
    )
    block, p0_a, p0_b, spots, base_p, base_q, p0, q4, source_planes, picked = lax.optimization_barrier(
        (block, p0_a, p0_b, spots, base_p, base_q, p0, q4, source_planes, picked)
    )

    stiff = block[:, 0].transpose(1, 0, 2)
    buoy = block[:, 1].transpose(1, 0, 2)
    slopes = jax.ShapeDtypeStruct((3, CX, CY, CZ), F32)
    images = jax.ShapeDtypeStruct((2, CX, CY, CZ), F32)

    send_a, send_b, f4 = call(
        model_kernel, [info], [stiff, buoy, q4], [four, plane_field(5), own]
    )
    edge_b = swap_second(send_b)
    edge_a = swap_first(send_a)

    p1, send_a, near, far, div0, slope0, wide = call(
        first_kernel,
        [info],
        [p0, p0_a, p0_b, base_p, source_planes, stiff, buoy, edge_a, edge_b, f4],
        [own, seven, seven, own, own, slopes, plane_field(CX + 8)],
        work(),
    )
    from_b = swap_second(p1)
    from_a = swap_first(send_a)
    far = swap_second(far)
    near = swap_first(near)
    (q_part,) = call(adjoint_part_kernel, [info], [base_q, f4, near, far, wide], [own], work())

    p2, send_a, div1, slope1 = call(
        second_kernel,
        [info],
        [p1, from_a, from_b, p0, source_planes, stiff, wide],
        [own, seven, own, slopes],
        work(),
    )
    from_b = swap_second(p2)
    from_a = swap_first(send_a)

    q3, f3, send_a, div2, slope2 = call(
        third_kernel,
        [info],
        [p2, from_a, from_b, p1, source_planes, stiff, wide, q_part, spots],
        [own, own, seven, own, slopes],
        work(),
    )
    from_b = swap_second(f3)
    from_a = swap_first(send_a)

    q2, f2, send_a, slope_q = call(
        adjoint_first_kernel,
        [info],
        [q3, q4, f3, from_a, from_b, stiff, wide, spots, p2],
        [own, own, seven, slopes],
        work(),
    )
    from_b = swap_second(f2)
    from_a = swap_first(send_a)
    image, q2_out = call(image_first_kernel, [], [q3, slope_q, div2, slope2, q2], [images, own])

    q1, f1, send_a, slope_q = call(
        adjoint_second_kernel,
        [info],
        [q2, q3, f2, from_a, from_b, stiff, wide, spots, p1],
        [own, own, four, slopes],
        work(),
    )
    from_b = swap_second(f1)
    from_a = swap_first(send_a)
    image, q1_out = call(
        image_second_kernel, [], [q2, slope_q, div1, slope1, image, q1], [images, own]
    )

    (image,) = call(
        image_kernel,
        [info],
        [q1, f1, from_a, from_b, div0, slope0, image],
        [images],
        [pltpu.VMEM((CX + 8, ROWS, CZ), F32)],
    )
    arrived = lax.all_to_all(image.transpose(2, 0, 1, 3), "shot", 0, 0, tiled=True)
    tiles = jax.ShapeDtypeStruct((TILES, CX, CZ), F32)
    grad_kappa, grad_buoy = call(gather_kernel, [], [picked, arrived], [tiles, tiles])
    return (grad_kappa, grad_buoy, q1_out[None], q2_out[None])


def solution(mesh):
    in_specs = (
        P("shot", "dom", None, None),
        P("shot", "dom", None, None),
        P("shot", "dom", None, None),
        P("shot", "dom", None, None),
        P(None, "dom", "shot"),
        P(None, "dom", "shot"),
        P(),
        P("shot"),
        P("shot", None),
        P("shot", None),
        P("shot", None, None),
    )
    out_specs = (
        P(None, "dom", "shot"),
        P(None, "dom", "shot"),
        P("shot", "dom", None, None),
        P("shot", "dom", None, None),
    )
    return jax.shard_map(shards, mesh=mesh, in_specs=in_specs, out_specs=out_specs, check_vma=False)
```

```python
import jax
import jax.numpy as jnp
from jax import lax
from jax.experimental import pallas as pl
from jax.experimental.pallas import tpu as pltpu
from jax.sharding import PartitionSpec as P

CX = 8
CY = 32
CZ = 128
TILES = 4
STEPS = 3
REC = 512
PAD = 8
ROWS = CY + 2 * PAD
WIDE = CX + 14

COEFFS = (1225.0 / 1024.0, -245.0 / 3072.0, 49.0 / 5120.0, -5.0 / 7168.0)
step_squared = 0.02

VMEM = pl.BlockSpec(memory_space=pltpu.VMEM)
SMEM = pl.BlockSpec(memory_space=pltpu.SMEM)
F32 = jnp.float32


def plane_field(count):
    return jax.ShapeDtypeStruct((count, CY, CZ), F32)


def lane_shift(plane, by, lane):
    if by == 0:
        return plane
    moved = pltpu.roll(plane, (-by) % CZ, 1)
    keep = lane < CZ - by if by > 0 else lane >= -by
    return jnp.where(keep, moved, 0.0)


def stencil(at):
    total = COEFFS[0] * (at(0) - at(-1))
    for k in range(2, 5):
        total = total + COEFFS[k - 1] * (at(k - 1) - at(-k))
    return total


def place(info, target, own, first, second, width):
    target[:, 0:PAD, :] = jnp.zeros((target.shape[0], PAD, CZ), F32)
    target[:, PAD + CY : ROWS, :] = jnp.zeros((target.shape[0], PAD, CZ), F32)
    inner = slice(PAD, PAD + CY)
    target[width : width + CX, inner, :] = own
    odd = info[0] == 1

    @pl.when(odd)
    def _():
        target[0:width, inner, :] = first
        target[width + CX : 2 * width + CX, inner, :] = second[0:width]

    @pl.when(jnp.logical_not(odd))
    def _():
        target[0:width, inner, :] = second[second.shape[0] - width :]
        target[width + CX : 2 * width + CX, inner, :] = first


def for_partner(info, target, head, tail):
    odd = info[0] == 1

    @pl.when(odd)
    def _():
        target[...] = head()

    @pl.when(jnp.logical_not(odd))
    def _():
        target[...] = tail()


def hand_over(info, send_a, field):
    width = send_a.shape[0]
    for_partner(info, send_a, lambda: field[0:width], lambda: field[CX - width : CX])


def slope_x(field, at):
    return stencil(lambda s: field[at + s, PAD : PAD + CY, :])


def slope_y(field, at):
    return stencil(lambda s: field[at, PAD + s : PAD + CY + s, :])


def slope_z(plane, lane):
    return stencil(lambda s: lane_shift(plane, s, lane))


def operate(field, width, buoy, gx, gy, acc, slopes):
    lane = lax.broadcasted_iota(jnp.int32, (CY, CZ), 1)
    gy[:, 0:PAD, :] = jnp.zeros((CX, PAD, CZ), F32)
    gy[:, PAD + CY : ROWS, :] = jnp.zeros((CX, PAD, CZ), F32)
    for cell in range(-3, CX + 4):
        sx = slope_x(field, cell + width)
        gx[cell + 3] = buoy[cell + 4] * sx
        if 0 <= cell < CX:
            weight = buoy[cell + 4]
            plane = field[cell + width, PAD : PAD + CY, :]
            sy = slope_y(field, cell + width)
            sz = slope_z(plane, lane)
            gy[cell, PAD : PAD + CY, :] = weight * sy
            gz = weight * sz
            acc[cell] = stencil(lambda s: lane_shift(gz, s + 1, lane))
            slopes(cell, sx, sy, sz)
    for cell in range(CX):
        div = stencil(lambda s: gx[cell + 4 + s])
        div = div + stencil(lambda s: gy[cell, PAD + 1 + s : PAD + 1 + s + CY, :])
        yield cell, div + acc[cell]


def prepare_kernel(
    info, wave, cells, seen, now, before, last, after, out, base_p, base_q, now_out, last_out, source_out
):
    base_p[...] = 2.0 * now[...] - before[...]
    base_q[...] = 2.0 * last[...] - after[...]
    now_out[...] = now[...]
    last_out[...] = last[...]
    y = lax.broadcasted_iota(jnp.int32, (CY, CZ), 0)
    z = lax.broadcasted_iota(jnp.int32, (CY, CZ), 1)
    hit = (y == info[2]) & (z == info[3])
    for n in range(STEPS):
        source_out[n] = jnp.where(hit, wave[n], 0.0)

    index = cells[...] - info[4]
    row = lax.shift_right_arithmetic(index, 7)
    z = lax.bitwise_and(index, 127)
    rows = lax.broadcasted_iota(jnp.int32, (CX * CY, REC), 0)
    pick = jnp.where(rows == row, 1.0, 0.0).astype(jnp.bfloat16)
    lanes = lax.broadcasted_iota(jnp.int32, (CZ, REC), 0)
    here = lanes == z

    def spread(values):
        right = jnp.where(here, values, 0.0).astype(jnp.bfloat16)
        return lax.dot_general(
            pick, right, (((1,), (1,)), ((), ())), preferred_element_type=F32
        )

    out[0] = spread(jnp.ones((1, REC), F32)).reshape(CX, CY, CZ)
    for n in range(STEPS):
        rest = seen[n : n + 1, :]
        total = None
        for _ in range(3):
            part = rest.astype(jnp.bfloat16).astype(F32)
            rest = rest - part
            total = spread(part) if total is None else total + spread(part)
        out[n + 1] = total.reshape(CX, CY, CZ)


def model_kernel(info, stiff, buoy, last, now, send_a, send_b, scaled):
    scaled[...] = stiff[...] * last[...]
    send_b[4:12] = now[...]
    for_partner(
        info,
        send_a,
        lambda: jnp.concatenate([buoy[0:4], now[0:7]], axis=0),
        lambda: jnp.concatenate([buoy[4:8], now[1:8]], axis=0),
    )
    for_partner(info, send_b.at[0:4], lambda: buoy[4:8], lambda: buoy[0:4])


def forward(info, source, base, stiff, field, buoy, gx, gy, acc, div_out, slope_out, store):
    def keep(cell, sx, sy, sz):
        slope_out[0, cell] = sx
        slope_out[1, cell] = sy
        slope_out[2, cell] = sz

    for cell, div in operate(field, 7, buoy, gx, gy, acc, keep):
        div_out[cell] = div
        value = base(cell) + step_squared * stiff[cell] * div
        store(cell, value + jnp.where(info[1] == cell, source, 0.0))


def widen_buoy(info, buoy, first, second, target):
    target[4 : 4 + CX] = buoy[...]
    odd = info[0] == 1

    @pl.when(odd)
    def _():
        target[0:4] = first[0:4]
        target[4 + CX : 8 + CX] = second[0:4]

    @pl.when(jnp.logical_not(odd))
    def _():
        target[0:4] = second[0:4]
        target[4 + CX : 8 + CX] = first[0:4]


def first_kernel(
    info, now, base, source, stiff, buoy, edge_a, edge_b, scaled,
    p_out, send_a, near, far, div_out, slope_out, buoy_out,
    field, gx, gy, acc,
):
    widen_buoy(info, buoy, edge_a, edge_b, buoy_out)
    place(info, field, now[...], edge_a[4:11], edge_b[4:12], 7)

    def store(cell, value):
        p_out[cell] = value

    forward(
        info, source[0], lambda cell: base[cell],
        stiff, field, buoy_out, gx, gy, acc, div_out, slope_out, store,
    )
    hand_over(info, send_a, p_out)
    hand_over(info, near, scaled)
    far[...] = scaled[...]


def adjoint_part_kernel(
    info, base, scaled, near, far, buoy,
    q_out,
    field, gx, gy, acc,
):
    place(info, field, scaled[...], near[...], far[...], 7)
    for cell, div in operate(field, 7, buoy, gx, gy, acc, lambda *_: None):
        q_out[cell] = base[cell] + step_squared * div


def second_kernel(
    info, now, now_a, now_b, before, source, stiff, buoy,
    p_out, send_a, div_out, slope_out,
    field, gx, gy, acc,
):
    place(info, field, now[...], now_a[...], now_b[...], 7)

    def store(cell, value):
        p_out[cell] = value

    forward(
        info, source[1], lambda cell: 2.0 * now[cell] - before[cell],
        stiff, field, buoy, gx, gy, acc, div_out, slope_out, store,
    )
    hand_over(info, send_a, p_out)


def third_kernel(
    info, now, now_a, now_b, before, source, stiff, buoy, q_part, spots,
    q_out, scaled, send_a, div_out, slope_out,
    field, gx, gy, acc,
):
    place(info, field, now[...], now_a[...], now_b[...], 7)

    def store(cell, value):
        q = q_part[cell] + (spots[0, cell] * value - spots[3, cell])
        q_out[cell] = q
        scaled[cell] = stiff[cell] * q

    forward(
        info, source[2], lambda cell: 2.0 * now[cell] - before[cell],
        stiff, field, buoy, gx, gy, acc, div_out, slope_out, store,
    )
    hand_over(info, send_a, scaled)


def adjoint_kernel(
    n, info, q_now, q_after, scaled, scaled_a, scaled_b, stiff, buoy, spots, p_then,
    q_out, scaled_out, send_a, slope_out,
    field, gx, gy, acc,
):
    place(info, field, scaled[...], scaled_a[...], scaled_b[...], 7)

    def keep(cell, sx, sy, sz):
        slope_out[0, cell] = sx
        slope_out[1, cell] = sy
        slope_out[2, cell] = sz

    for cell, total in operate(field, 7, buoy, gx, gy, acc, keep):
        q = 2.0 * q_now[cell] - q_after[cell] + step_squared * total
        q = q + (spots[0, cell] * p_then[cell] - spots[n + 1, cell])
        q_out[cell] = q
        scaled_out[cell] = stiff[cell] * q
    hand_over(info, send_a, scaled_out)


def adjoint_first_kernel(*refs):
    adjoint_kernel(1, *refs)


def adjoint_second_kernel(*refs):
    adjoint_kernel(0, *refs)


def image_first_kernel(q_now, slope_q, div, slope_p, q_new, out, q_out):
    q_out[...] = q_new[...]
    for cell in range(CX):
        out[0, cell] = q_now[cell] * div[cell]
        rho = slope_p[0, cell] * slope_q[0, cell] + slope_p[1, cell] * slope_q[1, cell]
        out[1, cell] = rho + slope_p[2, cell] * slope_q[2, cell]


def image_second_kernel(
    q_now, slope_q, div, slope_p, images, q_new, out, q_out
):
    q_out[...] = q_new[...]
    for cell in range(CX):
        out[0, cell] = images[0, cell] + q_now[cell] * div[cell]
        rho = slope_p[0, cell] * slope_q[0, cell] + slope_p[1, cell] * slope_q[1, cell]
        out[1, cell] = images[1, cell] + (rho + slope_p[2, cell] * slope_q[2, cell])


def image_kernel(info, q_now, scaled, scaled_a, scaled_b, div, slope, images, out, field):
    lane = lax.broadcasted_iota(jnp.int32, (CY, CZ), 1)
    place(info, field, scaled[...], scaled_a[...], scaled_b[...], 4)
    for cell in range(CX):
        plane = field[cell + 4, PAD : PAD + CY, :]
        rho = images[1, cell] + slope[0, cell] * slope_x(field, cell + 4)
        rho = rho + slope[1, cell] * slope_y(field, cell + 4)
        rho = rho + slope[2, cell] * slope_z(plane, lane)
        out[0, cell] = step_squared * (images[0, cell] + q_now[cell] * div[cell])
        out[1, cell] = -step_squared * rho


def gather_kernel(picked, arrived, out_kappa, out_buoy):
    for t in range(TILES):
        kappa = jnp.zeros((CX, CZ), F32)
        rho = jnp.zeros((CX, CZ), F32)
        for s in range(arrived.shape[0]):
            here = picked[t, s : s + 1, :] > 0.0
            kappa = kappa + jnp.where(here, arrived[s, 0], 0.0)
            rho = rho + jnp.where(here, arrived[s, 1], 0.0)
        out_kappa[t] = kappa
        out_buoy[t] = rho


def work():
    return [
        pltpu.VMEM((WIDE, ROWS, CZ), F32),
        pltpu.VMEM((CX + 7, CY, CZ), F32),
        pltpu.VMEM((CX, ROWS, CZ), F32),
        pltpu.VMEM((CX, CY, CZ), F32),
    ]


def call(kernel, scalars, arrays, outs, scratch=(), flops=2_000_000):
    moved = sum(4 * a.size for a in arrays) + sum(4 * o.size for o in outs)
    return pl.pallas_call(
        kernel,
        out_shape=outs,
        in_specs=[SMEM] * len(scalars) + [VMEM] * len(arrays),
        out_specs=[VMEM] * len(outs),
        scratch_shapes=list(scratch),
        compiler_params=pltpu.CompilerParams(vmem_limit_bytes=32 * 1024 * 1024),
        cost_estimate=pl.CostEstimate(flops=flops, bytes_accessed=moved, transcendentals=0),
    )(*scalars, *arrays)


def swap_first(planes):
    count = lax.axis_size("dom")
    return lax.ppermute(planes, "dom", [(i ^ 1, i) for i in range(count)])


def swap_second(planes):
    pairs = []
    for i in range(1, lax.axis_size("dom") - 1, 2):
        pairs += [(i, i + 1), (i + 1, i)]
    return lax.ppermute(planes, "dom", pairs)


def shards(
    pressure_now,
    pressure_prev,
    adjoint_last,
    adjoint_after,
    kappa_model,
    buoy_model,
    aperture,
    source_cell,
    source_wave,
    receiver_cell,
    observed,
):
    dom = lax.axis_index("dom")
    odd = lax.rem(dom, 2)
    offset = dom * (CX * CY * CZ)
    source = source_cell[0]
    info = jnp.stack(
        [odd, source // (CY * CZ) - dom * CX, (source // CZ) % CY, source % CZ, offset]
    ).astype(jnp.int32)

    column = lax.dynamic_index_in_dim(aperture, dom, 1, keepdims=False)
    stacked = jnp.stack((kappa_model, buoy_model), axis=1)
    picks = column[:, None, None, None]
    chosen = stacked[0][None]
    for t in range(1, TILES):
        chosen = jnp.where(picks == t, stacked[t][None], chosen)
    block = lax.all_to_all(chosen, "shot", 0, 0, tiled=True)

    p0, p_prev = pressure_now[0], pressure_prev[0]
    q4, q5 = adjoint_last[0], adjoint_after[0]
    own, seven, four = plane_field(CX), plane_field(7), plane_field(4)
    spots, base_p, base_q, p0, q4, source_planes = call(
        prepare_kernel,
        [info, source_wave[0]],
        [receiver_cell, observed[0], p0, p_prev, q4, q5],
        [jax.ShapeDtypeStruct((STEPS + 1, CX, CY, CZ), F32), own, own, own, own, plane_field(STEPS)],
        flops=400_000_000,
    )
    ids = jnp.arange(TILES, dtype=jnp.int32)[:, None, None]
    picked = jnp.broadcast_to(
        (column[None, :, None] == ids).astype(F32), (TILES, column.shape[0], CZ)
    )
    block, spots, base_p, base_q, p0, q4, source_planes, picked = lax.optimization_barrier(
        (block, spots, base_p, base_q, p0, q4, source_planes, picked)
    )

    stiff = block[:, 0].transpose(1, 0, 2)
    buoy = block[:, 1].transpose(1, 0, 2)
    slopes = jax.ShapeDtypeStruct((3, CX, CY, CZ), F32)
    images = jax.ShapeDtypeStruct((2, CX, CY, CZ), F32)

    send_a, send_b, f4 = call(
        model_kernel, [info], [stiff, buoy, q4, p0], [plane_field(11), plane_field(12), own]
    )
    edge_b = swap_second(send_b)
    edge_a = swap_first(send_a)

    p1, send_a, near, far, div0, slope0, wide = call(
        first_kernel,
        [info],
        [p0, base_p, source_planes, stiff, buoy, edge_a, edge_b, f4],
        [own, seven, seven, own, own, slopes, plane_field(CX + 8)],
        work(),
    )
    from_b = swap_second(p1)
    from_a = swap_first(send_a)
    far = swap_second(far)
    near = swap_first(near)
    (q_part,) = call(adjoint_part_kernel, [info], [base_q, f4, near, far, wide], [own], work())

    p2, send_a, div1, slope1 = call(
        second_kernel,
        [info],
        [p1, from_a, from_b, p0, source_planes, stiff, wide],
        [own, seven, own, slopes],
        work(),
    )
    from_b = swap_second(p2)
    from_a = swap_first(send_a)

    q3, f3, send_a, div2, slope2 = call(
        third_kernel,
        [info],
        [p2, from_a, from_b, p1, source_planes, stiff, wide, q_part, spots],
        [own, own, seven, own, slopes],
        work(),
    )
    from_b = swap_second(f3)
    from_a = swap_first(send_a)

    q2, f2, send_a, slope_q = call(
        adjoint_first_kernel,
        [info],
        [q3, q4, f3, from_a, from_b, stiff, wide, spots, p2],
        [own, own, seven, slopes],
        work(),
    )
    from_b = swap_second(f2)
    from_a = swap_first(send_a)
    image, q2_out = call(image_first_kernel, [], [q3, slope_q, div2, slope2, q2], [images, own])

    q1, f1, send_a, slope_q = call(
        adjoint_second_kernel,
        [info],
        [q2, q3, f2, from_a, from_b, stiff, wide, spots, p1],
        [own, own, four, slopes],
        work(),
    )
    from_b = swap_second(f1)
    from_a = swap_first(send_a)
    image, q1_out = call(
        image_second_kernel, [], [q2, slope_q, div1, slope1, image, q1], [images, own]
    )

    (image,) = call(
        image_kernel,
        [info],
        [q1, f1, from_a, from_b, div0, slope0, image],
        [images],
        [pltpu.VMEM((CX + 8, ROWS, CZ), F32)],
    )
    arrived = lax.all_to_all(image.transpose(2, 0, 1, 3), "shot", 0, 0, tiled=True)
    tiles = jax.ShapeDtypeStruct((TILES, CX, CZ), F32)
    grad_kappa, grad_buoy = call(gather_kernel, [], [picked, arrived], [tiles, tiles])
    return (grad_kappa, grad_buoy, q1_out[None], q2_out[None])


def solution(mesh):
    in_specs = (
        P("shot", "dom", None, None),
        P("shot", "dom", None, None),
        P("shot", "dom", None, None),
        P("shot", "dom", None, None),
        P(None, "dom", "shot"),
        P(None, "dom", "shot"),
        P(),
        P("shot"),
        P("shot", None),
        P("shot", None),
        P("shot", None, None),
    )
    out_specs = (
        P(None, "dom", "shot"),
        P(None, "dom", "shot"),
        P("shot", "dom", None, None),
        P("shot", "dom", None, None),
    )
    return jax.shard_map(shards, mesh=mesh, in_specs=in_specs, out_specs=out_specs, check_vma=False)
```

```python
import jax
import jax.numpy as jnp
from jax import lax
from jax.experimental import pallas as pl
from jax.experimental.pallas import tpu as pltpu
from jax.sharding import PartitionSpec as P

CX = 8
CY = 32
CZ = 128
TILES = 4
STEPS = 3
REC = 512
PAD = 8
ROWS = CY + 2 * PAD
WIDE = CX + 14

COEFFS = (1225.0 / 1024.0, -245.0 / 3072.0, 49.0 / 5120.0, -5.0 / 7168.0)
step_squared = 0.02

VMEM = pl.BlockSpec(memory_space=pltpu.VMEM)
SMEM = pl.BlockSpec(memory_space=pltpu.SMEM)
F32 = jnp.float32


def plane_field(count):
    return jax.ShapeDtypeStruct((count, CY, CZ), F32)


def far_rows(count):
    return jax.ShapeDtypeStruct((count * CY + 8, CZ), F32)


def rows_of(planes):
    return planes.reshape(planes.shape[0] * CY, CZ)


def planes_at(rows, start, count):
    return rows[start * CY : (start + count) * CY, :].reshape(count, CY, CZ)


def lane_shift(plane, by, lane):
    if by == 0:
        return plane
    moved = pltpu.roll(plane, (-by) % CZ, 1)
    keep = lane < CZ - by if by > 0 else lane >= -by
    return jnp.where(keep, moved, 0.0)


def stencil(at):
    total = COEFFS[0] * (at(0) - at(-1))
    for k in range(2, 5):
        total = total + COEFFS[k - 1] * (at(k - 1) - at(-k))
    return total


def place(info, target, own, first, second, width):
    target[:, 0:PAD, :] = jnp.zeros((target.shape[0], PAD, CZ), F32)
    target[:, PAD + CY : ROWS, :] = jnp.zeros((target.shape[0], PAD, CZ), F32)
    inner = slice(PAD, PAD + CY)
    target[width : width + CX, inner, :] = own
    odd = info[0] == 1

    @pl.when(odd)
    def _():
        target[0:width, inner, :] = first
        target[width + CX : 2 * width + CX, inner, :] = second

    @pl.when(jnp.logical_not(odd))
    def _():
        target[0:width, inner, :] = second
        target[width + CX : 2 * width + CX, inner, :] = first


def for_partner(info, target, head, tail):
    odd = info[0] == 1

    @pl.when(odd)
    def _():
        target[...] = head()

    @pl.when(jnp.logical_not(odd))
    def _():
        target[...] = tail()


def hand_over(info, send_a, send_b, field):
    width = send_a.shape[0]
    for_partner(info, send_a, lambda: field[0:width], lambda: field[CX - width : CX])
    for_partner(
        info,
        send_b.at[0 : width * CY],
        lambda: rows_of(field[CX - width : CX]),
        lambda: rows_of(field[0:width]),
    )
    send_b[width * CY :, :] = jnp.zeros((8, CZ), F32)


def slope_x(field, at):
    return stencil(lambda s: field[at + s, PAD : PAD + CY, :])


def slope_y(field, at):
    return stencil(lambda s: field[at, PAD + s : PAD + CY + s, :])


def slope_z(plane, lane):
    return stencil(lambda s: lane_shift(plane, s, lane))


def operate(field, width, buoy, gx, gy, acc, slopes):
    lane = lax.broadcasted_iota(jnp.int32, (CY, CZ), 1)
    gy[:, 0:PAD, :] = jnp.zeros((CX, PAD, CZ), F32)
    gy[:, PAD + CY : ROWS, :] = jnp.zeros((CX, PAD, CZ), F32)
    for cell in range(-3, CX + 4):
        sx = slope_x(field, cell + width)
        gx[cell + 3] = buoy[cell + 4] * sx
        if 0 <= cell < CX:
            weight = buoy[cell + 4]
            plane = field[cell + width, PAD : PAD + CY, :]
            sy = slope_y(field, cell + width)
            sz = slope_z(plane, lane)
            gy[cell, PAD : PAD + CY, :] = weight * sy
            gz = weight * sz
            acc[cell] = stencil(lambda s: lane_shift(gz, s + 1, lane))
            slopes(cell, sx, sy, sz)
    for cell in range(CX):
        div = stencil(lambda s: gx[cell + 4 + s])
        div = div + stencil(lambda s: gy[cell, PAD + 1 + s : PAD + 1 + s + CY, :])
        yield cell, div + acc[cell]


def prepare_kernel(
    info, wave, cells, seen, now, before, last, after, out, base_p, base_q, now_out, last_out, source_out
):
    base_p[...] = 2.0 * now[...] - before[...]
    base_q[...] = 2.0 * last[...] - after[...]
    now_out[...] = now[...]
    last_out[...] = last[...]
    y = lax.broadcasted_iota(jnp.int32, (CY, CZ), 0)
    z = lax.broadcasted_iota(jnp.int32, (CY, CZ), 1)
    hit = (y == info[2]) & (z == info[3])
    for n in range(STEPS):
        source_out[n] = jnp.where(hit, wave[n], 0.0)

    index = cells[...] - info[4]
    row = lax.shift_right_arithmetic(index, 7)
    z = lax.bitwise_and(index, 127)
    rows = lax.broadcasted_iota(jnp.int32, (CX * CY, REC), 0)
    pick = jnp.where(rows == row, 1.0, 0.0).astype(jnp.bfloat16)
    lanes = lax.broadcasted_iota(jnp.int32, (CZ, REC), 0)
    here = lanes == z

    def spread(values):
        right = jnp.where(here, values, 0.0).astype(jnp.bfloat16)
        return lax.dot_general(
            pick, right, (((1,), (1,)), ((), ())), preferred_element_type=F32
        )

    out[0] = spread(jnp.ones((1, REC), F32)).reshape(CX, CY, CZ)
    for n in range(STEPS):
        rest = seen[n : n + 1, :]
        total = None
        for _ in range(3):
            part = rest.astype(jnp.bfloat16).astype(F32)
            rest = rest - part
            total = spread(part) if total is None else total + spread(part)
        out[n + 1] = total.reshape(CX, CY, CZ)


def model_kernel(info, stiff, buoy, last, now, send_a, send_b, scaled):
    scaled[...] = stiff[...] * last[...]

    def head():
        return jnp.concatenate([buoy[0:4], now[0:7]], axis=0)

    def tail():
        return jnp.concatenate([buoy[4:8], now[1:8]], axis=0)

    for_partner(info, send_a, head, tail)
    for_partner(
        info, send_b.at[0 : 11 * CY], lambda: rows_of(tail()), lambda: rows_of(head())
    )
    send_b[11 * CY :, :] = jnp.zeros((8, CZ), F32)


def forward(info, source, base, stiff, field, buoy, gx, gy, acc, div_out, slope_out, store):
    def keep(cell, sx, sy, sz):
        slope_out[0, cell] = sx
        slope_out[1, cell] = sy
        slope_out[2, cell] = sz

    for cell, div in operate(field, 7, buoy, gx, gy, acc, keep):
        div_out[cell] = div
        value = base(cell) + step_squared * stiff[cell] * div
        store(cell, value + jnp.where(info[1] == cell, source, 0.0))


def widen_buoy(info, buoy, first, second, target):
    target[4 : 4 + CX] = buoy[...]
    odd = info[0] == 1

    @pl.when(odd)
    def _():
        target[0:4] = first[0:4]
        target[4 + CX : 8 + CX] = planes_at(second, 0, 4)

    @pl.when(jnp.logical_not(odd))
    def _():
        target[0:4] = planes_at(second, 0, 4)
        target[4 + CX : 8 + CX] = first[0:4]


def first_kernel(
    info, now, base, source, stiff, buoy, edge_a, edge_b, scaled,
    p_out, send_a, send_b, near, far, div_out, slope_out, buoy_out,
    field, gx, gy, acc,
):
    widen_buoy(info, buoy, edge_a, edge_b, buoy_out)
    place(info, field, now[...], edge_a[4:11], planes_at(edge_b, 4, 7), 7)

    def store(cell, value):
        p_out[cell] = value

    forward(
        info, source[0], lambda cell: base[cell],
        stiff, field, buoy_out, gx, gy, acc, div_out, slope_out, store,
    )
    hand_over(info, send_a, send_b, p_out)
    hand_over(info, near, far, scaled)


def adjoint_part_kernel(
    info, base, scaled, near, far, buoy,
    q_out,
    field, gx, gy, acc,
):
    place(info, field, scaled[...], near[...], planes_at(far, 0, 7), 7)
    for cell, div in operate(field, 7, buoy, gx, gy, acc, lambda *_: None):
        q_out[cell] = base[cell] + step_squared * div


def second_kernel(
    info, now, now_a, now_b, before, source, stiff, buoy,
    p_out, send_a, send_b, div_out, slope_out,
    field, gx, gy, acc,
):
    place(info, field, now[...], now_a[...], planes_at(now_b, 0, 7), 7)

    def store(cell, value):
        p_out[cell] = value

    forward(
        info, source[1], lambda cell: 2.0 * now[cell] - before[cell],
        stiff, field, buoy, gx, gy, acc, div_out, slope_out, store,
    )
    hand_over(info, send_a, send_b, p_out)


def third_kernel(
    info, now, now_a, now_b, before, source, stiff, buoy, q_part, spots,
    q_out, scaled, send_a, send_b, div_out, slope_out,
    field, gx, gy, acc,
):
    place(info, field, now[...], now_a[...], planes_at(now_b, 0, 7), 7)

    def store(cell, value):
        q = q_part[cell] + (spots[0, cell] * value - spots[3, cell])
        q_out[cell] = q
        scaled[cell] = stiff[cell] * q

    forward(
        info, source[2], lambda cell: 2.0 * now[cell] - before[cell],
        stiff, field, buoy, gx, gy, acc, div_out, slope_out, store,
    )
    hand_over(info, send_a, send_b, scaled)


def adjoint_kernel(
    n, info, q_now, q_after, scaled, scaled_a, scaled_b, stiff, buoy, spots, p_then,
    q_out, scaled_out, send_a, send_b, slope_out,
    field, gx, gy, acc,
):
    place(info, field, scaled[...], scaled_a[...], planes_at(scaled_b, 0, 7), 7)

    def keep(cell, sx, sy, sz):
        slope_out[0, cell] = sx
        slope_out[1, cell] = sy
        slope_out[2, cell] = sz

    for cell, total in operate(field, 7, buoy, gx, gy, acc, keep):
        q = 2.0 * q_now[cell] - q_after[cell] + step_squared * total
        q = q + (spots[0, cell] * p_then[cell] - spots[n + 1, cell])
        q_out[cell] = q
        scaled_out[cell] = stiff[cell] * q
    hand_over(info, send_a, send_b, scaled_out)


def adjoint_first_kernel(*refs):
    adjoint_kernel(1, *refs)


def adjoint_second_kernel(*refs):
    adjoint_kernel(0, *refs)


def image_first_kernel(q_now, slope_q, div, slope_p, q_new, out, q_out):
    q_out[...] = q_new[...]
    for cell in range(CX):
        out[0, cell] = q_now[cell] * div[cell]
        rho = slope_p[0, cell] * slope_q[0, cell] + slope_p[1, cell] * slope_q[1, cell]
        out[1, cell] = rho + slope_p[2, cell] * slope_q[2, cell]


def image_second_kernel(
    q_now, slope_q, div, slope_p, images, q_new, out, q_out
):
    q_out[...] = q_new[...]
    for cell in range(CX):
        out[0, cell] = images[0, cell] + q_now[cell] * div[cell]
        rho = slope_p[0, cell] * slope_q[0, cell] + slope_p[1, cell] * slope_q[1, cell]
        out[1, cell] = images[1, cell] + (rho + slope_p[2, cell] * slope_q[2, cell])


def image_kernel(info, q_now, scaled, scaled_a, scaled_b, div, slope, images, out, field):
    lane = lax.broadcasted_iota(jnp.int32, (CY, CZ), 1)
    place(info, field, scaled[...], scaled_a[...], planes_at(scaled_b, 0, 4), 4)
    for cell in range(CX):
        plane = field[cell + 4, PAD : PAD + CY, :]
        rho = images[1, cell] + slope[0, cell] * slope_x(field, cell + 4)
        rho = rho + slope[1, cell] * slope_y(field, cell + 4)
        rho = rho + slope[2, cell] * slope_z(plane, lane)
        out[0, cell] = step_squared * (images[0, cell] + q_now[cell] * div[cell])
        out[1, cell] = -step_squared * rho


def gather_kernel(picked, arrived, out_kappa, out_buoy):
    for t in range(TILES):
        kappa = jnp.zeros((CX, CZ), F32)
        rho = jnp.zeros((CX, CZ), F32)
        for s in range(arrived.shape[0]):
            here = picked[t, s : s + 1, :] > 0.0
            kappa = kappa + jnp.where(here, arrived[s, 0], 0.0)
            rho = rho + jnp.where(here, arrived[s, 1], 0.0)
        out_kappa[t] = kappa
        out_buoy[t] = rho


def work():
    return [
        pltpu.VMEM((WIDE, ROWS, CZ), F32),
        pltpu.VMEM((CX + 7, CY, CZ), F32),
        pltpu.VMEM((CX, ROWS, CZ), F32),
        pltpu.VMEM((CX, CY, CZ), F32),
    ]


def call(kernel, scalars, arrays, outs, scratch=(), flops=2_000_000):
    moved = sum(4 * a.size for a in arrays) + sum(4 * o.size for o in outs)
    return pl.pallas_call(
        kernel,
        out_shape=outs,
        in_specs=[SMEM] * len(scalars) + [VMEM] * len(arrays),
        out_specs=[VMEM] * len(outs),
        scratch_shapes=list(scratch),
        compiler_params=pltpu.CompilerParams(vmem_limit_bytes=32 * 1024 * 1024),
        cost_estimate=pl.CostEstimate(flops=flops, bytes_accessed=moved, transcendentals=0),
    )(*scalars, *arrays)


def swap_first(planes):
    count = lax.axis_size("dom")
    return lax.ppermute(planes, "dom", [(i ^ 1, i) for i in range(count)])


def swap_second(planes):
    pairs = []
    for i in range(1, lax.axis_size("dom") - 1, 2):
        pairs += [(i, i + 1), (i + 1, i)]
    return lax.ppermute(planes, "dom", pairs)


def shards(
    pressure_now,
    pressure_prev,
    adjoint_last,
    adjoint_after,
    kappa_model,
    buoy_model,
    aperture,
    source_cell,
    source_wave,
    receiver_cell,
    observed,
):
    dom = lax.axis_index("dom")
    odd = lax.rem(dom, 2)
    offset = dom * (CX * CY * CZ)
    source = source_cell[0]
    info = jnp.stack(
        [odd, source // (CY * CZ) - dom * CX, (source // CZ) % CY, source % CZ, offset]
    ).astype(jnp.int32)

    column = lax.dynamic_index_in_dim(aperture, dom, 1, keepdims=False)
    stacked = jnp.stack((kappa_model, buoy_model), axis=1)
    picks = column[:, None, None, None]
    chosen = stacked[0][None]
    for t in range(1, TILES):
        chosen = jnp.where(picks == t, stacked[t][None], chosen)
    block = lax.all_to_all(chosen, "shot", 0, 0, tiled=True)

    p0, p_prev = pressure_now[0], pressure_prev[0]
    q4, q5 = adjoint_last[0], adjoint_after[0]
    own, seven, four = plane_field(CX), plane_field(7), plane_field(4)
    spots, base_p, base_q, p0, q4, source_planes = call(
        prepare_kernel,
        [info, source_wave[0]],
        [receiver_cell, observed[0], p0, p_prev, q4, q5],
        [jax.ShapeDtypeStruct((STEPS + 1, CX, CY, CZ), F32), own, own, own, own, plane_field(STEPS)],
        flops=400_000_000,
    )
    ids = jnp.arange(TILES, dtype=jnp.int32)[:, None, None]
    picked = jnp.broadcast_to(
        (column[None, :, None] == ids).astype(F32), (TILES, column.shape[0], CZ)
    )
    block, spots, base_p, base_q, p0, q4, source_planes, picked = lax.optimization_barrier(
        (block, spots, base_p, base_q, p0, q4, source_planes, picked)
    )

    stiff = block[:, 0].transpose(1, 0, 2)
    buoy = block[:, 1].transpose(1, 0, 2)
    slopes = jax.ShapeDtypeStruct((3, CX, CY, CZ), F32)
    images = jax.ShapeDtypeStruct((2, CX, CY, CZ), F32)

    send_a, send_b, f4 = call(
        model_kernel, [info], [stiff, buoy, q4, p0], [plane_field(11), far_rows(11), own]
    )
    edge_b = swap_second(send_b)
    edge_a = swap_first(send_a)

    p1, send_a, send_b, near, far, div0, slope0, wide = call(
        first_kernel,
        [info],
        [p0, base_p, source_planes, stiff, buoy, edge_a, edge_b, f4],
        [own, seven, far_rows(7), seven, far_rows(7), own, slopes, plane_field(CX + 8)],
        work(),
    )
    from_b = swap_second(send_b)
    from_a = swap_first(send_a)
    far = swap_second(far)
    near = swap_first(near)
    (q_part,) = call(adjoint_part_kernel, [info], [base_q, f4, near, far, wide], [own], work())

    p2, send_a, send_b, div1, slope1 = call(
        second_kernel,
        [info],
        [p1, from_a, from_b, p0, source_planes, stiff, wide],
        [own, seven, far_rows(7), own, slopes],
        work(),
    )
    from_b = swap_second(send_b)
    from_a = swap_first(send_a)

    q3, f3, send_a, send_b, div2, slope2 = call(
        third_kernel,
        [info],
        [p2, from_a, from_b, p1, source_planes, stiff, wide, q_part, spots],
        [own, own, seven, far_rows(7), own, slopes],
        work(),
    )
    from_b = swap_second(send_b)
    from_a = swap_first(send_a)

    q2, f2, send_a, send_b, slope_q = call(
        adjoint_first_kernel,
        [info],
        [q3, q4, f3, from_a, from_b, stiff, wide, spots, p2],
        [own, own, seven, far_rows(7), slopes],
        work(),
    )
    from_b = swap_second(send_b)
    from_a = swap_first(send_a)
    image, q2_out = call(image_first_kernel, [], [q3, slope_q, div2, slope2, q2], [images, own])

    q1, f1, send_a, send_b, slope_q = call(
        adjoint_second_kernel,
        [info],
        [q2, q3, f2, from_a, from_b, stiff, wide, spots, p1],
        [own, own, four, far_rows(4), slopes],
        work(),
    )
    from_b = swap_second(send_b)
    from_a = swap_first(send_a)
    image, q1_out = call(
        image_second_kernel, [], [q2, slope_q, div1, slope1, image, q1], [images, own]
    )

    (image,) = call(
        image_kernel,
        [info],
        [q1, f1, from_a, from_b, div0, slope0, image],
        [images],
        [pltpu.VMEM((CX + 8, ROWS, CZ), F32)],
    )
    arrived = lax.all_to_all(image.transpose(2, 0, 1, 3), "shot", 0, 0, tiled=True)
    tiles = jax.ShapeDtypeStruct((TILES, CX, CZ), F32)
    grad_kappa, grad_buoy = call(gather_kernel, [], [picked, arrived], [tiles, tiles])
    return (grad_kappa, grad_buoy, q1_out[None], q2_out[None])


def solution(mesh):
    in_specs = (
        P("shot", "dom", None, None),
        P("shot", "dom", None, None),
        P("shot", "dom", None, None),
        P("shot", "dom", None, None),
        P(None, "dom", "shot"),
        P(None, "dom", "shot"),
        P(),
        P("shot"),
        P("shot", None),
        P("shot", None),
        P("shot", None, None),
    )
    out_specs = (
        P(None, "dom", "shot"),
        P(None, "dom", "shot"),
        P("shot", "dom", None, None),
        P("shot", "dom", None, None),
    )
    return jax.shard_map(shards, mesh=mesh, in_specs=in_specs, out_specs=out_specs, check_vma=False)
```

```python
import jax
import jax.numpy as jnp
from jax import lax
from jax.experimental import pallas as pl
from jax.experimental.pallas import tpu as pltpu
from jax.sharding import PartitionSpec as P

CX = 8
CY = 32
CZ = 128
TILES = 4
STEPS = 3
REC = 512
PAD = 8
ROWS = CY + 2 * PAD
WIDE = CX + 14

COEFFS = (1225.0 / 1024.0, -245.0 / 3072.0, 49.0 / 5120.0, -5.0 / 7168.0)
step_squared = 0.02

VMEM = pl.BlockSpec(memory_space=pltpu.VMEM)
SMEM = pl.BlockSpec(memory_space=pltpu.SMEM)
F32 = jnp.float32


def plane_field(count):
    return jax.ShapeDtypeStruct((count, CY, CZ), F32)


def far_rows(count):
    return jax.ShapeDtypeStruct((count * CY + 8, CZ), F32)


def rows_of(planes):
    return planes.reshape(planes.shape[0] * CY, CZ)


def planes_at(rows, start, count):
    return rows[start * CY : (start + count) * CY, :].reshape(count, CY, CZ)


def lane_shift(plane, by, lane):
    if by == 0:
        return plane
    moved = pltpu.roll(plane, (-by) % CZ, 1)
    keep = lane < CZ - by if by > 0 else lane >= -by
    return jnp.where(keep, moved, 0.0)


def stencil(at):
    total = COEFFS[0] * (at(0) - at(-1))
    for k in range(2, 5):
        total = total + COEFFS[k - 1] * (at(k - 1) - at(-k))
    return total


def place(info, target, own, first, second, width):
    target[:, 0:PAD, :] = jnp.zeros((target.shape[0], PAD, CZ), F32)
    target[:, PAD + CY : ROWS, :] = jnp.zeros((target.shape[0], PAD, CZ), F32)
    inner = slice(PAD, PAD + CY)
    target[width : width + CX, inner, :] = own
    odd = info[0] == 1

    @pl.when(odd)
    def _():
        target[0:width, inner, :] = first
        target[width + CX : 2 * width + CX, inner, :] = second

    @pl.when(jnp.logical_not(odd))
    def _():
        target[0:width, inner, :] = second
        target[width + CX : 2 * width + CX, inner, :] = first


def for_partner(info, target, head, tail):
    odd = info[0] == 1

    @pl.when(odd)
    def _():
        target[...] = head()

    @pl.when(jnp.logical_not(odd))
    def _():
        target[...] = tail()


def hand_over(info, send_a, send_b, field):
    width = send_a.shape[0]
    for_partner(info, send_a, lambda: field[0:width], lambda: field[CX - width : CX])
    for_partner(
        info,
        send_b.at[0 : width * CY],
        lambda: rows_of(field[CX - width : CX]),
        lambda: rows_of(field[0:width]),
    )
    send_b[width * CY :, :] = jnp.zeros((8, CZ), F32)


def slope_x(field, at):
    return stencil(lambda s: field[at + s, PAD : PAD + CY, :])


def slope_y(field, at):
    return stencil(lambda s: field[at, PAD + s : PAD + CY + s, :])


def slope_z(plane, lane):
    return stencil(lambda s: lane_shift(plane, s, lane))


def operate(field, width, buoy, gx, gy, acc, slopes):
    lane = lax.broadcasted_iota(jnp.int32, (CY, CZ), 1)
    gy[:, 0:PAD, :] = jnp.zeros((CX, PAD, CZ), F32)
    gy[:, PAD + CY : ROWS, :] = jnp.zeros((CX, PAD, CZ), F32)
    for cell in range(-3, CX + 4):
        sx = slope_x(field, cell + width)
        gx[cell + 3] = buoy[cell + 4] * sx
        if 0 <= cell < CX:
            weight = buoy[cell + 4]
            plane = field[cell + width, PAD : PAD + CY, :]
            sy = slope_y(field, cell + width)
            sz = slope_z(plane, lane)
            gy[cell, PAD : PAD + CY, :] = weight * sy
            gz = weight * sz
            acc[cell] = stencil(lambda s: lane_shift(gz, s + 1, lane))
            slopes(cell, sx, sy, sz)
    for cell in range(CX):
        div = stencil(lambda s: gx[cell + 4 + s])
        div = div + stencil(lambda s: gy[cell, PAD + 1 + s : PAD + 1 + s + CY, :])
        yield cell, div + acc[cell]


def prepare_kernel(
    info, wave, cells, seen, now, before, last, after, out, base_p, base_q, now_out, last_out, source_out
):
    base_p[...] = 2.0 * now[...] - before[...]
    base_q[...] = 2.0 * last[...] - after[...]
    now_out[...] = now[...]
    last_out[...] = last[...]
    y = lax.broadcasted_iota(jnp.int32, (CY, CZ), 0)
    z = lax.broadcasted_iota(jnp.int32, (CY, CZ), 1)
    hit = (y == info[2]) & (z == info[3])
    for n in range(STEPS):
        source_out[n] = jnp.where(hit, wave[n], 0.0)

    index = cells[...] - info[4]
    row = lax.shift_right_arithmetic(index, 7)
    z = lax.bitwise_and(index, 127)
    rows = lax.broadcasted_iota(jnp.int32, (CX * CY, REC), 0)
    pick = jnp.where(rows == row, 1.0, 0.0).astype(jnp.bfloat16)
    lanes = lax.broadcasted_iota(jnp.int32, (CZ, REC), 0)
    here = lanes == z

    def spread(values):
        right = jnp.where(here, values, 0.0).astype(jnp.bfloat16)
        return lax.dot_general(
            pick, right, (((1,), (1,)), ((), ())), preferred_element_type=F32
        )

    out[0] = spread(jnp.ones((1, REC), F32)).reshape(CX, CY, CZ)
    for n in range(STEPS):
        rest = seen[n : n + 1, :]
        total = None
        for _ in range(3):
            part = rest.astype(jnp.bfloat16).astype(F32)
            rest = rest - part
            total = spread(part) if total is None else total + spread(part)
        out[n + 1] = total.reshape(CX, CY, CZ)


def model_kernel(info, stiff, buoy, last, send_a, send_b, scaled):
    scaled[...] = stiff[...] * last[...]
    for_partner(info, send_a, lambda: buoy[0:4], lambda: buoy[4:8])
    for_partner(
        info,
        send_b.at[0 : 4 * CY],
        lambda: rows_of(buoy[4:8]),
        lambda: rows_of(buoy[0:4]),
    )
    send_b[4 * CY :, :] = jnp.zeros((8, CZ), F32)


def widen_kernel(info, now, now_a, now_b, out):
    place(info, out, now[...], now_a[...], now_b[...], 7)


def forward(info, source, base, stiff, field, buoy, gx, gy, acc, div_out, slope_out, store):
    def keep(cell, sx, sy, sz):
        slope_out[0, cell] = sx
        slope_out[1, cell] = sy
        slope_out[2, cell] = sz

    for cell, div in operate(field, 7, buoy, gx, gy, acc, keep):
        div_out[cell] = div
        value = base(cell) + step_squared * stiff[cell] * div
        store(cell, value + jnp.where(info[1] == cell, source, 0.0))


def widen_buoy(info, buoy, first, second, target):
    target[4 : 4 + CX] = buoy[...]
    odd = info[0] == 1

    @pl.when(odd)
    def _():
        target[0:4] = first[0:4]
        target[4 + CX : 8 + CX] = planes_at(second, 0, 4)

    @pl.when(jnp.logical_not(odd))
    def _():
        target[0:4] = planes_at(second, 0, 4)
        target[4 + CX : 8 + CX] = first[0:4]


def first_kernel(
    info, padded, base, source, stiff, buoy, edge_a, edge_b, scaled,
    p_out, send_a, send_b, near, far, div_out, slope_out, buoy_out,
    gx, gy, acc,
):
    widen_buoy(info, buoy, edge_a, edge_b, buoy_out)

    def store(cell, value):
        p_out[cell] = value

    forward(
        info, source[0], lambda cell: base[cell],
        stiff, padded, buoy_out, gx, gy, acc, div_out, slope_out, store,
    )
    hand_over(info, send_a, send_b, p_out)
    hand_over(info, near, far, scaled)


def adjoint_part_kernel(
    info, base, scaled, near, far, buoy,
    q_out,
    field, gx, gy, acc,
):
    place(info, field, scaled[...], near[...], planes_at(far, 0, 7), 7)
    for cell, div in operate(field, 7, buoy, gx, gy, acc, lambda *_: None):
        q_out[cell] = base[cell] + step_squared * div


def second_kernel(
    info, now, now_a, now_b, before, source, stiff, buoy,
    p_out, send_a, send_b, div_out, slope_out,
    field, gx, gy, acc,
):
    place(info, field, now[...], now_a[...], planes_at(now_b, 0, 7), 7)

    def store(cell, value):
        p_out[cell] = value

    forward(
        info, source[1], lambda cell: 2.0 * now[cell] - before[cell],
        stiff, field, buoy, gx, gy, acc, div_out, slope_out, store,
    )
    hand_over(info, send_a, send_b, p_out)


def third_kernel(
    info, now, now_a, now_b, before, source, stiff, buoy, q_part, spots,
    q_out, scaled, send_a, send_b, div_out, slope_out,
    field, gx, gy, acc,
):
    place(info, field, now[...], now_a[...], planes_at(now_b, 0, 7), 7)

    def store(cell, value):
        q = q_part[cell] + (spots[0, cell] * value - spots[3, cell])
        q_out[cell] = q
        scaled[cell] = stiff[cell] * q

    forward(
        info, source[2], lambda cell: 2.0 * now[cell] - before[cell],
        stiff, field, buoy, gx, gy, acc, div_out, slope_out, store,
    )
    hand_over(info, send_a, send_b, scaled)


def adjoint_kernel(
    n, info, q_now, q_after, scaled, scaled_a, scaled_b, stiff, buoy, spots, p_then,
    q_out, scaled_out, send_a, send_b, slope_out,
    field, gx, gy, acc,
):
    place(info, field, scaled[...], scaled_a[...], planes_at(scaled_b, 0, 7), 7)

    def keep(cell, sx, sy, sz):
        slope_out[0, cell] = sx
        slope_out[1, cell] = sy
        slope_out[2, cell] = sz

    for cell, total in operate(field, 7, buoy, gx, gy, acc, keep):
        q = 2.0 * q_now[cell] - q_after[cell] + step_squared * total
        q = q + (spots[0, cell] * p_then[cell] - spots[n + 1, cell])
        q_out[cell] = q
        scaled_out[cell] = stiff[cell] * q
    hand_over(info, send_a, send_b, scaled_out)


def adjoint_first_kernel(*refs):
    adjoint_kernel(1, *refs)


def adjoint_second_kernel(*refs):
    adjoint_kernel(0, *refs)


def image_first_kernel(q_now, slope_q, div, slope_p, q_new, out, q_out):
    q_out[...] = q_new[...]
    for cell in range(CX):
        out[0, cell] = q_now[cell] * div[cell]
        rho = slope_p[0, cell] * slope_q[0, cell] + slope_p[1, cell] * slope_q[1, cell]
        out[1, cell] = rho + slope_p[2, cell] * slope_q[2, cell]


def image_second_kernel(
    q_now, slope_q, div, slope_p, images, q_new, out, q_out
):
    q_out[...] = q_new[...]
    for cell in range(CX):
        out[0, cell] = images[0, cell] + q_now[cell] * div[cell]
        rho = slope_p[0, cell] * slope_q[0, cell] + slope_p[1, cell] * slope_q[1, cell]
        out[1, cell] = images[1, cell] + (rho + slope_p[2, cell] * slope_q[2, cell])


def image_kernel(info, q_now, scaled, scaled_a, scaled_b, div, slope, images, out, field):
    lane = lax.broadcasted_iota(jnp.int32, (CY, CZ), 1)
    place(info, field, scaled[...], scaled_a[...], planes_at(scaled_b, 0, 4), 4)
    for cell in range(CX):
        plane = field[cell + 4, PAD : PAD + CY, :]
        rho = images[1, cell] + slope[0, cell] * slope_x(field, cell + 4)
        rho = rho + slope[1, cell] * slope_y(field, cell + 4)
        rho = rho + slope[2, cell] * slope_z(plane, lane)
        out[0, cell] = step_squared * (images[0, cell] + q_now[cell] * div[cell])
        out[1, cell] = -step_squared * rho


def gather_kernel(picked, arrived, out_kappa, out_buoy):
    for t in range(TILES):
        kappa = jnp.zeros((CX, CZ), F32)
        rho = jnp.zeros((CX, CZ), F32)
        for s in range(arrived.shape[0]):
            here = picked[t, s : s + 1, :] > 0.0
            kappa = kappa + jnp.where(here, arrived[s, 0], 0.0)
            rho = rho + jnp.where(here, arrived[s, 1], 0.0)
        out_kappa[t] = kappa
        out_buoy[t] = rho


def work():
    return [
        pltpu.VMEM((WIDE, ROWS, CZ), F32),
        pltpu.VMEM((CX + 7, CY, CZ), F32),
        pltpu.VMEM((CX, ROWS, CZ), F32),
        pltpu.VMEM((CX, CY, CZ), F32),
    ]


def call(kernel, scalars, arrays, outs, scratch=(), flops=2_000_000):
    moved = sum(4 * a.size for a in arrays) + sum(4 * o.size for o in outs)
    return pl.pallas_call(
        kernel,
        out_shape=outs,
        in_specs=[SMEM] * len(scalars) + [VMEM] * len(arrays),
        out_specs=[VMEM] * len(outs),
        scratch_shapes=list(scratch),
        compiler_params=pltpu.CompilerParams(vmem_limit_bytes=32 * 1024 * 1024),
        cost_estimate=pl.CostEstimate(flops=flops, bytes_accessed=moved, transcendentals=0),
    )(*scalars, *arrays)


def swap_first(planes):
    count = lax.axis_size("dom")
    return lax.ppermute(planes, "dom", [(i ^ 1, i) for i in range(count)])


def swap_second(planes):
    pairs = []
    for i in range(1, lax.axis_size("dom") - 1, 2):
        pairs += [(i, i + 1), (i + 1, i)]
    return lax.ppermute(planes, "dom", pairs)


def shards(
    pressure_now,
    pressure_prev,
    adjoint_last,
    adjoint_after,
    kappa_model,
    buoy_model,
    aperture,
    source_cell,
    source_wave,
    receiver_cell,
    observed,
):
    dom = lax.axis_index("dom")
    odd = lax.rem(dom, 2)
    offset = dom * (CX * CY * CZ)
    source = source_cell[0]
    info = jnp.stack(
        [odd, source // (CY * CZ) - dom * CX, (source // CZ) % CY, source % CZ, offset]
    ).astype(jnp.int32)

    column = lax.dynamic_index_in_dim(aperture, dom, 1, keepdims=False)
    stacked = jnp.stack((kappa_model, buoy_model), axis=1)
    picks = column[:, None, None, None]
    chosen = stacked[0][None]
    for t in range(1, TILES):
        chosen = jnp.where(picks == t, stacked[t][None], chosen)
    block = lax.all_to_all(chosen, "shot", 0, 0, tiled=True)

    p0, p_prev = pressure_now[0], pressure_prev[0]
    q4, q5 = adjoint_last[0], adjoint_after[0]
    p0_b = swap_second(jnp.where(odd == 1, pressure_now[0][1:8], pressure_now[0][0:7]))
    p0_a = swap_first(jnp.where(odd == 1, pressure_now[0][0:7], pressure_now[0][1:8]))
    own, seven, four = plane_field(CX), plane_field(7), plane_field(4)
    spots, base_p, base_q, p0, q4, source_planes = call(
        prepare_kernel,
        [info, source_wave[0]],
        [receiver_cell, observed[0], p0, p_prev, q4, q5],
        [jax.ShapeDtypeStruct((STEPS + 1, CX, CY, CZ), F32), own, own, own, own, plane_field(STEPS)],
        flops=400_000_000,
    )
    ids = jnp.arange(TILES, dtype=jnp.int32)[:, None, None]
    picked = jnp.broadcast_to(
        (column[None, :, None] == ids).astype(F32), (TILES, column.shape[0], CZ)
    )
    block, spots, base_p, base_q, p0, q4, source_planes, picked = lax.optimization_barrier(
        (block, spots, base_p, base_q, p0, q4, source_planes, picked)
    )

    stiff = block[:, 0].transpose(1, 0, 2)
    buoy = block[:, 1].transpose(1, 0, 2)
    slopes = jax.ShapeDtypeStruct((3, CX, CY, CZ), F32)
    images = jax.ShapeDtypeStruct((2, CX, CY, CZ), F32)

    send_a, send_b, f4 = call(
        model_kernel, [info], [stiff, buoy, q4], [four, far_rows(4), own]
    )
    edge_b = swap_second(send_b)
    edge_a = swap_first(send_a)

    (padded,) = call(
        widen_kernel,
        [info],
        [p0, p0_a, p0_b],
        [jax.ShapeDtypeStruct((WIDE, ROWS, CZ), F32)],
    )
    p1, send_a, send_b, near, far, div0, slope0, wide = call(
        first_kernel,
        [info],
        [padded, base_p, source_planes, stiff, buoy, edge_a, edge_b, f4],
        [own, seven, far_rows(7), seven, far_rows(7), own, slopes, plane_field(CX + 8)],
        work()[1:],
    )
    from_b = swap_second(send_b)
    from_a = swap_first(send_a)
    far = swap_second(far)
    near = swap_first(near)
    (q_part,) = call(adjoint_part_kernel, [info], [base_q, f4, near, far, wide], [own], work())

    p2, send_a, send_b, div1, slope1 = call(
        second_kernel,
        [info],
        [p1, from_a, from_b, p0, source_planes, stiff, wide],
        [own, seven, far_rows(7), own, slopes],
        work(),
    )
    from_b = swap_second(send_b)
    from_a = swap_first(send_a)

    q3, f3, send_a, send_b, div2, slope2 = call(
        third_kernel,
        [info],
        [p2, from_a, from_b, p1, source_planes, stiff, wide, q_part, spots],
        [own, own, seven, far_rows(7), own, slopes],
        work(),
    )
    from_b = swap_second(send_b)
    from_a = swap_first(send_a)

    q2, f2, send_a, send_b, slope_q = call(
        adjoint_first_kernel,
        [info],
        [q3, q4, f3, from_a, from_b, stiff, wide, spots, p2],
        [own, own, seven, far_rows(7), slopes],
        work(),
    )
    from_b = swap_second(send_b)
    from_a = swap_first(send_a)
    image, q2_out = call(image_first_kernel, [], [q3, slope_q, div2, slope2, q2], [images, own])

    q1, f1, send_a, send_b, slope_q = call(
        adjoint_second_kernel,
        [info],
        [q2, q3, f2, from_a, from_b, stiff, wide, spots, p1],
        [own, own, four, far_rows(4), slopes],
        work(),
    )
    from_b = swap_second(send_b)
    from_a = swap_first(send_a)
    image, q1_out = call(
        image_second_kernel, [], [q2, slope_q, div1, slope1, image, q1], [images, own]
    )

    (image,) = call(
        image_kernel,
        [info],
        [q1, f1, from_a, from_b, div0, slope0, image],
        [images],
        [pltpu.VMEM((CX + 8, ROWS, CZ), F32)],
    )
    arrived = lax.all_to_all(image.transpose(2, 0, 1, 3), "shot", 0, 0, tiled=True)
    tiles = jax.ShapeDtypeStruct((TILES, CX, CZ), F32)
    grad_kappa, grad_buoy = call(gather_kernel, [], [picked, arrived], [tiles, tiles])
    return (grad_kappa, grad_buoy, q1_out[None], q2_out[None])


def solution(mesh):
    in_specs = (
        P("shot", "dom", None, None),
        P("shot", "dom", None, None),
        P("shot", "dom", None, None),
        P("shot", "dom", None, None),
        P(None, "dom", "shot"),
        P(None, "dom", "shot"),
        P(),
        P("shot"),
        P("shot", None),
        P("shot", None),
        P("shot", None, None),
    )
    out_specs = (
        P(None, "dom", "shot"),
        P(None, "dom", "shot"),
        P("shot", "dom", None, None),
        P("shot", "dom", None, None),
    )
    return jax.shard_map(shards, mesh=mesh, in_specs=in_specs, out_specs=out_specs, check_vma=False)
```

```python
import jax
import jax.numpy as jnp
from jax import lax
from jax.experimental import pallas as pl
from jax.experimental.pallas import tpu as pltpu
from jax.sharding import PartitionSpec as P

CX = 8
CY = 32
CZ = 128
TILES = 4
STEPS = 3
REC = 512
PAD = 8
ROWS = CY + 2 * PAD
WIDE = CX + 14

COEFFS = (1225.0 / 1024.0, -245.0 / 3072.0, 49.0 / 5120.0, -5.0 / 7168.0)
step_squared = 0.02

VMEM = pl.BlockSpec(memory_space=pltpu.VMEM)
SMEM = pl.BlockSpec(memory_space=pltpu.SMEM)
F32 = jnp.float32


def plane_field(count):
    return jax.ShapeDtypeStruct((count, CY, CZ), F32)


def far_rows(count):
    return jax.ShapeDtypeStruct((count * CY + 8, CZ), F32)


def rows_of(planes):
    return planes.reshape(planes.shape[0] * CY, CZ)


def planes_at(rows, start, count):
    return rows[start * CY : (start + count) * CY, :].reshape(count, CY, CZ)


def lane_shift(plane, by, lane):
    if by == 0:
        return plane
    moved = pltpu.roll(plane, (-by) % CZ, 1)
    keep = lane < CZ - by if by > 0 else lane >= -by
    return jnp.where(keep, moved, 0.0)


def stencil(at):
    total = COEFFS[0] * (at(0) - at(-1))
    for k in range(2, 5):
        total = total + COEFFS[k - 1] * (at(k - 1) - at(-k))
    return total


def place(info, target, own, first, second, width):
    target[:, 0:PAD, :] = jnp.zeros((target.shape[0], PAD, CZ), F32)
    target[:, PAD + CY : ROWS, :] = jnp.zeros((target.shape[0], PAD, CZ), F32)
    inner = slice(PAD, PAD + CY)
    for cell in range(CX):
        target[width + cell, inner, :] = own[cell]
    odd = info[0] == 1

    @pl.when(odd)
    def _():
        target[0:width, inner, :] = first()
        target[width + CX : 2 * width + CX, inner, :] = second()

    @pl.when(jnp.logical_not(odd))
    def _():
        target[0:width, inner, :] = second()
        target[width + CX : 2 * width + CX, inner, :] = first()


def for_partner(info, target, head, tail):
    odd = info[0] == 1

    @pl.when(odd)
    def _():
        target[...] = head()

    @pl.when(jnp.logical_not(odd))
    def _():
        target[...] = tail()


def hand_over(info, send_a, send_b, field):
    width = send_a.shape[0]
    for_partner(info, send_a, lambda: field[0:width], lambda: field[CX - width : CX])
    for_partner(
        info,
        send_b.at[0 : width * CY],
        lambda: rows_of(field[CX - width : CX]),
        lambda: rows_of(field[0:width]),
    )
    send_b[width * CY :, :] = jnp.zeros((8, CZ), F32)


def slope_x(field, at):
    return stencil(lambda s: field[at + s, PAD : PAD + CY, :])


def slope_y(field, at):
    return stencil(lambda s: field[at, PAD + s : PAD + CY + s, :])


def slope_z(plane, lane):
    return stencil(lambda s: lane_shift(plane, s, lane))


def along_z(planes, table):
    rows = planes.reshape(CX * CY, CZ)
    out = lax.dot_general(
        rows,
        table,
        (((1,), (0,)), ((), ())),
        precision=lax.Precision.HIGHEST,
        preferred_element_type=F32,
    )
    return out.reshape(CX, CY, CZ)


def operate(field, width, buoy, tables, gx, gy, acc, slopes):
    gy[:, 0:PAD, :] = jnp.zeros((CX, PAD, CZ), F32)
    gy[:, PAD + CY : ROWS, :] = jnp.zeros((CX, PAD, CZ), F32)
    slope = along_z(field[width : width + CX, PAD : PAD + CY, :], tables[0])
    acc[...] = along_z(buoy[4 : 4 + CX] * slope, tables[1])
    for cell in range(-3, CX + 4):
        sx = slope_x(field, cell + width)
        gx[cell + 3] = buoy[cell + 4] * sx
        if 0 <= cell < CX:
            sy = slope_y(field, cell + width)
            gy[cell, PAD : PAD + CY, :] = buoy[cell + 4] * sy
            slopes(cell, sx, sy, slope[cell])
    for cell in range(CX):
        div = stencil(lambda s: gx[cell + 4 + s])
        div = div + stencil(lambda s: gy[cell, PAD + 1 + s : PAD + 1 + s + CY, :])
        yield cell, div + acc[cell]


def prepare_kernel(
    info, wave, cells, seen, now, before, last, after, out, base_p, base_q, now_out, last_out, source_out,
    tables,
):
    gap = lax.broadcasted_iota(jnp.int32, (CZ, CZ), 0) - lax.broadcasted_iota(jnp.int32, (CZ, CZ), 1)
    for at in range(2):
        table = jnp.zeros((CZ, CZ), F32)
        for k in range(1, 5):
            table = table + jnp.where(gap == k - 1 + at, COEFFS[k - 1], 0.0)
            table = table - jnp.where(gap == at - k, COEFFS[k - 1], 0.0)
        tables[at] = table
    base_p[...] = 2.0 * now[...] - before[...]
    base_q[...] = 2.0 * last[...] - after[...]
    now_out[...] = now[...]
    last_out[...] = last[...]
    y = lax.broadcasted_iota(jnp.int32, (CY, CZ), 0)
    z = lax.broadcasted_iota(jnp.int32, (CY, CZ), 1)
    hit = (y == info[2]) & (z == info[3])
    for n in range(STEPS):
        source_out[n] = jnp.where(hit, wave[n], 0.0)

    index = cells[...] - info[4]
    row = lax.shift_right_arithmetic(index, 7)
    z = lax.bitwise_and(index, 127)
    rows = lax.broadcasted_iota(jnp.int32, (CX * CY, REC), 0)
    pick = jnp.where(rows == row, 1.0, 0.0).astype(jnp.bfloat16)
    lanes = lax.broadcasted_iota(jnp.int32, (CZ, REC), 0)
    here = lanes == z

    def spread(values):
        right = jnp.where(here, values, 0.0).astype(jnp.bfloat16)
        return lax.dot_general(
            pick, right, (((1,), (1,)), ((), ())), preferred_element_type=F32
        )

    out[0] = spread(jnp.ones((1, REC), F32)).reshape(CX, CY, CZ)
    for n in range(STEPS):
        rest = seen[n : n + 1, :]
        total = None
        for _ in range(3):
            part = rest.astype(jnp.bfloat16).astype(F32)
            rest = rest - part
            total = spread(part) if total is None else total + spread(part)
        out[n + 1] = total.reshape(CX, CY, CZ)


def model_kernel(info, stiff, buoy, last, send_a, send_b, scaled):
    scaled[...] = stiff[...] * last[...]
    for_partner(info, send_a, lambda: buoy[0:4], lambda: buoy[4:8])
    for_partner(
        info,
        send_b.at[0 : 4 * CY],
        lambda: rows_of(buoy[4:8]),
        lambda: rows_of(buoy[0:4]),
    )
    send_b[4 * CY :, :] = jnp.zeros((8, CZ), F32)


def widen_kernel(info, now, now_a, now_b, out):
    place(info, out, now, lambda: now_a[...], lambda: now_b[...], 7)


def forward(info, source, base, stiff, field, buoy, tables, gx, gy, acc, div_out, slope_out, store):
    def keep(cell, sx, sy, sz):
        slope_out[0, cell] = sx
        slope_out[1, cell] = sy
        slope_out[2, cell] = sz

    for cell, div in operate(field, 7, buoy, tables, gx, gy, acc, keep):
        div_out[cell] = div
        value = base(cell) + step_squared * stiff[cell] * div
        store(cell, value + jnp.where(info[1] == cell, source, 0.0))


def widen_buoy(info, buoy, first, second, target):
    target[4 : 4 + CX] = buoy[...]
    odd = info[0] == 1

    @pl.when(odd)
    def _():
        target[0:4] = first[0:4]
        target[4 + CX : 8 + CX] = planes_at(second, 0, 4)

    @pl.when(jnp.logical_not(odd))
    def _():
        target[0:4] = planes_at(second, 0, 4)
        target[4 + CX : 8 + CX] = first[0:4]


def first_kernel(
    info, tables, padded, base, source, stiff, buoy, edge_a, edge_b, scaled,
    p_out, send_a, send_b, near, far, div_out, slope_out, buoy_out,
    gx, gy, acc,
):
    widen_buoy(info, buoy, edge_a, edge_b, buoy_out)

    def store(cell, value):
        p_out[cell] = value

    forward(
        info, source[0], lambda cell: base[cell],
        stiff, padded, buoy_out, tables, gx, gy, acc, div_out, slope_out, store,
    )
    hand_over(info, send_a, send_b, p_out)
    hand_over(info, near, far, scaled)


def adjoint_part_kernel(
    info, tables, base, scaled, near, far, buoy,
    q_out,
    field, gx, gy, acc,
):
    place(info, field, scaled, lambda: near[...], lambda: planes_at(far, 0, 7), 7)
    for cell, div in operate(field, 7, buoy, tables, gx, gy, acc, lambda *_: None):
        q_out[cell] = base[cell] + step_squared * div


def second_kernel(
    info, tables, now, now_a, now_b, before, source, stiff, buoy,
    p_out, send_a, send_b, div_out, slope_out,
    field, gx, gy, acc,
):
    place(info, field, now, lambda: now_a[...], lambda: planes_at(now_b, 0, 7), 7)

    def store(cell, value):
        p_out[cell] = value

    forward(
        info, source[1], lambda cell: 2.0 * now[cell] - before[cell],
        stiff, field, buoy, tables, gx, gy, acc, div_out, slope_out, store,
    )
    hand_over(info, send_a, send_b, p_out)


def third_kernel(
    info, tables, now, now_a, now_b, before, source, stiff, buoy, q_part, spots,
    q_out, scaled, send_a, send_b, div_out, slope_out,
    field, gx, gy, acc,
):
    place(info, field, now, lambda: now_a[...], lambda: planes_at(now_b, 0, 7), 7)

    def store(cell, value):
        q = q_part[cell] + (spots[0, cell] * value - spots[3, cell])
        q_out[cell] = q
        scaled[cell] = stiff[cell] * q

    forward(
        info, source[2], lambda cell: 2.0 * now[cell] - before[cell],
        stiff, field, buoy, tables, gx, gy, acc, div_out, slope_out, store,
    )
    hand_over(info, send_a, send_b, scaled)


def adjoint_kernel(
    n, info, tables, q_now, q_after, scaled, scaled_a, scaled_b, stiff, buoy, spots, p_then,
    q_out, scaled_out, send_a, send_b, slope_out,
    field, gx, gy, acc,
):
    place(info, field, scaled, lambda: scaled_a[...], lambda: planes_at(scaled_b, 0, 7), 7)

    def keep(cell, sx, sy, sz):
        slope_out[0, cell] = sx
        slope_out[1, cell] = sy
        slope_out[2, cell] = sz

    for cell, total in operate(field, 7, buoy, tables, gx, gy, acc, keep):
        q = 2.0 * q_now[cell] - q_after[cell] + step_squared * total
        q = q + (spots[0, cell] * p_then[cell] - spots[n + 1, cell])
        q_out[cell] = q
        scaled_out[cell] = stiff[cell] * q
    hand_over(info, send_a, send_b, scaled_out)


def adjoint_first_kernel(*refs):
    adjoint_kernel(1, *refs)


def adjoint_second_kernel(*refs):
    adjoint_kernel(0, *refs)


def image_first_kernel(q_now, slope_q, div, slope_p, q_new, out, q_out):
    q_out[...] = q_new[...]
    for cell in range(CX):
        out[0, cell] = q_now[cell] * div[cell]
        rho = slope_p[0, cell] * slope_q[0, cell] + slope_p[1, cell] * slope_q[1, cell]
        out[1, cell] = rho + slope_p[2, cell] * slope_q[2, cell]


def image_second_kernel(
    q_now, slope_q, div, slope_p, images, q_new, out, q_out
):
    q_out[...] = q_new[...]
    for cell in range(CX):
        out[0, cell] = images[0, cell] + q_now[cell] * div[cell]
        rho = slope_p[0, cell] * slope_q[0, cell] + slope_p[1, cell] * slope_q[1, cell]
        out[1, cell] = images[1, cell] + (rho + slope_p[2, cell] * slope_q[2, cell])


def image_kernel(info, q_now, scaled, scaled_a, scaled_b, div, slope, images, out, field):
    lane = lax.broadcasted_iota(jnp.int32, (CY, CZ), 1)
    place(info, field, scaled, lambda: scaled_a[...], lambda: planes_at(scaled_b, 0, 4), 4)
    for cell in range(CX):
        plane = field[cell + 4, PAD : PAD + CY, :]
        rho = images[1, cell] + slope[0, cell] * slope_x(field, cell + 4)
        rho = rho + slope[1, cell] * slope_y(field, cell + 4)
        rho = rho + slope[2, cell] * slope_z(plane, lane)
        out[0, cell] = step_squared * (images[0, cell] + q_now[cell] * div[cell])
        out[1, cell] = -step_squared * rho


def gather_kernel(picked, arrived, out_kappa, out_buoy):
    for t in range(TILES):
        kappa = jnp.zeros((CX, CZ), F32)
        rho = jnp.zeros((CX, CZ), F32)
        for s in range(arrived.shape[0]):
            here = picked[t, s : s + 1, :] > 0.0
            kappa = kappa + jnp.where(here, arrived[s, 0], 0.0)
            rho = rho + jnp.where(here, arrived[s, 1], 0.0)
        out_kappa[t] = kappa
        out_buoy[t] = rho


def work():
    return [
        pltpu.VMEM((WIDE, ROWS, CZ), F32),
        pltpu.VMEM((CX + 7, CY, CZ), F32),
        pltpu.VMEM((CX, ROWS, CZ), F32),
        pltpu.VMEM((CX, CY, CZ), F32),
    ]


def call(kernel, scalars, arrays, outs, scratch=(), flops=2_000_000):
    moved = sum(4 * a.size for a in arrays) + sum(4 * o.size for o in outs)
    return pl.pallas_call(
        kernel,
        out_shape=outs,
        in_specs=[SMEM] * len(scalars) + [VMEM] * len(arrays),
        out_specs=[VMEM] * len(outs),
        scratch_shapes=list(scratch),
        compiler_params=pltpu.CompilerParams(vmem_limit_bytes=32 * 1024 * 1024),
        cost_estimate=pl.CostEstimate(flops=flops, bytes_accessed=moved, transcendentals=0),
    )(*scalars, *arrays)


def swap_first(planes):
    count = lax.axis_size("dom")
    return lax.ppermute(planes, "dom", [(i ^ 1, i) for i in range(count)])


def swap_second(planes):
    pairs = []
    for i in range(1, lax.axis_size("dom") - 1, 2):
        pairs += [(i, i + 1), (i + 1, i)]
    return lax.ppermute(planes, "dom", pairs)


def shards(
    pressure_now,
    pressure_prev,
    adjoint_last,
    adjoint_after,
    kappa_model,
    buoy_model,
    aperture,
    source_cell,
    source_wave,
    receiver_cell,
    observed,
):
    dom = lax.axis_index("dom")
    odd = lax.rem(dom, 2)
    offset = dom * (CX * CY * CZ)
    source = source_cell[0]
    info = jnp.stack(
        [odd, source // (CY * CZ) - dom * CX, (source // CZ) % CY, source % CZ, offset]
    ).astype(jnp.int32)

    column = lax.dynamic_index_in_dim(aperture, dom, 1, keepdims=False)
    stacked = jnp.stack((kappa_model, buoy_model), axis=1)
    picks = column[:, None, None, None]
    chosen = stacked[0][None]
    for t in range(1, TILES):
        chosen = jnp.where(picks == t, stacked[t][None], chosen)
    block = lax.all_to_all(chosen, "shot", 0, 0, tiled=True)

    p0, p_prev = pressure_now[0], pressure_prev[0]
    q4, q5 = adjoint_last[0], adjoint_after[0]
    p0_b = swap_second(jnp.where(odd == 1, pressure_now[0][1:8], pressure_now[0][0:7]))
    p0_a = swap_first(jnp.where(odd == 1, pressure_now[0][0:7], pressure_now[0][1:8]))
    own, seven, four = plane_field(CX), plane_field(7), plane_field(4)
    spots, base_p, base_q, p0, q4, source_planes, tables = call(
        prepare_kernel,
        [info, source_wave[0]],
        [receiver_cell, observed[0], p0, p_prev, q4, q5],
        [jax.ShapeDtypeStruct((STEPS + 1, CX, CY, CZ), F32), own, own, own, own, plane_field(STEPS),
         jax.ShapeDtypeStruct((2, CZ, CZ), F32)],
        flops=400_000_000,
    )
    ids = jnp.arange(TILES, dtype=jnp.int32)[:, None, None]
    picked = jnp.broadcast_to(
        (column[None, :, None] == ids).astype(F32), (TILES, column.shape[0], CZ)
    )
    block, spots, base_p, base_q, p0, q4, source_planes, picked, tables = lax.optimization_barrier(
        (block, spots, base_p, base_q, p0, q4, source_planes, picked, tables)
    )

    stiff = block[:, 0].transpose(1, 0, 2)
    buoy = block[:, 1].transpose(1, 0, 2)
    slopes = jax.ShapeDtypeStruct((3, CX, CY, CZ), F32)
    images = jax.ShapeDtypeStruct((2, CX, CY, CZ), F32)

    send_a, send_b, f4 = call(
        model_kernel, [info], [stiff, buoy, q4], [four, far_rows(4), own]
    )
    edge_b = swap_second(send_b)
    edge_a = swap_first(send_a)

    (padded,) = call(
        widen_kernel,
        [info],
        [p0, p0_a, p0_b],
        [jax.ShapeDtypeStruct((WIDE, ROWS, CZ), F32)],
    )
    p1, send_a, send_b, near, far, div0, slope0, wide = call(
        first_kernel,
        [info],
        [tables, padded, base_p, source_planes, stiff, buoy, edge_a, edge_b, f4],
        [own, seven, far_rows(7), seven, far_rows(7), own, slopes, plane_field(CX + 8)],
        work()[1:],
    )
    from_b = swap_second(send_b)
    from_a = swap_first(send_a)
    far = swap_second(far)
    near = swap_first(near)
    (q_part,) = call(adjoint_part_kernel, [info], [tables, base_q, f4, near, far, wide], [own], work())

    p2, send_a, send_b, div1, slope1 = call(
        second_kernel,
        [info],
        [tables, p1, from_a, from_b, p0, source_planes, stiff, wide],
        [own, seven, far_rows(7), own, slopes],
        work(),
    )
    from_b = swap_second(send_b)
    from_a = swap_first(send_a)

    q3, f3, send_a, send_b, div2, slope2 = call(
        third_kernel,
        [info],
        [tables, p2, from_a, from_b, p1, source_planes, stiff, wide, q_part, spots],
        [own, own, seven, far_rows(7), own, slopes],
        work(),
    )
    from_b = swap_second(send_b)
    from_a = swap_first(send_a)

    q2, f2, send_a, send_b, slope_q = call(
        adjoint_first_kernel,
        [info],
        [tables, q3, q4, f3, from_a, from_b, stiff, wide, spots, p2],
        [own, own, seven, far_rows(7), slopes],
        work(),
    )
    from_b = swap_second(send_b)
    from_a = swap_first(send_a)
    image, q2_out = call(image_first_kernel, [], [q3, slope_q, div2, slope2, q2], [images, own])

    q1, f1, send_a, send_b, slope_q = call(
        adjoint_second_kernel,
        [info],
        [tables, q2, q3, f2, from_a, from_b, stiff, wide, spots, p1],
        [own, own, four, far_rows(4), slopes],
        work(),
    )
    from_b = swap_second(send_b)
    from_a = swap_first(send_a)
    image, q1_out = call(
        image_second_kernel, [], [q2, slope_q, div1, slope1, image, q1], [images, own]
    )

    (image,) = call(
        image_kernel,
        [info],
        [q1, f1, from_a, from_b, div0, slope0, image],
        [images],
        [pltpu.VMEM((CX + 8, ROWS, CZ), F32)],
    )
    arrived = lax.all_to_all(image.transpose(2, 0, 1, 3), "shot", 0, 0, tiled=True)
    tiles = jax.ShapeDtypeStruct((TILES, CX, CZ), F32)
    grad_kappa, grad_buoy = call(gather_kernel, [], [picked, arrived], [tiles, tiles])
    return (grad_kappa, grad_buoy, q1_out[None], q2_out[None])


def solution(mesh):
    in_specs = (
        P("shot", "dom", None, None),
        P("shot", "dom", None, None),
        P("shot", "dom", None, None),
        P("shot", "dom", None, None),
        P(None, "dom", "shot"),
        P(None, "dom", "shot"),
        P(),
        P("shot"),
        P("shot", None),
        P("shot", None),
        P("shot", None, None),
    )
    out_specs = (
        P(None, "dom", "shot"),
        P(None, "dom", "shot"),
        P("shot", "dom", None, None),
        P("shot", "dom", None, None),
    )
    return jax.shard_map(shards, mesh=mesh, in_specs=in_specs, out_specs=out_specs, check_vma=False)
```

```python
import jax
import jax.numpy as jnp
from jax import lax
from jax.experimental import pallas as pl
from jax.experimental.pallas import tpu as pltpu
from jax.sharding import PartitionSpec as P

CX = 8
CY = 32
CZ = 128
TILES = 4
STEPS = 3
REC = 512
PAD = 8
ROWS = CY + 2 * PAD
WIDE = CX + 14

COEFFS = (1225.0 / 1024.0, -245.0 / 3072.0, 49.0 / 5120.0, -5.0 / 7168.0)
step_squared = 0.02

VMEM = pl.BlockSpec(memory_space=pltpu.VMEM)
SMEM = pl.BlockSpec(memory_space=pltpu.SMEM)
F32 = jnp.float32


def plane_field(count):
    return jax.ShapeDtypeStruct((count, CY, CZ), F32)


def far_rows(count):
    return jax.ShapeDtypeStruct((count * CY + 8, CZ), F32)


def rows_of(planes):
    return planes.reshape(planes.shape[0] * CY, CZ)


def planes_at(rows, start, count):
    return rows[start * CY : (start + count) * CY, :].reshape(count, CY, CZ)


def lane_shift(plane, by, lane):
    if by == 0:
        return plane
    moved = pltpu.roll(plane, (-by) % CZ, 1)
    keep = lane < CZ - by if by > 0 else lane >= -by
    return jnp.where(keep, moved, 0.0)


def stencil(at):
    total = COEFFS[0] * (at(0) - at(-1))
    for k in range(2, 5):
        total = total + COEFFS[k - 1] * (at(k - 1) - at(-k))
    return total


def place(info, target, own, first, second, width):
    target[:, 0:PAD, :] = jnp.zeros((target.shape[0], PAD, CZ), F32)
    target[:, PAD + CY : ROWS, :] = jnp.zeros((target.shape[0], PAD, CZ), F32)
    inner = slice(PAD, PAD + CY)
    for cell in range(CX):
        target[width + cell, inner, :] = own[cell]
    odd = info[0] == 1

    @pl.when(odd)
    def _():
        target[0:width, inner, :] = first()
        target[width + CX : 2 * width + CX, inner, :] = second()

    @pl.when(jnp.logical_not(odd))
    def _():
        target[0:width, inner, :] = second()
        target[width + CX : 2 * width + CX, inner, :] = first()


def for_partner(info, target, head, tail):
    odd = info[0] == 1

    @pl.when(odd)
    def _():
        target[...] = head()

    @pl.when(jnp.logical_not(odd))
    def _():
        target[...] = tail()


def choose_kernel(where, aperture, kappa, buoy, out):
    lanes = lax.broadcasted_iota(jnp.int32, aperture.shape, 1)
    mine = jnp.where(lanes == where[0], aperture[...], 0).astype(F32)
    tiles = jnp.broadcast_to(jnp.sum(mine, axis=1, keepdims=True), (aperture.shape[0], CZ))
    for s in range(out.shape[0]):
        tile = jnp.broadcast_to(tiles[s : s + 1, :], (CX, CZ))
        for half, model in enumerate((kappa, buoy)):
            value = model[0]
            for t in range(1, TILES):
                value = jnp.where(tile == float(t), model[t], value)
            out[s, half] = value


def hand_over(info, send_a, send_b, field):
    width = send_a.shape[0]
    for_partner(info, send_a, lambda: field[0:width], lambda: field[CX - width : CX])
    for_partner(
        info,
        send_b.at[0 : width * CY],
        lambda: rows_of(field[CX - width : CX]),
        lambda: rows_of(field[0:width]),
    )
    send_b[width * CY :, :] = jnp.zeros((8, CZ), F32)


def slope_x(field, at):
    return stencil(lambda s: field[at + s, PAD : PAD + CY, :])


def slope_y(field, at):
    return stencil(lambda s: field[at, PAD + s : PAD + CY + s, :])


def slope_z(plane, lane):
    return stencil(lambda s: lane_shift(plane, s, lane))


def along_z(planes, table):
    rows = planes.reshape(CX * CY, CZ)
    out = lax.dot_general(
        rows,
        table,
        (((1,), (0,)), ((), ())),
        precision=lax.Precision.HIGHEST,
        preferred_element_type=F32,
    )
    return out.reshape(CX, CY, CZ)


def operate(field, width, buoy, tables, gx, gy, acc, slopes):
    gy[:, 0:PAD, :] = jnp.zeros((CX, PAD, CZ), F32)
    gy[:, PAD + CY : ROWS, :] = jnp.zeros((CX, PAD, CZ), F32)
    slope = along_z(field[width : width + CX, PAD : PAD + CY, :], tables[0])
    acc[...] = along_z(buoy[4 : 4 + CX] * slope, tables[1])
    for cell in range(-3, CX + 4):
        sx = slope_x(field, cell + width)
        gx[cell + 3] = buoy[cell + 4] * sx
        if 0 <= cell < CX:
            sy = slope_y(field, cell + width)
            gy[cell, PAD : PAD + CY, :] = buoy[cell + 4] * sy
            slopes(cell, sx, sy, slope[cell])
    for cell in range(CX):
        div = stencil(lambda s: gx[cell + 4 + s])
        div = div + stencil(lambda s: gy[cell, PAD + 1 + s : PAD + 1 + s + CY, :])
        yield cell, div + acc[cell]


def prepare_kernel(
    info, wave, cells, seen, now, before, last, after, out, base_p, base_q, now_out, last_out, source_out,
    tables,
):
    gap = lax.broadcasted_iota(jnp.int32, (CZ, CZ), 0) - lax.broadcasted_iota(jnp.int32, (CZ, CZ), 1)
    for at in range(2):
        table = jnp.zeros((CZ, CZ), F32)
        for k in range(1, 5):
            table = table + jnp.where(gap == k - 1 + at, COEFFS[k - 1], 0.0)
            table = table - jnp.where(gap == at - k, COEFFS[k - 1], 0.0)
        tables[at] = table
    base_p[...] = 2.0 * now[...] - before[...]
    base_q[...] = 2.0 * last[...] - after[...]
    now_out[...] = now[...]
    last_out[...] = last[...]
    y = lax.broadcasted_iota(jnp.int32, (CY, CZ), 0)
    z = lax.broadcasted_iota(jnp.int32, (CY, CZ), 1)
    hit = (y == info[2]) & (z == info[3])
    for n in range(STEPS):
        source_out[n] = jnp.where(hit, wave[n], 0.0)

    index = cells[...] - info[4]
    row = lax.shift_right_arithmetic(index, 7)
    z = lax.bitwise_and(index, 127)
    rows = lax.broadcasted_iota(jnp.int32, (CX * CY, REC), 0)
    pick = jnp.where(rows == row, 1.0, 0.0).astype(jnp.bfloat16)
    lanes = lax.broadcasted_iota(jnp.int32, (CZ, REC), 0)
    here = lanes == z

    def spread(values):
        right = jnp.where(here, values, 0.0).astype(jnp.bfloat16)
        return lax.dot_general(
            pick, right, (((1,), (1,)), ((), ())), preferred_element_type=F32
        )

    out[0] = spread(jnp.ones((1, REC), F32)).reshape(CX, CY, CZ)
    for n in range(STEPS):
        rest = seen[n : n + 1, :]
        total = None
        for _ in range(3):
            part = rest.astype(jnp.bfloat16).astype(F32)
            rest = rest - part
            total = spread(part) if total is None else total + spread(part)
        out[n + 1] = total.reshape(CX, CY, CZ)


def model_kernel(info, stiff, buoy, last, send_a, send_b, scaled):
    scaled[...] = stiff[...] * last[...]
    for_partner(info, send_a, lambda: buoy[0:4], lambda: buoy[4:8])
    for_partner(
        info,
        send_b.at[0 : 4 * CY],
        lambda: rows_of(buoy[4:8]),
        lambda: rows_of(buoy[0:4]),
    )
    send_b[4 * CY :, :] = jnp.zeros((8, CZ), F32)


def widen_kernel(info, now, now_a, now_b, scaled, out, near, far):
    hand_over(info, near, far, scaled)
    place(info, out, now, lambda: now_a[...], lambda: now_b[...], 7)


def forward(info, source, base, stiff, field, buoy, tables, gx, gy, acc, div_out, slope_out, store):
    def keep(cell, sx, sy, sz):
        slope_out[0, cell] = sx
        slope_out[1, cell] = sy
        slope_out[2, cell] = sz

    for cell, div in operate(field, 7, buoy, tables, gx, gy, acc, keep):
        div_out[cell] = div
        value = base(cell) + step_squared * stiff[cell] * div
        store(cell, value + jnp.where(info[1] == cell, source, 0.0))


def widen_buoy(info, buoy, first, second, target):
    target[4 : 4 + CX] = buoy[...]
    odd = info[0] == 1

    @pl.when(odd)
    def _():
        target[0:4] = first[0:4]
        target[4 + CX : 8 + CX] = planes_at(second, 0, 4)

    @pl.when(jnp.logical_not(odd))
    def _():
        target[0:4] = planes_at(second, 0, 4)
        target[4 + CX : 8 + CX] = first[0:4]


def first_kernel(
    info, tables, padded, base, source, stiff, buoy, edge_a, edge_b,
    p_out, send_a, send_b, div_out, slope_out, buoy_out,
    gx, gy, acc,
):
    widen_buoy(info, buoy, edge_a, edge_b, buoy_out)

    def store(cell, value):
        p_out[cell] = value

    forward(
        info, source[0], lambda cell: base[cell],
        stiff, padded, buoy_out, tables, gx, gy, acc, div_out, slope_out, store,
    )
    hand_over(info, send_a, send_b, p_out)


def adjoint_part_kernel(
    info, tables, base, scaled, near, far, buoy,
    q_out,
    field, gx, gy, acc,
):
    place(info, field, scaled, lambda: near[...], lambda: planes_at(far, 0, 7), 7)
    for cell, div in operate(field, 7, buoy, tables, gx, gy, acc, lambda *_: None):
        q_out[cell] = base[cell] + step_squared * div


def second_kernel(
    info, tables, now, now_a, now_b, before, source, stiff, buoy,
    p_out, send_a, send_b, div_out, slope_out,
    field, gx, gy, acc,
):
    place(info, field, now, lambda: now_a[...], lambda: planes_at(now_b, 0, 7), 7)

    def store(cell, value):
        p_out[cell] = value

    forward(
        info, source[1], lambda cell: 2.0 * now[cell] - before[cell],
        stiff, field, buoy, tables, gx, gy, acc, div_out, slope_out, store,
    )
    hand_over(info, send_a, send_b, p_out)


def third_kernel(
    info, tables, now, now_a, now_b, before, source, stiff, buoy, q_part, spots,
    q_out, scaled, send_a, send_b, div_out, slope_out,
    field, gx, gy, acc,
):
    place(info, field, now, lambda: now_a[...], lambda: planes_at(now_b, 0, 7), 7)

    def store(cell, value):
        q = q_part[cell] + (spots[0, cell] * value - spots[3, cell])
        q_out[cell] = q
        scaled[cell] = stiff[cell] * q

    forward(
        info, source[2], lambda cell: 2.0 * now[cell] - before[cell],
        stiff, field, buoy, tables, gx, gy, acc, div_out, slope_out, store,
    )
    hand_over(info, send_a, send_b, scaled)


def adjoint_kernel(
    n, info, tables, q_now, q_after, scaled, scaled_a, scaled_b, stiff, buoy, spots, p_then,
    q_out, scaled_out, send_a, send_b, slope_out,
    field, gx, gy, acc,
):
    place(info, field, scaled, lambda: scaled_a[...], lambda: planes_at(scaled_b, 0, 7), 7)

    def keep(cell, sx, sy, sz):
        slope_out[0, cell] = sx
        slope_out[1, cell] = sy
        slope_out[2, cell] = sz

    for cell, total in operate(field, 7, buoy, tables, gx, gy, acc, keep):
        q = 2.0 * q_now[cell] - q_after[cell] + step_squared * total
        q = q + (spots[0, cell] * p_then[cell] - spots[n + 1, cell])
        q_out[cell] = q
        scaled_out[cell] = stiff[cell] * q
    hand_over(info, send_a, send_b, scaled_out)


def adjoint_first_kernel(*refs):
    adjoint_kernel(1, *refs)


def adjoint_second_kernel(*refs):
    adjoint_kernel(0, *refs)


def image_first_kernel(q_now, slope_q, div, slope_p, q_new, out, q_out):
    q_out[...] = q_new[...]
    for cell in range(CX):
        out[0, cell] = q_now[cell] * div[cell]
        rho = slope_p[0, cell] * slope_q[0, cell] + slope_p[1, cell] * slope_q[1, cell]
        out[1, cell] = rho + slope_p[2, cell] * slope_q[2, cell]


def image_second_kernel(
    q_now, slope_q, div, slope_p, images, q_new, out, q_out
):
    q_out[...] = q_new[...]
    for cell in range(CX):
        out[0, cell] = images[0, cell] + q_now[cell] * div[cell]
        rho = slope_p[0, cell] * slope_q[0, cell] + slope_p[1, cell] * slope_q[1, cell]
        out[1, cell] = images[1, cell] + (rho + slope_p[2, cell] * slope_q[2, cell])


def image_kernel(info, tables, q_now, scaled, scaled_a, scaled_b, div, slope, images, out, field):
    place(info, field, scaled, lambda: scaled_a[...], lambda: planes_at(scaled_b, 0, 4), 4)
    along = along_z(field[4 : 4 + CX, PAD : PAD + CY, :], tables[0])
    for cell in range(CX):
        rho = images[1, cell] + slope[0, cell] * slope_x(field, cell + 4)
        rho = rho + slope[1, cell] * slope_y(field, cell + 4)
        rho = rho + slope[2, cell] * along[cell]
        out[0, cell] = step_squared * (images[0, cell] + q_now[cell] * div[cell])
        out[1, cell] = -step_squared * rho


def gather_kernel(picked, arrived, out_kappa, out_buoy):
    for t in range(TILES):
        kappa = jnp.zeros((CX, CZ), F32)
        rho = jnp.zeros((CX, CZ), F32)
        for s in range(arrived.shape[0]):
            here = picked[t, s : s + 1, :] > 0.0
            kappa = kappa + jnp.where(here, arrived[s, 0], 0.0)
            rho = rho + jnp.where(here, arrived[s, 1], 0.0)
        out_kappa[t] = kappa
        out_buoy[t] = rho


def work():
    return [
        pltpu.VMEM((WIDE, ROWS, CZ), F32),
        pltpu.VMEM((CX + 7, CY, CZ), F32),
        pltpu.VMEM((CX, ROWS, CZ), F32),
        pltpu.VMEM((CX, CY, CZ), F32),
    ]


def call(kernel, scalars, arrays, outs, scratch=(), flops=2_000_000):
    moved = sum(4 * a.size for a in arrays) + sum(4 * o.size for o in outs)
    return pl.pallas_call(
        kernel,
        out_shape=outs,
        in_specs=[SMEM] * len(scalars) + [VMEM] * len(arrays),
        out_specs=[VMEM] * len(outs),
        scratch_shapes=list(scratch),
        compiler_params=pltpu.CompilerParams(vmem_limit_bytes=32 * 1024 * 1024),
        cost_estimate=pl.CostEstimate(flops=flops, bytes_accessed=moved, transcendentals=0),
    )(*scalars, *arrays)


def swap_first(planes):
    count = lax.axis_size("dom")
    return lax.ppermute(planes, "dom", [(i ^ 1, i) for i in range(count)])


def swap_second(planes):
    pairs = []
    for i in range(1, lax.axis_size("dom") - 1, 2):
        pairs += [(i, i + 1), (i + 1, i)]
    return lax.ppermute(planes, "dom", pairs)


def shards(
    pressure_now,
    pressure_prev,
    adjoint_last,
    adjoint_after,
    kappa_model,
    buoy_model,
    aperture,
    source_cell,
    source_wave,
    receiver_cell,
    observed,
):
    dom = lax.axis_index("dom")
    odd = lax.rem(dom, 2)
    offset = dom * (CX * CY * CZ)
    source = source_cell[0]
    info = jnp.stack(
        [odd, source // (CY * CZ) - dom * CX, (source // CZ) % CY, source % CZ, offset]
    ).astype(jnp.int32)

    column = lax.dynamic_index_in_dim(aperture, dom, 1, keepdims=False)
    (chosen,) = call(
        choose_kernel,
        [dom.reshape(1).astype(jnp.int32)],
        [aperture, kappa_model, buoy_model],
        [jax.ShapeDtypeStruct((aperture.shape[0], 2, CX, CZ), F32)],
    )
    block = lax.all_to_all(chosen, "shot", 0, 0, tiled=True)

    p0, p_prev = pressure_now[0], pressure_prev[0]
    q4, q5 = adjoint_last[0], adjoint_after[0]
    p0_b = swap_second(jnp.where(odd == 1, pressure_now[0][1:8], pressure_now[0][0:7]))
    p0_a = swap_first(jnp.where(odd == 1, pressure_now[0][0:7], pressure_now[0][1:8]))
    own, seven, four = plane_field(CX), plane_field(7), plane_field(4)
    spots, base_p, base_q, p0, q4, source_planes, tables = call(
        prepare_kernel,
        [info, source_wave[0]],
        [receiver_cell, observed[0], p0, p_prev, q4, q5],
        [jax.ShapeDtypeStruct((STEPS + 1, CX, CY, CZ), F32), own, own, own, own, plane_field(STEPS),
         jax.ShapeDtypeStruct((2, CZ, CZ), F32)],
        flops=400_000_000,
    )
    ids = jnp.arange(TILES, dtype=jnp.int32)[:, None, None]
    picked = jnp.broadcast_to(
        (column[None, :, None] == ids).astype(F32), (TILES, column.shape[0], CZ)
    )
    block, spots, base_p, base_q, p0, q4, source_planes, picked, tables = lax.optimization_barrier(
        (block, spots, base_p, base_q, p0, q4, source_planes, picked, tables)
    )

    stiff = block[:, 0].transpose(1, 0, 2)
    buoy = block[:, 1].transpose(1, 0, 2)
    slopes = jax.ShapeDtypeStruct((3, CX, CY, CZ), F32)
    images = jax.ShapeDtypeStruct((2, CX, CY, CZ), F32)

    send_a, send_b, f4 = call(
        model_kernel, [info], [stiff, buoy, q4], [four, far_rows(4), own]
    )
    edge_b = swap_second(send_b)
    edge_a = swap_first(send_a)

    padded, near, far = call(
        widen_kernel,
        [info],
        [p0, p0_a, p0_b, f4],
        [jax.ShapeDtypeStruct((WIDE, ROWS, CZ), F32), seven, far_rows(7)],
    )
    p1, send_a, send_b, div0, slope0, wide = call(
        first_kernel,
        [info],
        [tables, padded, base_p, source_planes, stiff, buoy, edge_a, edge_b],
        [own, seven, far_rows(7), own, slopes, plane_field(CX + 8)],
        work()[1:],
    )
    from_b = swap_second(send_b)
    from_a = swap_first(send_a)
    far = swap_second(far)
    near = swap_first(near)
    (q_part,) = call(adjoint_part_kernel, [info], [tables, base_q, f4, near, far, wide], [own], work())

    p2, send_a, send_b, div1, slope1 = call(
        second_kernel,
        [info],
        [tables, p1, from_a, from_b, p0, source_planes, stiff, wide],
        [own, seven, far_rows(7), own, slopes],
        work(),
    )
    from_b = swap_second(send_b)
    from_a = swap_first(send_a)

    q3, f3, send_a, send_b, div2, slope2 = call(
        third_kernel,
        [info],
        [tables, p2, from_a, from_b, p1, source_planes, stiff, wide, q_part, spots],
        [own, own, seven, far_rows(7), own, slopes],
        work(),
    )
    from_b = swap_second(send_b)
    from_a = swap_first(send_a)

    q2, f2, send_a, send_b, slope_q = call(
        adjoint_first_kernel,
        [info],
        [tables, q3, q4, f3, from_a, from_b, stiff, wide, spots, p2],
        [own, own, seven, far_rows(7), slopes],
        work(),
    )
    from_b = swap_second(send_b)
    from_a = swap_first(send_a)
    image, q2_out = call(image_first_kernel, [], [q3, slope_q, div2, slope2, q2], [images, own])

    q1, f1, send_a, send_b, slope_q = call(
        adjoint_second_kernel,
        [info],
        [tables, q2, q3, f2, from_a, from_b, stiff, wide, spots, p1],
        [own, own, four, far_rows(4), slopes],
        work(),
    )
    from_b = swap_second(send_b)
    from_a = swap_first(send_a)
    image, q1_out = call(
        image_second_kernel, [], [q2, slope_q, div1, slope1, image, q1], [images, own]
    )

    (image,) = call(
        image_kernel,
        [info],
        [tables, q1, f1, from_a, from_b, div0, slope0, image],
        [images],
        [pltpu.VMEM((CX + 8, ROWS, CZ), F32)],
    )
    arrived = lax.all_to_all(image.transpose(2, 0, 1, 3), "shot", 0, 0, tiled=True)
    tiles = jax.ShapeDtypeStruct((TILES, CX, CZ), F32)
    grad_kappa, grad_buoy = call(gather_kernel, [], [picked, arrived], [tiles, tiles])
    return (grad_kappa, grad_buoy, q1_out[None], q2_out[None])


def solution(mesh):
    in_specs = (
        P("shot", "dom", None, None),
        P("shot", "dom", None, None),
        P("shot", "dom", None, None),
        P("shot", "dom", None, None),
        P(None, "dom", "shot"),
        P(None, "dom", "shot"),
        P(),
        P("shot"),
        P("shot", None),
        P("shot", None),
        P("shot", None, None),
    )
    out_specs = (
        P(None, "dom", "shot"),
        P(None, "dom", "shot"),
        P("shot", "dom", None, None),
        P("shot", "dom", None, None),
    )
    return jax.shard_map(shards, mesh=mesh, in_specs=in_specs, out_specs=out_specs, check_vma=False)
```
